32 devices in a mesh: seq: 4 (over z), dp: 8 (over y, x, core).
Axes of the slice: x: 2, y: 2, z: 4, core: 2. Of those that a mesh axis runs over, the one named last changes fastest.
Arguments:
- tokens: bfloat16 [8, 1536, 1024], P('dp', 'seq'), may hold values from -6 to 6
- enc_states: bfloat16 [8, 512, 1024], P('dp', 'seq'), may hold values from -6 to 6
- order: int32 [8, 1536], P('dp'), may hold values from 0 to 1535, each once within a row
- lengths: int32 [8, 3], P('dp'), may hold values from 256 to 832, as said below
- enc_lengths: int32 [8, 3], P('dp'), may hold values from 64 to 304, as said below
- attn_in: bfloat16 [1024, 3072], P(None, 'dp'), may hold values from -0.1875 to 0.1875
- attn_out: bfloat16 [1024, 1024], P(None, 'dp'), may hold values from -1.5 to 1.5
- cross_q: bfloat16 [1024, 1024], P(None, 'dp'), may hold values from -0.1875 to 0.1875
- cross_kv: bfloat16 [1024, 2048], P(None, 'dp'), may hold values from -0.1875 to 0.1875
- cross_out: bfloat16 [1024, 1024], P(None, 'dp'), may hold values from -1.5 to 1.5
- ffn_in: bfloat16 [1024, 4096], P(None, 'dp'), may hold values from -0.1875 to 0.1875
- ffn_out: bfloat16 [4096, 1024], P(None, 'dp'), may hold values from -0.09375 to 0.09375
- proj_bias: bfloat16 [7, 1024], P(None, 'dp'), may hold values from -1.5 to 1.5
- gains: bfloat16 [4, 1024], P(None, 'dp'), may hold values from 0.099609375 to 1.8984375
- ln_bias: bfloat16 [4, 1024], P(None, 'dp'), may hold values from -1.5 to 1.5
- ffn_bias: bfloat16 [1, 4096], P(None, 'dp'), may hold values from -1.5 to 1.5
- cotangent: bfloat16 [8, 1536, 1024], P('dp', 'seq'), may hold values from -6 to 6
Outputs:
- output: bfloat16 [8, 1536, 1024], P('dp', 'seq')
- tokens_grad: float32 [8, 1536, 1024], P('dp', 'seq')
- enc_grad: float32 [8, 512, 1024], P('dp', 'seq')
- attn_in_grad: float32 [1024, 3072], P(None, 'dp')
- attn_out_grad: float32 [1024, 1024], P(None, 'dp')
- cross_q_grad: float32 [1024, 1024], P(None, 'dp')
- cross_kv_grad: float32 [1024, 2048], P(None, 'dp')
- cross_out_grad: float32 [1024, 1024], P(None, 'dp')
- ffn_in_grad: float32 [1024, 4096], P(None, 'dp')
- ffn_out_grad: float32 [4096, 1024], P(None, 'dp')
- proj_bias_grad: float32 [7, 1024], P(None, 'dp')
- gains_grad: float32 [4, 1024], P(None, 'dp')
- ln_bias_grad: float32 [4, 1024], P(None, 'dp')
- ffn_bias_grad: float32 [1, 4096], P(None, 'dp')
The draws below stay inside these ranges and needn't reach their ends.
Inputs may be any that keep to these rules, and one draw needn't show every extreme that they name: Each row is a permutation; row r of a group's 1536 rows of tokens and cotangent is the token at place order[r] when the group's sequences stand end to end in order. lengths of a group's 3 sequences in the order in which they stand end to end; they sum to 1536, and exactly one of them is 832. `enc_lengths`: encoder states of a group's sequences, in the same order, laid end to end in its 512 rows; they sum to 512, and exactly one of them is 304.
All inputs are finite; a program needn't handle non-finite values.
Results may differ from the reference program's by a relative error of at most 0.022.
Values may be sent and summed in bfloat16 or wider, within the bound.
No kernel may reach another device: no remote copies, remote signals or barrier semaphores. Data moves between devices by JAX's collectives and lax.ppermute only.
A program may use at most 192 MiB of HBM per device.

```python
import jax
import jax.numpy as jnp
from jax import lax

D = 1024
HEADS = 16
FF = 4096
HEAD_DIM = 64
SEQS = 3
MINLEN = 256
ENC_MIN = 64
GROUP_TOK = 1536
ENC_GROUP = 512
MAXLEN = 832
ENC_MAX = 304
N_DP = 8


def split_lengths(key, total, least, most):
    spare = total - SEQS * least - (most - least)
    key_cuts, key_place = jax.random.split(key)
    cuts = jnp.sort(jax.random.randint(key_cuts, (N_DP, SEQS - 2), 0, spare + 1), axis=1)
    bounds = jnp.concatenate([jnp.zeros((N_DP, 1), jnp.int32), cuts.astype(jnp.int32), jnp.full((N_DP, 1), spare, jnp.int32)], axis=1)
    others = least + jnp.diff(bounds, axis=1)
    place = jax.random.randint(key_place, (N_DP, 1), 0, SEQS)
    column = jnp.arange(SEQS, dtype=jnp.int32)[None, :]
    source = jnp.clip(jnp.where(column < place, column, column - 1), 0, SEQS - 2)
    taken = jnp.take_along_axis(others, jnp.broadcast_to(source, (N_DP, SEQS)), axis=1)
    return jnp.where(column == place, most, taken).astype(jnp.int32)


def draw_lengths(key, part):
    return split_lengths(jax.random.fold_in(key, 11), GROUP_TOK, MINLEN, MAXLEN)


def draw_enc_lengths(key, part):
    return split_lengths(jax.random.fold_in(key, 23), ENC_GROUP, ENC_MIN, ENC_MAX)


def steps_of(own_key, dims, cuts, low, largest):
    level, own = 1.0, jax.random.fold_in(own_key, 6)
    for dim, blocks in cuts:
        heights = jnp.exp(jax.random.uniform(jax.random.fold_in(own, dim), (blocks,), jnp.float32, low / len(cuts), largest / len(cuts)))
        level = level * jnp.repeat(heights, dims[dim] // blocks).reshape([-1 if axis == dim else 1 for axis in range(len(dims))])
    return level


def noise(own_key, shape, spread, reach, shards=(), held_as=jnp.bfloat16):
    array = spread * jax.random.normal(own_key, shape, jnp.float32)
    if shards:
        array = array * steps_of(own_key, shape, shards, -0.22, 0.18)
    return jnp.clip(array, -reach, reach).astype(held_as)


def setup_inputs(seed: int = 0) -> dict:
    keys = jax.random.split(jax.random.key(seed), 18)
    tokens = noise(keys[0], (N_DP, GROUP_TOK, D), 1.0, 6.0, ((0, 8), (1, 4)))
    enc_states = noise(keys[1], (N_DP, ENC_GROUP, D), 1.0, 6.0, ((0, 8), (1, 4)))
    order = jax.vmap(lambda own: jax.random.permutation(own, GROUP_TOK))(jax.random.split(keys[2], N_DP)).reshape((N_DP, GROUP_TOK)).astype(jnp.int32)
    lengths = draw_lengths(jax.random.fold_in(keys[17], 71), 0)
    enc_lengths = draw_enc_lengths(jax.random.fold_in(keys[17], 71), 0)
    attn_in = noise(keys[5], (D, 3 * D), D ** -0.5, 0.1875, ((1, 8),))
    attn_out = noise(keys[6], (D, D), 16 ** -0.5, 1.5, ((1, 8),))
    cross_q = noise(keys[7], (D, D), D ** -0.5, 0.1875, ((1, 8),))
    cross_kv = noise(keys[8], (D, 2 * D), D ** -0.5, 0.1875, ((1, 8),))
    cross_out = noise(keys[9], (D, D), 16 ** -0.5, 1.5, ((1, 8),))
    ffn_in = noise(keys[10], (D, FF), D ** -0.5, 0.1875, ((1, 8),))
    ffn_out = noise(keys[11], (FF, D), FF ** -0.5, 0.09375, ((1, 8),))
    proj_bias = noise(keys[12], (7, D), 0.3, 1.5, ((1, 8),))
    gains = jnp.clip(1.0 + 0.18 * jax.random.normal(keys[13], (4, D), jnp.float32), 0.099609375, 1.8984375).astype(jnp.bfloat16)
    ln_bias = noise(keys[14], (4, D), 0.3, 1.5, ((1, 8),))
    ffn_bias = noise(keys[15], (1, FF), 0.3, 1.5, ((1, 8),))
    cotangent = noise(keys[16], (N_DP, GROUP_TOK, D), 1.0, 6.0, ((0, 8), (1, 4)))
    return dict(tokens=tokens, enc_states=enc_states, order=order, lengths=lengths, enc_lengths=enc_lengths, attn_in=attn_in, attn_out=attn_out, cross_q=cross_q, cross_kv=cross_kv, cross_out=cross_out, ffn_in=ffn_in, ffn_out=ffn_out, proj_bias=proj_bias, gains=gains, ln_bias=ln_bias, ffn_bias=ffn_bias, cotangent=cotangent)


EPSILON = 1e-05
PRECISE = lax.Precision.HIGHEST

@jax.custom_vjp
def low(v):
    return lax.optimization_barrier(v.astype(jnp.bfloat16)).astype(jnp.float32)

@jax.custom_vjp
def low_back(v):
    return v

def low_keep(v):
    return (low(v), None)

def low_pass(kept, grad):
    return (grad,)

def back_keep(v):
    return (v, None)

def back_low(kept, grad):
    return (low(grad),)
low.defvjp(low_keep, low_pass)
low_back.defvjp(back_keep, back_low)

def matmul(left, right):
    return jnp.dot(left, right, precision=PRECISE)

def apply_layer_norm(input_tokens, gain, shift):
    center = input_tokens - lax.optimization_barrier(jnp.mean(input_tokens, axis=-1, keepdims=True))
    inv_dev = lax.rsqrt(lax.optimization_barrier(jnp.mean(center * center, axis=-1, keepdims=True)) + EPSILON)
    return center * inv_dev * gain + shift

def segment_ids(positions, seq_lengths):
    ends = jnp.cumsum(seq_lengths)
    return lax.optimization_barrier(jnp.sum((positions[:, None] >= ends[None, :]).astype(jnp.int32), axis=1))

def attend_block(query_blk, mask_blk, keys_all, values_all):
    scale_val = query_blk.shape[-1] ** (-0.5)
    scores = low_back(jnp.einsum('qhd,khd->hqk', query_blk, keys_all, precision=PRECISE) * scale_val)
    scores = jnp.where(mask_blk[None], scores, -1e+30)
    row_peak = lax.optimization_barrier(jnp.max(scores, axis=-1, keepdims=True))
    row_exp = jnp.exp(scores - row_peak)
    probs_full = row_exp / lax.optimization_barrier(jnp.sum(row_exp, axis=-1, keepdims=True))
    return jnp.einsum('hqk,khd->qhd', low(probs_full), values_all, precision=PRECISE)

def attention(queries, keys_all, values_all, query_pos, query_seg, key_pos, key_seg, causal):
    row_total = queries.shape[0]
    block_rows = min(512, row_total)
    block_count = row_total // block_rows

    def per_block(pieces):
        query_blk, pos_blk, seg_blk = pieces
        mask_blk = seg_blk[:, None] == key_seg[None, :]
        if causal:
            mask_blk = mask_blk & (key_pos[None, :] <= pos_blk[:, None])
        return attend_block(query_blk, mask_blk, keys_all, values_all)
    results = lax.map(jax.checkpoint(per_block), (queries.reshape((block_count, block_rows) + queries.shape[1:]), query_pos.reshape(block_count, block_rows), query_seg.reshape(block_count, block_rows)))
    return results.reshape(queries.shape)

def group_forward(weights, input_tokens, states, order_row, length_row, enc_length_row):
    attn_in, attn_out, cross_q, cross_kv, cross_out, ffn_in, ffn_out, proj_bias, gains, ln_bias, ffn_bias = weights
    rows_here = input_tokens.shape[0]
    enc_rows = states.shape[0]
    positions = order_row
    seg_query = segment_ids(positions, length_row)
    seg_enc = segment_ids(jnp.arange(enc_rows, dtype=jnp.int32), enc_length_row)
    zero_row = jnp.zeros((D,), jnp.float32)
    act_one = low(apply_layer_norm(input_tokens, gains[0], ln_bias[0]))
    qkv = matmul(act_one, attn_in) + jnp.concatenate([proj_bias[0], zero_row, proj_bias[1]])
    qkv = low_back(low(qkv)).reshape(rows_here, 3, HEADS, HEAD_DIM)
    enc_kv = matmul(states, cross_kv) + jnp.concatenate([zero_row, proj_bias[4]])
    enc_kv = low_back(low(enc_kv)).reshape(enc_rows, 2, HEADS, HEAD_DIM)
    self_res = attention(qkv[:, 0], qkv[:, 1], qkv[:, 2], positions, seg_query, positions, seg_query, True)
    self_res = low_back(low(self_res.reshape(rows_here, D)))
    first_residual_state = input_tokens + low_back(matmul(self_res, attn_out)) + proj_bias[2]
    act_two = low(apply_layer_norm(first_residual_state, gains[1], ln_bias[1]))
    cross_query = low_back(low(matmul(act_two, cross_q) + proj_bias[3])).reshape(rows_here, HEADS, HEAD_DIM)
    cross_res = attention(cross_query, enc_kv[:, 0], enc_kv[:, 1], positions, seg_query, seg_enc, seg_enc, False)
    cross_res = low_back(low(cross_res.reshape(rows_here, D)))
    second_residual_state = first_residual_state + low_back(matmul(cross_res, cross_out)) + proj_bias[5]
    act_three = low(apply_layer_norm(second_residual_state, gains[2], ln_bias[2]))
    up_proj = low_back(matmul(act_three, ffn_in) + ffn_bias[0])
    gelu_out = low(jax.nn.gelu(up_proj, approximate=True))
    third_residual_state = second_residual_state + low_back(matmul(gelu_out, ffn_out)) + proj_bias[6]
    return apply_layer_norm(third_residual_state, gains[3], ln_bias[3])

def reference(tokens, enc_states, order, lengths, enc_lengths, attn_in, attn_out, cross_q, cross_kv, cross_out, ffn_in, ffn_out, proj_bias, gains, ln_bias, ffn_bias, cotangent):
    floats = (attn_in.astype(jnp.float32), attn_out.astype(jnp.float32), cross_q.astype(jnp.float32), cross_kv.astype(jnp.float32), cross_out.astype(jnp.float32), ffn_in.astype(jnp.float32), ffn_out.astype(jnp.float32), proj_bias.astype(jnp.float32), gains.astype(jnp.float32), ln_bias.astype(jnp.float32), ffn_bias.astype(jnp.float32))

    def forward(weights, input_tokens, states):

        def per_group(pieces):
            return group_forward(weights, pieces[0], pieces[1], pieces[2], pieces[3], pieces[4])
        return lax.map(jax.checkpoint(per_group), (input_tokens, states, order, lengths, enc_lengths))
    result, pullback = jax.vjp(forward, floats, tokens.astype(jnp.float32), enc_states.astype(jnp.float32))
    weight_grads, input_grad, state_grad = pullback(cotangent.astype(jnp.float32))
    return (result.astype(jnp.bfloat16), input_grad, state_grad, weight_grads[0], weight_grads[1], weight_grads[2], weight_grads[3], weight_grads[4], weight_grads[5], weight_grads[6], weight_grads[7], weight_grads[8], weight_grads[9], weight_grads[10])
```

```python
import functools

import jax
import jax.numpy as jnp
from jax import lax
from jax.experimental import pallas as pl
from jax.experimental.pallas import tpu as pltpu
from jax.sharding import PartitionSpec as P

HEADS = 16
EPSILON = 1e-05
BF = jnp.bfloat16
F32 = jnp.float32
NEG = -1e30
VMEM_LIMIT = 56 * 1024 * 1024


def params(**kw):
    return pltpu.CompilerParams(vmem_limit_bytes=VMEM_LIMIT, **kw)


def layer_norm(v, gain, shift):
    center = v - jnp.mean(v, axis=-1, keepdims=True)
    inv = lax.rsqrt(jnp.mean(center * center, axis=-1, keepdims=True) + EPSILON)
    normed = center * inv
    return normed * gain + shift, normed, inv


def norm_input_grad(normed, inv, gain, c):
    e = c * gain
    return inv * (
        e
        - jnp.mean(e, axis=-1, keepdims=True)
        - normed * jnp.mean(e * normed, axis=-1, keepdims=True)
    )


def norm_sums(normed, c):
    return jnp.sum(c * normed, axis=0), jnp.sum(c, axis=0)


def dense(a, b):
    return jnp.dot(a, b, preferred_element_type=F32)


def dense_t(a, b):
    return lax.dot_general(a, b, (((1,), (1,)), ((), ())), preferred_element_type=F32)


def dense_left(a, b):
    return lax.dot_general(a, b, (((0,), (0,)), ((), ())), preferred_element_type=F32)


def segment_ids(positions, lengths):
    ends = jnp.cumsum(lengths)
    return jnp.sum((positions[:, None] >= ends[None, :]).astype(jnp.int32), axis=1)


def split_heads(block, scale):
    head = block.shape[1] // 2
    lane = lax.broadcasted_iota(jnp.int32, block.shape, 1)
    zero = jnp.zeros_like(block)
    both = jnp.concatenate(
        [jnp.where(lane < head, block, zero), jnp.where(lane >= head, block, zero)], axis=0
    )
    return both if scale is None else both * jnp.asarray(scale, both.dtype)


def join_heads(acc):
    head, rows = acc.shape[0] // 2, acc.shape[1] // 2
    return jnp.concatenate([acc[:head, :rows], acc[head:, rows:]], axis=0)


def nt(a, b):
    return lax.dot_general(a, b, (((1,), (1,)), ((), ())), preferred_element_type=F32)


def tn(a, b):
    return lax.dot_general(a, b, (((0,), (0,)), ((), ())), preferred_element_type=F32)


def attn_fwd_kernel(scale, chunk, q_ref, k_ref, v_ref, bias_ref, o_ref, lse_ref, acc_ref, m_ref, l_ref):
    both = split_heads(q_ref[...], scale)
    acc_ref[...] = jnp.zeros_like(acc_ref)
    m_ref[...] = jnp.full_like(m_ref, NEG)
    l_ref[...] = jnp.zeros_like(l_ref)

    @pl.loop(0, k_ref.shape[0] // chunk)
    def _(c):
        rows = pl.ds(pl.multiple_of(c * chunk, chunk), chunk)
        b = bias_ref[rows, :]
        s = nt(k_ref[rows, :], both) + jnp.concatenate([b, b], axis=1)
        m_old = m_ref[...]
        m_new = jnp.maximum(m_old, jnp.max(s, axis=0, keepdims=True))
        alpha = jnp.exp(m_old - m_new)
        p = jnp.exp(s - m_new)
        m_ref[...] = m_new
        l_ref[...] = l_ref[...] * alpha + jnp.sum(p, axis=0, keepdims=True)
        acc_ref[...] = acc_ref[...] * alpha + tn(v_ref[rows, :], p.astype(BF))

    total = l_ref[...]
    o_ref[...] = jnp.transpose(join_heads(acc_ref[...] / total)).astype(BF)
    lse_ref[0] = m_ref[...] + jnp.log(total)


def attn_fwd(q, kv, bias):
    nq, width = q.shape
    nk = kv.shape[0]
    head = width // HEADS
    pairs, pw = HEADS // 2, 2 * head
    chunk = 256
    return pl.pallas_call(
        functools.partial(attn_fwd_kernel, head**-0.5, chunk),
        grid=(pairs,),
        in_specs=[
            pl.BlockSpec((nq, pw), lambda i: (0, i)),
            pl.BlockSpec((nk, pw), lambda i: (0, i)),
            pl.BlockSpec((nk, pw), lambda i: (0, pairs + i)),
            pl.BlockSpec((nk, nq), lambda i: (0, 0)),
        ],
        out_specs=[
            pl.BlockSpec((nq, pw), lambda i: (0, i)),
            pl.BlockSpec((1, 1, 2 * nq), lambda i: (i, 0, 0)),
        ],
        out_shape=[
            jax.ShapeDtypeStruct((nq, width), BF),
            jax.ShapeDtypeStruct((pairs, 1, 2 * nq), F32),
        ],
        scratch_shapes=[
            pltpu.VMEM((pw, 2 * nq), F32),
            pltpu.VMEM((1, 2 * nq), F32),
            pltpu.VMEM((1, 2 * nq), F32),
        ],
        compiler_params=params(),
        cost_estimate=pl.CostEstimate(
            flops=8 * HEADS * nq * nk * head,
            bytes_accessed=4 * nk * width + 4 * nq * width + 4 * nk * nq,
            transcendentals=HEADS * nq * nk,
        ),
    )(q, kv, kv, bias)


def attn_bwd_kernel(
    scale, chunk, q_ref, k_ref, v_ref, do_ref, bias_ref, lse_ref, delta_ref, dq_ref, dk_ref, dv_ref, acc_ref
):
    both = split_heads(q_ref[...], scale)
    dboth = split_heads(do_ref[...], None)
    acc_ref[...] = jnp.zeros_like(acc_ref)
    lse = lse_ref[0]
    delta = delta_ref[0]

    @pl.loop(0, k_ref.shape[0] // chunk)
    def _(c):
        rows = pl.ds(pl.multiple_of(c * chunk, chunk), chunk)
        b = bias_ref[rows, :]
        k = k_ref[rows, :]
        p = jnp.exp(nt(k, both) + jnp.concatenate([b, b], axis=1) - lse)
        ds = (p * (nt(v_ref[rows, :], dboth) - delta)).astype(BF)
        dk_ref[rows, :] = dense(ds, both).astype(BF)
        dv_ref[rows, :] = dense(p.astype(BF), dboth).astype(BF)
        acc_ref[...] += tn(k, ds)

    dq_ref[...] = jnp.transpose(join_heads(acc_ref[...]) * scale).astype(BF)


def attn_bwd(q, kv, bias, lse, out, dout):
    nq, width = q.shape
    nk = kv.shape[0]
    head = width // HEADS
    pairs, pw = HEADS // 2, 2 * head
    chunk = 256
    delta = jnp.sum((dout.astype(F32) * out.astype(F32)).reshape(nq, HEADS, head), axis=-1)
    delta = delta.T.reshape(pairs, 1, 2 * nq)
    row_spec = pl.BlockSpec((nq, pw), lambda i: (0, i))
    key_spec = pl.BlockSpec((nk, pw), lambda i: (0, i))
    vec_spec = pl.BlockSpec((1, 1, 2 * nq), lambda i: (i, 0, 0))
    return pl.pallas_call(
        functools.partial(attn_bwd_kernel, head**-0.5, chunk),
        grid=(pairs,),
        in_specs=[
            row_spec,
            key_spec,
            pl.BlockSpec((nk, pw), lambda i: (0, pairs + i)),
            row_spec,
            pl.BlockSpec((nk, nq), lambda i: (0, 0)),
            vec_spec,
            vec_spec,
        ],
        out_specs=[row_spec, key_spec, key_spec],
        out_shape=[
            jax.ShapeDtypeStruct((nq, width), BF),
            jax.ShapeDtypeStruct((nk, width), BF),
            jax.ShapeDtypeStruct((nk, width), BF),
        ],
        scratch_shapes=[pltpu.VMEM((pw, 2 * nq), F32)],
        compiler_params=params(),
        cost_estimate=pl.CostEstimate(
            flops=20 * HEADS * nq * nk * head,
            bytes_accessed=8 * nk * width + 6 * nq * width + 4 * nk * nq,
            transcendentals=HEADS * nq * nk,
        ),
    )(q, kv, kv, dout, bias, lse, delta)


def swap(v, bit):
    return lax.ppermute(v, "dp", [(i, i ^ bit) for i in range(8)])


def assemble_kernel(me_ref, mine_ref, other_ref, out_ref, sems):
    n = mine_ref.shape[2]
    copies = []
    for i in range(4):
        for t, ref in enumerate((mine_ref, other_ref)):
            d = jnp.bitwise_xor(me_ref[0], 2 * i + t)
            dst = out_ref.at[:, pl.ds(pl.multiple_of(d * n, 128), n)]
            copies.append(pltpu.make_async_copy(ref.at[i], dst, sems.at[2 * i + t]))
    for c in copies:
        c.start()
    for c in copies:
        c.wait()


def assemble(me, mine, other):
    _, rows, n = mine.shape
    return pl.pallas_call(
        assemble_kernel,
        in_specs=[
            pl.BlockSpec(memory_space=pltpu.SMEM),
            pl.BlockSpec(memory_space=pl.ANY),
            pl.BlockSpec(memory_space=pl.ANY),
        ],
        out_specs=pl.BlockSpec(memory_space=pl.ANY),
        out_shape=jax.ShapeDtypeStruct((rows, 8 * n), mine.dtype),
        scratch_shapes=[pltpu.SemaphoreType.DMA((8,))],
        compiler_params=params(),
        cost_estimate=pl.CostEstimate(flops=0, bytes_accessed=32 * rows * n, transcendentals=0),
    )(me, mine, other)


def gather_columns(w, me):
    half = w.shape[0] // 2
    top, low = w[:half], w[half:]
    x_top, y_low = swap(top, 2), swap(low, 4)
    y_top, x_low = swap(top, 4), swap(low, 2)
    xy_top, xy_low = swap(x_top, 4), swap(y_low, 2)
    mine = jnp.concatenate([top, low, x_top, x_low, y_top, y_low, xy_top, xy_low], axis=0)
    mine = mine.reshape((4,) + w.shape)
    return assemble(me, mine, swap(mine, 1))


def wgrad_kernel(me_ref, x_ref, keep_in, send_in, keep_ref, send_ref, xt_ref):
    @pl.when((pl.program_id(0) == 0) & (pl.program_id(1) == 0))
    def _():
        xt_ref[...] = jnp.transpose(x_ref[...])

    n = keep_in.shape[1]
    res = dense(xt_ref[...], jnp.concatenate([keep_in[...], send_in[...]], axis=1))
    keep_ref[0] = res[:, :n].astype(BF)
    send_ref[0] = res[:, n:].astype(BF)


def wgrad(me, x, dy):
    tok, rows = x.shape
    n = dy.shape[1] // 8
    block = 128
    nb = n // block
    col = lambda t: lambda i, j, me_ref: (0, jnp.bitwise_xor(me_ref[0], 2 * i + t) * nb + j)
    out_spec = pl.BlockSpec((1, rows, block), lambda i, j, me_ref: (i, 0, j))
    return pl.pallas_call(
        wgrad_kernel,
        grid_spec=pltpu.PrefetchScalarGridSpec(
            num_scalar_prefetch=1,
            grid=(4, nb),
            in_specs=[
                pl.BlockSpec((tok, rows), lambda i, j, me_ref: (0, 0)),
                pl.BlockSpec((tok, block), col(0)),
                pl.BlockSpec((tok, block), col(1)),
            ],
            out_specs=[out_spec, out_spec],
            scratch_shapes=[pltpu.VMEM((rows, tok), BF)],
        ),
        out_shape=[jax.ShapeDtypeStruct((4, rows, n), BF)] * 2,
        compiler_params=params(),
        cost_estimate=pl.CostEstimate(
            flops=2 * tok * rows * 8 * n,
            bytes_accessed=2 * (tok * rows + tok * 8 * n + rows * 8 * n),
            transcendentals=0,
        ),
    )(me, x, dy, dy)


def add(*terms):
    total = terms[0].astype(F32)
    for t in terms[1:]:
        total = total + t.astype(F32)
    return total.astype(BF)


def scatter_columns(keep, send):
    got = swap(send, 1)
    half = keep.shape[1] // 2
    ka, kb, ga, gb = keep[:, :half], keep[:, half:], got[:, :half], got[:, half:]
    pick = lambda a, i: jnp.stack([a[i], a[3]])
    xa = swap(add(pick(ka, 1), pick(ga, 1)), 2)
    yb = swap(add(pick(kb, 2), pick(gb, 2)), 4)
    ya = swap(add(ka[2], ga[2], xa[1]), 4)
    xb = swap(add(kb[1], gb[1], yb[1]), 2)
    return jnp.concatenate([add(ka[0], ga[0], xa[0], ya), add(kb[0], gb[0], yb[0], xb)], axis=0)


def shift(v, n, step, pairs):
    return lax.ppermute(v, "seq", [(a, a + step) for a in pairs if 0 <= a + step < n])


def gather_rows(v, z, n):
    right, left = [v], [v]
    for s in range(n - 1):
        right.append(shift(right[-1], n, 1, range(s, n)))
        left.append(shift(left[-1], n, -1, range(0, n - s)))
    out = []
    for k in range(n):
        val = v
        for d in range(1, n):
            if k + d < n:
                val = jnp.where(z == k + d, right[d], val)
            if k - d >= 0:
                val = jnp.where(z == k - d, left[d], val)
        out.append(val)
    return jnp.concatenate(out, axis=0)


def scatter_rows(v, z, n):
    part = lambda t: lax.dynamic_index_in_dim(v, jnp.clip(t, 0, n - 1), 0, keepdims=False)
    r = l = None
    for p in range(1, n):
        rv, lv = part(n - p + z), part(p - n + z)
        if r is not None:
            rv, lv = rv + r.astype(F32), lv + l.astype(F32)
        r = shift(rv.astype(BF), n, 1, range(0, p))
        l = shift(lv.astype(BF), n, -1, range(n - p, n))
    return part(z) + r.astype(F32) + l.astype(F32)


def local(
    tokens, enc_states, order, lengths, enc_lengths, attn_in, attn_out, cross_q, cross_kv,
    cross_out, ffn_in, ffn_out, proj_bias, gains, ln_bias, ffn_bias, cotangent,
):
    n_dp, n_seq = lax.axis_size("dp"), lax.axis_size("seq")
    z = lax.axis_index("seq")
    dp = lax.axis_index("dp")
    me = dp.astype(jnp.int32).reshape(1)
    fast = n_dp == 8 and attn_out.shape[1] % 128 == 0
    x = tokens[0]
    rows, width = x.shape
    enc_rows = enc_states.shape[1] * n_seq
    group_rows = rows * n_seq
    shard = attn_out.shape[1]

    x_full = gather_rows(x, z, n_seq)
    states = gather_rows(enc_states[0], z, n_seq)
    small = jnp.concatenate([proj_bias, gains, ln_bias, ffn_bias.reshape(-1, shard)], axis=0)
    count = small.shape[0]
    if fast:
        pad_rows = 32
        w = attn_in.shape[1]
        flat = jnp.concatenate([small.reshape(-1), jnp.zeros((pad_rows * w - small.size,), BF)])
        first = gather_columns(jnp.concatenate([attn_in, flat.reshape(pad_rows, w)], axis=0), me)
        w_in = first[:width]
        small_all = first[width:].reshape(pad_rows, n_dp, w).transpose(1, 0, 2).reshape(n_dp, -1)
        small_all = small_all[:, : small.size].reshape(n_dp, count, shard)
        gather = lambda v: gather_columns(v, me)
    else:
        gather = lambda v: lax.all_gather(v, "dp", axis=1, tiled=True)
        w_in = gather(attn_in)
        small_all = lax.all_gather(small, "dp", axis=0, tiled=False)
    w_ckv = gather(cross_kv)
    w_out = gather(attn_out)
    w_cq = gather(cross_q)
    w_cout = gather(cross_out)
    w_up = gather(ffn_in)
    w_down = gather(ffn_out)
    n_bias, n_norm = proj_bias.shape[0], gains.shape[0]
    rows_all = small_all[:, : n_bias + 2 * n_norm].transpose(1, 0, 2).reshape(-1, width).astype(F32)
    bias = rows_all[:n_bias]
    gain = rows_all[n_bias : n_bias + n_norm]
    shift_v = rows_all[n_bias + n_norm :]
    up_bias = small_all[:, n_bias + 2 * n_norm :].reshape(-1).astype(F32)

    place = order[0]
    seg = segment_ids(place, lengths[0])
    seg_enc = segment_ids(jnp.arange(enc_rows, dtype=jnp.int32), enc_lengths[0])
    my_place = lax.dynamic_slice_in_dim(place, z * rows, rows)
    my_seg = lax.dynamic_slice_in_dim(seg, z * rows, rows)
    self_keep = (seg[:, None] == my_seg[None, :]) & (place[:, None] <= my_place[None, :])
    self_bias = jnp.where(self_keep, 0.0, NEG).astype(F32)
    cross_bias = jnp.where(seg_enc[:, None] == my_seg[None, :], 0.0, NEG).astype(F32)
    zero_row = jnp.zeros((width,), F32)

    xf = x_full.astype(F32)
    v1, _, _ = layer_norm(xf, gain[0], shift_v[0])
    a1_full = v1.astype(BF)
    x32 = x.astype(F32)
    v1_own, xh1, rs1 = layer_norm(x32, gain[0], shift_v[0])
    a1 = v1_own.astype(BF)
    q = (dense(a1, w_in[:, :width]) + bias[0]).astype(BF)
    kv = (dense(a1_full, w_in[:, width:]) + jnp.concatenate([zero_row, bias[1]])).astype(BF)
    ekv = (dense(states, w_ckv) + jnp.concatenate([zero_row, bias[4]])).astype(BF)
    attn, lse = attn_fwd(q, kv, self_bias)
    h1 = x32 + dense(attn, w_out) + bias[2]
    v2, xh2, rs2 = layer_norm(h1, gain[1], shift_v[1])
    a2 = v2.astype(BF)
    cq = (dense(a2, w_cq) + bias[3]).astype(BF)
    cattn, clse = attn_fwd(cq, ekv, cross_bias)
    h2 = h1 + dense(cattn, w_cout) + bias[5]
    v3, xh3, rs3 = layer_norm(h2, gain[2], shift_v[2])
    a3 = v3.astype(BF)
    up = dense(a3, w_up) + up_bias
    gelu, gelu_back = jax.vjp(lambda u: jax.nn.gelu(u, approximate=True), up)
    gelu_h = gelu.astype(BF)
    h3 = h2 + dense(gelu_h, w_down) + bias[6]
    out, xh4, rs4 = layer_norm(h3, gain[3], shift_v[3])

    def reduce_dp(a, b):
        if fast:
            return scatter_columns(*wgrad(me, a, b))
        return lax.psum_scatter(dense_left(a, b), "dp", scatter_dimension=1, tiled=True).astype(BF)

    def reduce_seq(v):
        return lax.psum(v, "seq").astype(F32)

    ct = cotangent[0].astype(F32)
    g3, s3 = norm_sums(xh4, ct)
    dh3 = norm_input_grad(xh4, rs4, gain[3], ct)
    dz = dh3.astype(BF)
    g_down = reduce_dp(gelu_h, dz)
    du = gelu_back(dense_t(dz, w_down))[0].astype(BF)
    g_up = reduce_dp(a3, du)
    c3 = dense_t(du, w_up)
    g2, s2 = norm_sums(xh3, c3)
    dh2 = dh3 + norm_input_grad(xh3, rs3, gain[2], c3)
    dc = dh2.astype(BF)
    g_cout = reduce_dp(cattn, dc)
    dcattn = dense_t(dc, w_cout).astype(BF)
    dcq, dke, dve = attn_bwd(cq, ekv, cross_bias, clse, cattn, dcattn)
    dekv = jnp.concatenate([dke, dve], axis=1)
    g_cq = reduce_dp(a2, dcq)
    g_ckv = reduce_dp(states, dekv)
    enc_part = dense_t(dekv, w_ckv)
    enc_grad = scatter_rows(enc_part.reshape(n_seq, -1, width), z, n_seq)
    c2 = dense_t(dcq, w_cq)
    g1, s1 = norm_sums(xh2, c2)
    dh1 = dh2 + norm_input_grad(xh2, rs2, gain[1], c2)
    da = dh1.astype(BF)
    g_out = reduce_dp(attn, da)
    dattn = dense_t(da, w_out).astype(BF)
    dq, dk, dv = attn_bwd(q, kv, self_bias, lse, attn, dattn)
    dq_rows = lax.dynamic_update_slice(jnp.zeros((group_rows, width), BF), dq, (z * rows, 0))
    c1_part = dense_t(dk, w_in[:, width : 2 * width]) + dense_t(dv, w_in[:, 2 * width :])
    c1_q = dense_t(dq, w_in[:, :width])
    c1 = scatter_rows(c1_part.reshape(n_seq, rows, width), z, n_seq) + c1_q
    g_in = reduce_dp(a1_full, jnp.concatenate([dq_rows, dk, dv], axis=1))
    tokens_grad = dh1 + norm_input_grad(xh1, rs1, gain[0], c1)
    _, xh1_full, _ = layer_norm(xf, gain[0], shift_v[0])
    g0, s0 = (a + b for a, b in zip(norm_sums(xh1_full, c1_part), norm_sums(xh1, c1_q)))

    total = lambda v: jnp.sum(v, axis=0, dtype=F32)
    bias_rows = [total(dq), total(dv), total(dh1), total(dcq), total(dve), total(dh2), total(dh3)]
    small_rows = jnp.stack(bias_rows + [g0, g1, g2, g3, s0, s1, s2, s3])
    small_rows = small_rows.reshape(-1, n_dp, shard).transpose(1, 0, 2)
    small_rows = jnp.concatenate([small_rows, total(du).reshape(n_dp, -1, shard)], axis=1)
    small_own = lax.psum_scatter(small_rows, "dp", scatter_dimension=0, tiled=False)
    small_own = lax.psum(small_own, "seq")
    return (
        out.astype(BF)[None],
        tokens_grad[None],
        enc_grad[None],
        reduce_seq(g_in),
        reduce_seq(g_out),
        reduce_seq(g_cq),
        reduce_seq(g_ckv),
        reduce_seq(g_cout),
        reduce_seq(g_up),
        reduce_seq(g_down),
        small_own[:n_bias],
        small_own[n_bias : n_bias + n_norm],
        small_own[n_bias + n_norm : n_bias + 2 * n_norm],
        small_own[n_bias + 2 * n_norm :].reshape(1, -1),
    )


def solution(mesh):
    rows, cols, per_dp = P("dp", "seq", None), P(None, "dp"), P("dp", None)
    in_specs = (rows, rows, per_dp, per_dp, per_dp) + (cols,) * 11 + (rows,)
    out_specs = (rows,) * 3 + (cols,) * 11
    return jax.shard_map(local, mesh=mesh, in_specs=in_specs, out_specs=out_specs, check_vma=False)
```

```python
import functools

import jax
import jax.numpy as jnp
from jax import lax
from jax.experimental import pallas as pl
from jax.experimental.pallas import tpu as pltpu
from jax.sharding import PartitionSpec as P

HEADS = 16
EPSILON = 1e-05
BF = jnp.bfloat16
F32 = jnp.float32
NEG = -1e30
VMEM_LIMIT = 56 * 1024 * 1024


def params(**kw):
    return pltpu.CompilerParams(vmem_limit_bytes=VMEM_LIMIT, **kw)


def layer_norm(v, gain, shift):
    center = v - jnp.mean(v, axis=-1, keepdims=True)
    inv = lax.rsqrt(jnp.mean(center * center, axis=-1, keepdims=True) + EPSILON)
    normed = center * inv
    return normed * gain + shift, normed, inv


def norm_input_grad(normed, inv, gain, c):
    e = c * gain
    return inv * (
        e
        - jnp.mean(e, axis=-1, keepdims=True)
        - normed * jnp.mean(e * normed, axis=-1, keepdims=True)
    )


def norm_sums(normed, c):
    return jnp.sum(c * normed, axis=0), jnp.sum(c, axis=0)


def dense(a, b):
    return jnp.dot(a, b, preferred_element_type=F32)


def dense_t(a, b):
    return lax.dot_general(a, b, (((1,), (1,)), ((), ())), preferred_element_type=F32)


def dense_left(a, b):
    return lax.dot_general(a, b, (((0,), (0,)), ((), ())), preferred_element_type=F32)


def segment_ids(positions, lengths):
    ends = jnp.cumsum(lengths)
    return jnp.sum((positions[:, None] >= ends[None, :]).astype(jnp.int32), axis=1)


def split_heads(block, scale):
    head = block.shape[1] // 2
    lane = lax.broadcasted_iota(jnp.int32, block.shape, 1)
    zero = jnp.zeros_like(block)
    both = jnp.concatenate(
        [jnp.where(lane < head, block, zero), jnp.where(lane >= head, block, zero)], axis=0
    )
    return both if scale is None else both * jnp.asarray(scale, both.dtype)


def join_heads(acc):
    head, rows = acc.shape[0] // 2, acc.shape[1] // 2
    return jnp.concatenate([acc[:head, :rows], acc[head:, rows:]], axis=0)


def nt(a, b):
    return lax.dot_general(a, b, (((1,), (1,)), ((), ())), preferred_element_type=F32)


def tn(a, b):
    return lax.dot_general(a, b, (((0,), (0,)), ((), ())), preferred_element_type=F32)


def attn_fwd_kernel(scale, chunk, q_ref, k_ref, v_ref, bias_ref, o_ref, lse_ref, acc_ref, m_ref, l_ref):
    both = split_heads(q_ref[...], scale)
    acc_ref[...] = jnp.zeros_like(acc_ref)
    m_ref[...] = jnp.full_like(m_ref, NEG)
    l_ref[...] = jnp.zeros_like(l_ref)

    @pl.loop(0, k_ref.shape[0] // chunk)
    def _(c):
        rows = pl.ds(pl.multiple_of(c * chunk, chunk), chunk)
        b = bias_ref[rows, :]
        s = nt(k_ref[rows, :], both) + jnp.concatenate([b, b], axis=1)
        m_old = m_ref[...]
        m_new = jnp.maximum(m_old, jnp.max(s, axis=0, keepdims=True))
        alpha = jnp.exp(m_old - m_new)
        p = jnp.exp(s - m_new)
        m_ref[...] = m_new
        l_ref[...] = l_ref[...] * alpha + jnp.sum(p, axis=0, keepdims=True)
        acc_ref[...] = acc_ref[...] * alpha + tn(v_ref[rows, :], p.astype(BF))

    total = l_ref[...]
    o_ref[...] = jnp.transpose(join_heads(acc_ref[...] / total)).astype(BF)
    lse_ref[0] = m_ref[...] + jnp.log(total)


def attn_fwd(q, kv, bias, first=0, count=HEADS // 2):
    nq, width = q.shape
    nk = kv.shape[0]
    head = width // HEADS
    pairs, pw = HEADS // 2, 2 * head
    chunk = 256
    return pl.pallas_call(
        functools.partial(attn_fwd_kernel, head**-0.5, chunk),
        grid=(count,),
        in_specs=[
            pl.BlockSpec((nq, pw), lambda i: (0, first + i)),
            pl.BlockSpec((nk, pw), lambda i: (0, first + i)),
            pl.BlockSpec((nk, pw), lambda i: (0, pairs + first + i)),
            pl.BlockSpec((nk, nq), lambda i: (0, 0)),
        ],
        out_specs=[
            pl.BlockSpec((nq, pw), lambda i: (0, i)),
            pl.BlockSpec((1, 1, 2 * nq), lambda i: (i, 0, 0)),
        ],
        out_shape=[
            jax.ShapeDtypeStruct((nq, count * pw), BF),
            jax.ShapeDtypeStruct((count, 1, 2 * nq), F32),
        ],
        scratch_shapes=[
            pltpu.VMEM((pw, 2 * nq), F32),
            pltpu.VMEM((1, 2 * nq), F32),
            pltpu.VMEM((1, 2 * nq), F32),
        ],
        compiler_params=params(),
        cost_estimate=pl.CostEstimate(
            flops=16 * count * nq * nk * head,
            bytes_accessed=4 * nk * count * pw + 4 * nq * count * pw + 4 * nk * nq,
            transcendentals=2 * count * nq * nk,
        ),
    )(q, kv, kv, bias)


def attn_bwd_kernel(
    scale, chunk, q_ref, k_ref, v_ref, do_ref, bias_ref, lse_ref, delta_ref, dq_ref, dk_ref, dv_ref, acc_ref
):
    both = split_heads(q_ref[...], scale)
    dboth = split_heads(do_ref[...], None)
    acc_ref[...] = jnp.zeros_like(acc_ref)
    lse = lse_ref[0]
    delta = delta_ref[0]

    @pl.loop(0, k_ref.shape[0] // chunk)
    def _(c):
        rows = pl.ds(pl.multiple_of(c * chunk, chunk), chunk)
        b = bias_ref[rows, :]
        k = k_ref[rows, :]
        p = jnp.exp(nt(k, both) + jnp.concatenate([b, b], axis=1) - lse)
        ds = (p * (nt(v_ref[rows, :], dboth) - delta)).astype(BF)
        dk_ref[rows, :] = dense(ds, both).astype(BF)
        dv_ref[rows, :] = dense(p.astype(BF), dboth).astype(BF)
        acc_ref[...] += tn(k, ds)

    dq_ref[...] = jnp.transpose(join_heads(acc_ref[...]) * scale).astype(BF)


def attn_delta(out, dout):
    nq, width = out.shape
    delta = jnp.sum((dout.astype(F32) * out.astype(F32)).reshape(nq, HEADS, width // HEADS), axis=-1)
    return delta.T.reshape(HEADS // 2, 1, 2 * nq)


def attn_bwd(q, kv, bias, lse, delta, dout, first=0, count=HEADS // 2):
    nq, width = q.shape
    nk = kv.shape[0]
    head = width // HEADS
    pairs, pw = HEADS // 2, 2 * head
    chunk = 256
    row_spec = pl.BlockSpec((nq, pw), lambda i: (0, first + i))
    key_spec = pl.BlockSpec((nk, pw), lambda i: (0, first + i))
    vec_spec = pl.BlockSpec((1, 1, 2 * nq), lambda i: (first + i, 0, 0))
    new_spec = lambda n: pl.BlockSpec((n, pw), lambda i: (0, i))
    return pl.pallas_call(
        functools.partial(attn_bwd_kernel, head**-0.5, chunk),
        grid=(count,),
        in_specs=[
            row_spec,
            key_spec,
            pl.BlockSpec((nk, pw), lambda i: (0, pairs + first + i)),
            row_spec,
            pl.BlockSpec((nk, nq), lambda i: (0, 0)),
            vec_spec,
            vec_spec,
        ],
        out_specs=[new_spec(nq), new_spec(nk), new_spec(nk)],
        out_shape=[
            jax.ShapeDtypeStruct((nq, count * pw), BF),
            jax.ShapeDtypeStruct((nk, count * pw), BF),
            jax.ShapeDtypeStruct((nk, count * pw), BF),
        ],
        scratch_shapes=[pltpu.VMEM((pw, 2 * nq), F32)],
        compiler_params=params(),
        cost_estimate=pl.CostEstimate(
            flops=40 * count * nq * nk * head,
            bytes_accessed=8 * nk * count * pw + 6 * nq * count * pw + 4 * nk * nq,
            transcendentals=2 * count * nq * nk,
        ),
    )(q, kv, kv, dout, bias, lse, delta)


def swap(v, bit):
    return lax.ppermute(v, "dp", [(i, i ^ bit) for i in range(8)])


def assemble_kernel(widths, me_ref, *refs):
    ins, out_refs = refs[:10], refs[10:]
    upper = pl.program_id(0) < pl.num_programs(0) // 2
    start = 0
    for n, out_ref in zip(widths, out_refs):
        cols = slice(start, start + n)
        start += n

        def put(t, i, value):
            d = jnp.bitwise_xor(me_ref[0], 2 * i + t)
            out_ref[:, pl.ds(pl.multiple_of(d * n, 128), n)] = value

        for t in (0, 1):
            for i in range(3):
                put(t, i, ins[5 * t + i][:, cols])

            @pl.when(upper)
            def _():
                put(t, 3, ins[5 * t + 3][:, cols])

            @pl.when(jnp.logical_not(upper))
            def _():
                put(t, 3, ins[5 * t + 4][:, cols])


def assemble(me, mine, other, widths):
    rows, total = mine[0].shape
    block = next(b for b in (512, 256, 176, 128, 96, 64, 32, 16) if rows // 2 % b == 0)
    last = rows // 2 // block - 1
    every = pl.BlockSpec((block, total), lambda i, me_ref: (i, 0))
    upper = pl.BlockSpec((block, total), lambda i, me_ref: (jnp.minimum(i, last), 0))
    lower = pl.BlockSpec((block, total), lambda i, me_ref: (jnp.maximum(i - last - 1, 0), 0))
    return pl.pallas_call(
        functools.partial(assemble_kernel, widths),
        grid_spec=pltpu.PrefetchScalarGridSpec(
            num_scalar_prefetch=1,
            grid=(rows // block,),
            in_specs=[every, every, every, upper, lower] * 2,
            out_specs=[pl.BlockSpec((block, 8 * n), lambda i, me_ref: (i, 0)) for n in widths],
        ),
        out_shape=[jax.ShapeDtypeStruct((rows, 8 * n), BF) for n in widths],
        compiler_params=params(),
        cost_estimate=pl.CostEstimate(flops=0, bytes_accessed=32 * rows * total, transcendentals=0),
    )(me, *mine, *other)


def after(v, *others):
    return lax.optimization_barrier((v,) + others)[0]


def all_after(vs, *others):
    return lax.optimization_barrier(tuple(vs) + others)[: len(vs)]


def send_shard(ws, *wait):
    w = after(jnp.concatenate(ws, axis=1) if len(ws) > 1 else ws[0], *wait)
    return w, swap(w, 2), swap(w, 4)


def send_diagonal(got, *wait):
    x, y = all_after(got[1:], *wait)
    half = x.shape[0] // 2
    return swap(x[:half], 4), swap(y[half:], 2)


def send_core(parts, *wait):
    parts = all_after(parts, *wait)
    return parts, tuple(swap(v, 1) for v in parts)


def wgrad_kernel(me_ref, x_ref, keep_in, send_in, *refs):
    keep_ref, send_ref, xt_ref = refs[-3:]

    @pl.when(pl.program_id(0) == 0)
    def _():
        xt_ref[...] = jnp.transpose(x_ref[...])

    rows, n = xt_ref.shape[0], keep_in.shape[1]
    res = dense(xt_ref[...], jnp.concatenate([keep_in[...], send_in[...]], axis=1))
    for t, ref in enumerate((keep_ref, send_ref)):
        for j in range(n // 128):
            ref[0, j * rows : (j + 1) * rows] = res[:, t * n + j * 128 : t * n + (j + 1) * 128].astype(BF)


def wgrad(me, x, dy, into=None, at=0, whole=None):
    tok, rows = x.shape
    n = dy.shape[1] // 8
    stacked = n // 128 * rows
    col = lambda t: lambda i, me_ref: (0, jnp.bitwise_xor(me_ref[0], 2 * i + t))
    out_spec = pl.BlockSpec((1, stacked, 128), lambda i, me_ref: (i, at, 0))
    in_specs = [
        pl.BlockSpec((tok, rows), lambda i, me_ref: (0, 0)),
        pl.BlockSpec((tok, n), col(0)),
        pl.BlockSpec((tok, n), col(1)),
    ]
    extra = () if into is None else tuple(into)
    height = extra[0].shape[1] if extra else whole or stacked
    return pl.pallas_call(
        wgrad_kernel,
        grid_spec=pltpu.PrefetchScalarGridSpec(
            num_scalar_prefetch=1,
            grid=(4,),
            in_specs=in_specs + [pl.BlockSpec(memory_space=pl.ANY)] * len(extra),
            out_specs=[out_spec, out_spec],
            scratch_shapes=[pltpu.VMEM((rows, tok), BF)],
        ),
        out_shape=[jax.ShapeDtypeStruct((4, height, 128), BF)] * 2,
        input_output_aliases={4: 0, 5: 1} if extra else {},
        compiler_params=params(),
        cost_estimate=pl.CostEstimate(
            flops=2 * tok * rows * 8 * n,
            bytes_accessed=2 * (tok * rows + tok * 8 * n + rows * 8 * n),
            transcendentals=0,
        ),
    )(me, x, dy, dy, *extra)


def add(*terms):
    total = terms[0].astype(F32)
    for t in terms[1:]:
        total = total + t.astype(F32)
    return total.astype(BF)


def pick(v, i, half):
    rows = v.shape[1] // 2
    return v[i, half * rows : (half + 1) * rows]


def sum_near(keep, got, *wait):
    keep, got = all_after((keep, got), *wait)
    term = lambda i, h: add(pick(keep, i, h), pick(got, i, h))
    xa = swap(jnp.stack([term(1, 0), term(3, 0)]), 2)
    yb = swap(jnp.stack([term(2, 1), term(3, 1)]), 4)
    return xa, yb


def sum_far(keep, got, near, *wait):
    xa, yb, keep, got = all_after(tuple(near) + (keep, got), *wait)
    ya = swap(add(pick(keep, 2, 0), pick(got, 2, 0), xa[1]), 4)
    xb = swap(add(pick(keep, 1, 1), pick(got, 1, 1), yb[1]), 2)
    return ya, xb


def sum_own(keep, got, near, far):
    halves = [add(pick(keep, 0, h), pick(got, 0, h), near[h][0], far[h]) for h in (0, 1)]
    return jnp.concatenate(halves, axis=0)


def shift(v, n, step, pairs):
    return lax.ppermute(v, "seq", [(a, a + step) for a in pairs if 0 <= a + step < n])


def gather_rows(v, z, n):
    right, left = [v], [v]
    for s in range(n - 1):
        right.append(shift(right[-1], n, 1, range(s, n)))
        left.append(shift(left[-1], n, -1, range(0, n - s)))
    out = []
    for k in range(n):
        val = v
        for d in range(1, n):
            if k + d < n:
                val = jnp.where(z == k + d, right[d], val)
            if k - d >= 0:
                val = jnp.where(z == k - d, left[d], val)
        out.append(val)
    return jnp.concatenate(out, axis=0)


def scatter_rows(v, z, n):
    part = lambda t: lax.dynamic_index_in_dim(v, jnp.clip(t, 0, n - 1), 0, keepdims=False).astype(F32)
    r = l = None
    for p in range(1, n):
        rv, lv = part(n - p + z), part(p - n + z)
        if r is not None:
            rv, lv = rv + r.astype(F32), lv + l.astype(F32)
        r = shift(rv.astype(BF), n, 1, range(0, p))
        l = shift(lv.astype(BF), n, -1, range(n - p, n))
    return part(z) + r.astype(F32) + l.astype(F32)


def local(
    tokens, enc_states, order, lengths, enc_lengths, attn_in, attn_out, cross_q, cross_kv,
    cross_out, ffn_in, ffn_out, proj_bias, gains, ln_bias, ffn_bias, cotangent,
):
    n_dp, n_seq = lax.axis_size("dp"), lax.axis_size("seq")
    z = lax.axis_index("seq")
    dp = lax.axis_index("dp")
    me = dp.astype(jnp.int32).reshape(1)
    fast = n_dp == 8 and n_seq == 4 and attn_out.shape[1] % 128 == 0
    x = tokens[0]
    rows, width = x.shape
    enc_rows = enc_states.shape[1] * n_seq
    group_rows = rows * n_seq
    shard = attn_out.shape[1]

    small = jnp.concatenate([proj_bias, gains, ln_bias, ffn_bias.reshape(-1, shard)], axis=0)
    count = small.shape[0]
    if fast:
        pad_rows = 32
        w = attn_in.shape[1]
        flat = jnp.concatenate([small.reshape(-1), jnp.zeros((pad_rows * w - small.size,), BF)])
        a_near = send_shard([jnp.concatenate([attn_in, flat.reshape(pad_rows, w)], axis=0)])
        x_full = lax.all_gather(x, "seq", axis=0, tiled=True)
        a_far = send_diagonal(a_near)
        b_near = send_shard([cross_kv, attn_out, cross_q, cross_out], *a_near[1:])
        states = lax.all_gather(after(enc_states[0], x_full), "seq", axis=0, tiled=True)
        (first,) = assemble(me, *send_core(a_near + a_far), (w,))
        b_far = send_diagonal(b_near, first)
        w_in = first[:width]
        small_all = first[width:].reshape(pad_rows, n_dp, w).transpose(1, 0, 2).reshape(n_dp, -1)
        small_all = small_all[:, : small.size].reshape(n_dp, count, shard)
    else:
        x_full = gather_rows(x, z, n_seq)
        states = gather_rows(enc_states[0], z, n_seq)
        gather = lambda v: lax.all_gather(v, "dp", axis=1, tiled=True)
        w_in, w_ckv, w_out, w_cq = gather(attn_in), gather(cross_kv), gather(attn_out), gather(cross_q)
        w_cout, w_up, w_down = gather(cross_out), gather(ffn_in), gather(ffn_out)
        small_all = lax.all_gather(small, "dp", axis=0, tiled=False)
    n_bias, n_norm = proj_bias.shape[0], gains.shape[0]
    rows_all = small_all[:, : n_bias + 2 * n_norm].transpose(1, 0, 2).reshape(-1, width).astype(F32)
    bias = rows_all[:n_bias]
    gain = rows_all[n_bias : n_bias + n_norm]
    shift_v = rows_all[n_bias + n_norm :]
    up_bias = small_all[:, n_bias + 2 * n_norm :].reshape(-1).astype(F32)

    place = order[0]
    seg = segment_ids(place, lengths[0])
    seg_enc = segment_ids(jnp.arange(enc_rows, dtype=jnp.int32), enc_lengths[0])
    my_place = lax.dynamic_slice_in_dim(place, z * rows, rows)
    my_seg = lax.dynamic_slice_in_dim(seg, z * rows, rows)
    self_keep = (seg[:, None] == my_seg[None, :]) & (place[:, None] <= my_place[None, :])
    self_bias = jnp.where(self_keep, 0.0, NEG).astype(F32)
    cross_bias = jnp.where(seg_enc[:, None] == my_seg[None, :], 0.0, NEG).astype(F32)
    zero_row = jnp.zeros((width,), F32)

    xf = x_full.astype(F32)
    v1, _, _ = layer_norm(xf, gain[0], shift_v[0])
    a1_full = v1.astype(BF)
    x32 = x.astype(F32)
    v1_own, xh1, rs1 = layer_norm(x32, gain[0], shift_v[0])
    a1 = v1_own.astype(BF)
    kv = (dense(a1_full, w_in[:, width:]) + jnp.concatenate([zero_row, bias[1]])).astype(BF)
    q = (dense(a1, w_in[:, :width]) + bias[0]).astype(BF)
    if fast:
        b_parts, b_other = send_core(b_near + b_far, kv)
        c_near = send_shard([ffn_in], kv)
        q, kv, *_ = all_after((q, kv), *b_far, states)
    half = HEADS // 4
    attn_a, lse_a = attn_fwd(q, kv, self_bias, 0, half)
    if fast:
        q, attn_a, lse_a = all_after((q, attn_a, lse_a), *c_near[1:], *b_other)
        c_far = send_diagonal(c_near, attn_a)
        d_near = send_shard([ffn_out], attn_a)
    attn_b, lse_b = attn_fwd(q, kv, self_bias, half, half)
    attn = jnp.concatenate([attn_a, attn_b], axis=1)
    lse = jnp.concatenate([lse_a, lse_b], axis=0)
    if fast:
        attn, lse = all_after((attn, lse), *c_far)
        widths = tuple(v.shape[1] for v in (cross_kv, attn_out, cross_q, cross_out))
        c_parts, c_other = send_core(c_near + c_far, attn)
        b_parts = all_after(b_parts, attn)
        w_ckv, w_out, w_cq, w_cout = assemble(me, b_parts, b_other, widths)
    h1 = x32 + dense(attn, w_out) + bias[2]
    v2, xh2, rs2 = layer_norm(h1, gain[1], shift_v[1])
    a2 = v2.astype(BF)
    cq = (dense(a2, w_cq) + bias[3]).astype(BF)
    ekv = (dense(states, w_ckv) + jnp.concatenate([zero_row, bias[4]])).astype(BF)
    if fast:
        cq = after(cq, ekv, *c_other, *d_near[1:])
        d_far = send_diagonal(d_near, cq)
    cattn, clse = attn_fwd(cq, ekv, cross_bias)
    if fast:
        cattn = after(cattn, *d_far)
        d_parts, d_other = send_core(d_near + d_far, cattn)
        c_parts = all_after(c_parts, cattn)
        (w_up,) = assemble(me, c_parts, c_other, (ffn_in.shape[1],))
    h2 = h1 + dense(cattn, w_cout) + bias[5]
    v3, xh3, rs3 = layer_norm(h2, gain[2], shift_v[2])
    a3 = v3.astype(BF)
    up = dense(a3, w_up) + up_bias
    gelu, gelu_back = jax.vjp(lambda u: jax.nn.gelu(u, approximate=True), up)
    gelu_h = gelu.astype(BF)
    if fast:
        d_parts = all_after(d_parts, gelu_h)
        (w_down,) = assemble(me, d_parts, d_other, (shard,))
    h3 = h2 + dense(gelu_h, w_down) + bias[6]
    out, xh4, rs4 = layer_norm(h3, gain[3], shift_v[3])

    total = lambda v: jnp.sum(v, axis=0, dtype=F32)
    by_columns = lambda a, b: lax.psum_scatter(dense_left(a, b), "dp", scatter_dimension=1, tiled=True).astype(BF)
    by_chain = lambda v: lax.psum(v, "seq")
    ct = cotangent[0].astype(F32)
    g3, s3 = norm_sums(xh4, ct)
    dh3 = norm_input_grad(xh4, rs4, gain[3], ct)
    dz = dh3.astype(BF)
    if fast:
        d_keep, d_send = wgrad(me, gelu_h, dz)
        dz, d_keep, d_send = all_after((dz, d_keep, d_send))
        d_got = swap(d_send, 1)
    du = gelu_back(dense_t(dz, w_down))[0].astype(BF)
    if fast:
        du, d_got = all_after((du, d_got))
        d_n = sum_near(d_keep, d_got, du)
        c_keep, c_send = wgrad(me, a3, du)
        du, c_send = all_after((du, c_send))
        c_got = swap(c_send, 1)
    c3 = dense_t(du, w_up)
    g2, s2 = norm_sums(xh3, c3)
    dh2 = dh3 + norm_input_grad(xh3, rs3, gain[2], c3)
    dc = dh2.astype(BF)
    if fast:
        dc, c_got = all_after((dc, c_got))
        e_rows = (2 * shard + cross_kv.shape[1]) // 128 * width
        e_grads = wgrad(me, cattn, dc, None, 0, e_rows)
        dc, *e_grads = all_after((dc, *e_grads))
    dcattn = dense_t(dc, w_cout).astype(BF)
    cdelta = attn_delta(cattn, dcattn)
    if fast:
        dcattn, cdelta = all_after((dcattn, cdelta), *d_n)
        d_f = sum_far(d_keep, d_got, d_n, dcattn)
    dcq, dke, dve = attn_bwd(cq, ekv, cross_bias, clse, cdelta, dcattn)
    dekv = jnp.concatenate([dke, dve], axis=1)
    if fast:
        dcq, dekv = all_after((dcq, dekv), *d_f)
        c_n = sum_near(c_keep, c_got, dcq)
        e_grads = wgrad(me, a2, dcq, e_grads, 1)
        e_keep, e_send = wgrad(me, states, dekv, e_grads, 1)
        dcq, dekv, e_keep, e_send = all_after((dcq, dekv, e_keep, e_send))
        e_got = swap(e_send, 1)
        d_all = by_chain(sum_own(d_keep, d_got, d_n, d_f))
        enc_part = dense_t(dekv, w_ckv).astype(BF)
        dcq, enc_part = all_after((dcq, enc_part))
        enc_part = after(enc_part, d_all)
        enc_sum = lax.psum_scatter(enc_part, "seq", scatter_dimension=0, tiled=True)
        enc_grad = enc_sum.astype(F32)
    c2 = dense_t(dcq, w_cq)
    g1, s1 = norm_sums(xh2, c2)
    dh1 = dh2 + norm_input_grad(xh2, rs2, gain[1], c2)
    da = dh1.astype(BF)
    if fast:
        i_rows = (shard + attn_in.shape[1]) // 128 * width
        i_grads = wgrad(me, attn, da, None, attn_in.shape[1] // 128, i_rows)
        da, *i_grads = all_after((da, *i_grads), *c_n, e_got)
        c_f = sum_far(c_keep, c_got, c_n, da)
    dattn = dense_t(da, w_out).astype(BF)
    delta = attn_delta(attn, dattn)
    if fast:
        dattn, delta = all_after((dattn, delta), *c_f, enc_sum)
        e_n = sum_near(e_keep, e_got, dattn)
        c_sum = sum_own(c_keep, c_got, c_n, c_f)
        c_all = by_chain(after(c_sum, enc_sum))
    dq_a, dk_a, dv_a = attn_bwd(q, kv, self_bias, lse, delta, dattn, 0, 5)
    if fast:
        dattn, dq_a, dk_a, dv_a = all_after((dattn, dq_a, dk_a, dv_a), *e_n)
        e_f = sum_far(e_keep, e_got, e_n, dattn)
    dq_b, dk_b, dv_b = attn_bwd(q, kv, self_bias, lse, delta, dattn, 5, 3)
    if fast:
        dq_b, dk_b, dv_b = all_after((dq_b, dk_b, dv_b), *e_f)
        e_sum = sum_own(e_keep, e_got, e_n, e_f)
        e_all = by_chain(after(e_sum, c_all))
    dq, dk, dv = (jnp.concatenate(p, axis=1) for p in ((dq_a, dq_b), (dk_a, dk_b), (dv_a, dv_b)))
    dq_rows = lax.dynamic_update_slice(jnp.zeros((group_rows, width), BF), dq, (z * rows, 0))
    dqkv = jnp.concatenate([dq_rows, dk, dv], axis=1)
    if fast:
        i_keep, i_send = wgrad(me, a1_full, dqkv, i_grads, 0)
        dq, dk, dv, i_keep, i_send = all_after((dq, dk, dv, i_keep, i_send), c_all)
        i_got = swap(i_send, 1)
    c1_part = dense_t(dk, w_in[:, width : 2 * width]) + dense_t(dv, w_in[:, 2 * width :])
    c1_q = dense_t(dq, w_in[:, :width])
    if fast:
        c1_part, i_got = all_after((c1_part, i_got))
        c1_sum = scatter_rows(c1_part.astype(BF).reshape(n_seq, rows, width), z, n_seq)
        i_n = sum_near(i_keep, i_got)
        i_f = sum_far(i_keep, i_got, i_n, e_all)
        i_sum = scatter_rows(sum_own(i_keep, i_got, i_n, i_f).reshape(n_seq, -1, 128), z, n_seq)
        i_all = gather_rows(i_sum.astype(BF), z, n_seq)
        c1 = c1_sum + c1_q
        flat_out = lambda v, r: jnp.concatenate(jnp.split(v, v.shape[0] // r, axis=0), axis=1).astype(F32)
        r_up, r_down = flat_out(c_all, width), d_all.astype(F32)
        r_in, r_out = flat_out(i_all[:-width], width), i_all[-width:].astype(F32)
        r_cout, r_cq, r_ckv = (flat_out(v, width) for v in jnp.split(e_all, [width, 2 * width], axis=0))
    else:
        c1 = lax.psum_scatter(c1_part, "seq", scatter_dimension=0, tiled=True) + c1_q
        enc_grad = lax.psum_scatter(dense_t(dekv, w_ckv), "seq", scatter_dimension=0, tiled=True)
        pairs = [(a1_full, dqkv), (attn, da), (a2, dcq), (states, dekv), (cattn, dc), (a3, du), (gelu_h, dz)]
        grads = [by_chain(by_columns(a, b)).astype(F32) for a, b in pairs]
        r_in, r_out, r_cq, r_ckv, r_cout, r_up, r_down = grads
    tokens_grad = dh1 + norm_input_grad(xh1, rs1, gain[0], c1)
    _, xh1_full, _ = layer_norm(xf, gain[0], shift_v[0])
    g0, s0 = (a + b for a, b in zip(norm_sums(xh1_full, c1_part), norm_sums(xh1, c1_q)))

    bias_rows = [total(dq), total(dv), total(dh1), total(dcq), total(dve), total(dh2), total(dh3)]
    small_rows = jnp.stack(bias_rows + [g0, g1, g2, g3, s0, s1, s2, s3])
    small_rows = small_rows.reshape(-1, n_dp, shard).transpose(1, 0, 2)
    small_rows = jnp.concatenate([small_rows, total(du).reshape(n_dp, -1, shard)], axis=1)
    if fast:
        for bit in (1, 2, 4):
            small_rows = small_rows + swap(small_rows, bit)
        for bit in (1, 2):
            small_rows = small_rows + lax.ppermute(small_rows, "seq", [(i, i ^ bit) for i in range(n_seq)])
    else:
        small_rows = lax.psum(small_rows, ("dp", "seq"))
    small_own = lax.dynamic_index_in_dim(small_rows, dp, 0, keepdims=False)
    return (
        out.astype(BF)[None],
        tokens_grad[None],
        enc_grad[None],
        r_in,
        r_out,
        r_cq,
        r_ckv,
        r_cout,
        r_up,
        r_down,
        small_own[:n_bias],
        small_own[n_bias : n_bias + n_norm],
        small_own[n_bias + n_norm : n_bias + 2 * n_norm],
        small_own[n_bias + 2 * n_norm :].reshape(1, -1),
    )


def solution(mesh):
    rows, cols, per_dp = P("dp", "seq", None), P(None, "dp"), P("dp", None)
    in_specs = (rows, rows, per_dp, per_dp, per_dp) + (cols,) * 11 + (rows,)
    out_specs = (rows,) * 3 + (cols,) * 11
    return jax.shard_map(local, mesh=mesh, in_specs=in_specs, out_specs=out_specs, check_vma=False)
```

```python
import functools

import jax
import jax.numpy as jnp
from jax import lax
from jax.experimental import pallas as pl
from jax.experimental.pallas import tpu as pltpu
from jax.sharding import PartitionSpec as P

HEADS = 16
EPSILON = 1e-05
BF = jnp.bfloat16
F32 = jnp.float32
NEG = -1e30
VMEM_LIMIT = 56 * 1024 * 1024
SHORT = pl.CostEstimate(flops=0, bytes_accessed=0, transcendentals=0)


def params(**kw):
    return pltpu.CompilerParams(vmem_limit_bytes=VMEM_LIMIT, **kw)


def layer_norm(v, gain, shift):
    center = v - jnp.mean(v, axis=-1, keepdims=True)
    inv = lax.rsqrt(jnp.mean(center * center, axis=-1, keepdims=True) + EPSILON)
    normed = center * inv
    return normed * gain + shift, normed, inv


def norm_input_grad(normed, inv, gain, c):
    e = c * gain
    return inv * (
        e
        - jnp.mean(e, axis=-1, keepdims=True)
        - normed * jnp.mean(e * normed, axis=-1, keepdims=True)
    )


def norm_sums(normed, c):
    return jnp.sum(c * normed, axis=0), jnp.sum(c, axis=0)


def dense(a, b):
    return jnp.dot(a, b, preferred_element_type=F32)


def dense_t(a, b):
    return lax.dot_general(a, b, (((1,), (1,)), ((), ())), preferred_element_type=F32)


def dense_left(a, b):
    return lax.dot_general(a, b, (((0,), (0,)), ((), ())), preferred_element_type=F32)


def gelu_both(u):
    c = 0.7978845608028654
    sq = u * u
    t = jnp.tanh(c * u * (1.0 + 0.044715 * sq))
    half = 0.5 * (1.0 + t)
    return u * half, half + 0.5 * c * u * (1.0 - t * t) * (1.0 + 0.134145 * sq)


def segment_ids(positions, lengths):
    ends = jnp.cumsum(lengths)
    return jnp.sum((positions[:, None] >= ends[None, :]).astype(jnp.int32), axis=1)


def split_heads(block, scale):
    head = block.shape[1] // 2
    lane = lax.broadcasted_iota(jnp.int32, block.shape, 1)
    zero = jnp.zeros_like(block)
    both = jnp.concatenate(
        [jnp.where(lane < head, block, zero), jnp.where(lane >= head, block, zero)], axis=0
    )
    return both if scale is None else both * jnp.asarray(scale, both.dtype)


def join_heads(acc):
    head, rows = acc.shape[0] // 2, acc.shape[1] // 2
    return jnp.concatenate([acc[:head, :rows], acc[head:, rows:]], axis=0)


def nt(a, b):
    return lax.dot_general(a, b, (((1,), (1,)), ((), ())), preferred_element_type=F32)


def tn(a, b):
    return lax.dot_general(a, b, (((0,), (0,)), ((), ())), preferred_element_type=F32)


def attn_fwd_kernel(scale, chunk, q_ref, k_ref, v_ref, bias_ref, o_ref, lse_ref):
    both = split_heads(q_ref[...], scale)
    top = jnp.full(lse_ref.shape[1:], NEG, F32)
    total = jnp.zeros_like(top)
    acc = None
    for c in range(k_ref.shape[0] // chunk):
        rows = slice(c * chunk, (c + 1) * chunk)
        b = bias_ref[rows, :]
        s = nt(k_ref[rows, :], both) + jnp.concatenate([b, b], axis=1)
        new = jnp.maximum(top, jnp.max(s, axis=0, keepdims=True))
        p = jnp.exp(s - new)
        part = tn(v_ref[rows, :], p.astype(BF))
        if acc is None:
            total, acc = jnp.sum(p, axis=0, keepdims=True), part
        else:
            alpha = jnp.exp(top - new)
            total = total * alpha + jnp.sum(p, axis=0, keepdims=True)
            acc = acc * alpha + part
        top = new
    o_ref[...] = jnp.transpose(join_heads(acc / total)).astype(BF)
    lse_ref[0] = top + jnp.log(total)


def attn_fwd(q, kv, bias, first=0, count=HEADS // 2):
    nq, width = q.shape
    nk = kv.shape[0]
    head = width // HEADS
    pairs, pw = HEADS // 2, 2 * head
    chunk = 512
    return pl.pallas_call(
        functools.partial(attn_fwd_kernel, head**-0.5, chunk),
        grid=(count,),
        in_specs=[
            pl.BlockSpec((nq, pw), lambda i: (0, first + i)),
            pl.BlockSpec((nk, pw), lambda i: (0, first + i)),
            pl.BlockSpec((nk, pw), lambda i: (0, pairs + first + i)),
            pl.BlockSpec((nk, nq), lambda i: (0, 0)),
        ],
        out_specs=[
            pl.BlockSpec((nq, pw), lambda i: (0, i)),
            pl.BlockSpec((1, 1, 2 * nq), lambda i: (i, 0, 0)),
        ],
        out_shape=[
            jax.ShapeDtypeStruct((nq, count * pw), BF),
            jax.ShapeDtypeStruct((count, 1, 2 * nq), F32),
        ],
        compiler_params=params(),
        cost_estimate=SHORT,
    )(q, kv, kv, bias)


def attn_bwd_kernel(scale, chunk, padded, z_ref, q_ref, k_ref, v_ref, do_ref, out_ref, bias_ref, lse_ref, *refs):
    dq_ref, dkv_ref = refs[-2:]
    both = split_heads(q_ref[...], scale)
    dboth = split_heads(do_ref[...], None)
    lse = lse_ref[0]
    prod = do_ref[...].astype(F32) * out_ref[...].astype(F32)
    head = prod.shape[1] // 2
    lane = lax.broadcasted_iota(jnp.int32, (8, 2 * head), 1)
    row = lax.broadcasted_iota(jnp.int32, (8, 2 * head), 0)
    pick_head = jnp.where(lane // head == row, 1.0, 0.0)
    delta = lax.dot_general(
        pick_head, prod, (((1,), (1,)), ((), ())), precision=lax.Precision.HIGHEST, preferred_element_type=F32
    )
    delta = jnp.concatenate([delta[0:1], delta[1:2]], axis=1)
    acc = 0.0
    for c in range(k_ref.shape[0] // chunk):
        rows = slice(c * chunk, (c + 1) * chunk)
        b = bias_ref[rows, :]
        k = k_ref[rows, :]
        p = jnp.exp(nt(k, both) + jnp.concatenate([b, b], axis=1) - lse)
        ds = (p * (nt(v_ref[rows, :], dboth) - delta)).astype(BF)
        dkv_ref[padded, rows, :] = dense(ds, both).astype(BF)
        dkv_ref[padded + 1, rows, :] = dense(p.astype(BF), dboth).astype(BF)
        acc = acc + tn(k, ds)
    dq = jnp.transpose(join_heads(acc) * scale).astype(BF)
    dq_ref[...] = dq
    if padded:
        n = dq.shape[0]
        dkv_ref[0] = jnp.zeros(dkv_ref.shape[1:], BF)
        dkv_ref[0, pl.ds(pl.multiple_of(z_ref[0] * n, n), n), :] = dq


def attn_bwd(z, q, kv, bias, lse, out, dout, padded, first=0, count=HEADS // 2, into=()):
    nq, width = q.shape
    nk = kv.shape[0]
    head = width // HEADS
    pairs, pw = HEADS // 2, 2 * head
    chunk = 512
    row_spec = pl.BlockSpec((nq, pw), lambda i, z_ref: (0, first + i))
    key_spec = pl.BlockSpec((nk, pw), lambda i, z_ref: (0, first + i))
    vec_spec = pl.BlockSpec((1, 1, 2 * nq), lambda i, z_ref: (first + i, 0, 0))
    depth = 3 if padded else 2
    return pl.pallas_call(
        functools.partial(attn_bwd_kernel, head**-0.5, chunk, depth - 2),
        grid_spec=pltpu.PrefetchScalarGridSpec(
            num_scalar_prefetch=1,
            grid=(count,),
            in_specs=[
                row_spec,
                key_spec,
                pl.BlockSpec((nk, pw), lambda i, z_ref: (0, pairs + first + i)),
                row_spec,
                row_spec,
                pl.BlockSpec((nk, nq), lambda i, z_ref: (0, 0)),
                vec_spec,
            ]
            + [pl.BlockSpec(memory_space=pl.ANY)] * len(into),
            out_specs=[row_spec, pl.BlockSpec((depth, nk, pw), lambda i, z_ref: (0, 0, first + i))],
        ),
        out_shape=[
            jax.ShapeDtypeStruct((nq, width), BF),
            jax.ShapeDtypeStruct((depth, nk, width), BF),
        ],
        input_output_aliases={8: 0, 9: 1} if into else {},
        compiler_params=params(),
        cost_estimate=SHORT,
    )(z, q, kv, kv, dout, out, bias, lse, *into)


def swap(v, bit):
    return lax.ppermute(v, "dp", [(i, i ^ bit) for i in range(8)])


def assemble_kernel(widths, me_ref, *refs):
    ins, out_refs = refs[:10], refs[10:]
    upper = pl.program_id(0) < pl.num_programs(0) // 2
    start = 0
    for n, out_ref in zip(widths, out_refs):
        cols = slice(start, start + n)
        start += n

        def put(t, i, value):
            d = jnp.bitwise_xor(me_ref[0], 2 * i + t)
            out_ref[:, pl.ds(pl.multiple_of(d * n, 128), n)] = value

        for t in (0, 1):
            for i in range(3):
                put(t, i, ins[5 * t + i][:, cols])

            @pl.when(upper)
            def _():
                put(t, 3, ins[5 * t + 3][:, cols])

            @pl.when(jnp.logical_not(upper))
            def _():
                put(t, 3, ins[5 * t + 4][:, cols])


def assemble(me, mine, other, widths):
    rows, total = mine[0].shape
    block = next(b for b in (512, 256, 176, 128, 96, 64, 32, 16) if rows // 2 % b == 0)
    last = rows // 2 // block - 1
    every = pl.BlockSpec((block, total), lambda i, me_ref: (i, 0))
    upper = pl.BlockSpec((block, total), lambda i, me_ref: (jnp.minimum(i, last), 0))
    lower = pl.BlockSpec((block, total), lambda i, me_ref: (jnp.maximum(i - last - 1, 0), 0))
    return pl.pallas_call(
        functools.partial(assemble_kernel, widths),
        grid_spec=pltpu.PrefetchScalarGridSpec(
            num_scalar_prefetch=1,
            grid=(rows // block,),
            in_specs=[every, every, every, upper, lower] * 2,
            out_specs=[pl.BlockSpec((block, 8 * n), lambda i, me_ref: (i, 0)) for n in widths],
        ),
        out_shape=[jax.ShapeDtypeStruct((rows, 8 * n), BF) for n in widths],
        compiler_params=params(),
        cost_estimate=SHORT,
    )(me, *mine, *other)


def after(v, *others):
    return lax.optimization_barrier((v,) + others)[0]


def all_after(vs, *others):
    return lax.optimization_barrier(tuple(vs) + others)[: len(vs)]


def send_shard(ws, *wait):
    w = after(jnp.concatenate(ws, axis=1) if len(ws) > 1 else ws[0], *wait)
    return w, swap(w, 2), swap(w, 4)


def send_diagonal(got, *wait):
    x, y = all_after(got[1:], *wait)
    half = x.shape[0] // 2
    return swap(x[:half], 4), swap(y[half:], 2)


def send_core(parts, *wait):
    parts = all_after(parts, *wait)
    return parts, tuple(swap(v, 1) for v in parts)


def wgrad_kernel(counts, me_ref, *refs):
    keep_ref, send_ref = refs[-2 - len(counts) : -len(counts)]
    scratch = refs[-len(counts) :]
    at = first = 0
    for blocks, xt_ref in zip(counts, scratch):
        x_ref = refs[at]
        keep_in = [r[0] for r in refs[at + 1 : at + 1 + blocks]]
        send_in = [r[0] for r in refs[at + 1 + blocks : at + 1 + 2 * blocks]]
        at += 1 + 2 * blocks

        @pl.when(pl.program_id(0) == 0)
        def _():
            xt_ref[...] = jnp.transpose(x_ref[...])

        rows = xt_ref.shape[0]
        res = dense(xt_ref[...], jnp.concatenate(keep_in + send_in, axis=1))
        wide = res.shape[1] // 256
        for t, ref in enumerate((keep_ref, send_ref)):
            for j in range(wide):
                col = (t * wide + j) * 128
                ref[0, first + j * rows : first + (j + 1) * rows] = res[:, col : col + 128].astype(BF)
        first += wide * rows


def wgrad(me, *products):
    in_specs, operands, counts, scratch = [], [], [], []
    height = flops = moved = 0
    for x, dy in products:
        tok, rows = x.shape
        parts, _, cols = dy.shape
        n = parts * cols // 8
        width = n if parts == 1 else 128
        per = cols // width
        blocks = n // width
        in_specs.append(pl.BlockSpec((tok, rows), lambda i, me_ref: (0, 0)))
        operands.append(x)
        for t in (0, 1):
            for j in range(blocks):

                def place(i, me_ref, t=t, j=j, blocks=blocks, per=per):
                    b = jnp.bitwise_xor(me_ref[0], 2 * i + t) * blocks + j
                    return (b // per, 0, b % per)

                in_specs.append(pl.BlockSpec((1, tok, width), place))
                operands.append(dy)
        counts.append(blocks)
        scratch.append(pltpu.VMEM((rows, tok), BF))
        height += n // 128 * rows
        flops += 2 * tok * rows * 8 * n
        moved += 2 * (tok * rows + tok * 8 * n + rows * 8 * n)
    out_spec = pl.BlockSpec((1, height, 128), lambda i, me_ref: (i, 0, 0))
    return pl.pallas_call(
        functools.partial(wgrad_kernel, tuple(counts)),
        grid_spec=pltpu.PrefetchScalarGridSpec(
            num_scalar_prefetch=1,
            grid=(4,),
            in_specs=in_specs,
            out_specs=[out_spec, out_spec],
            scratch_shapes=scratch,
        ),
        out_shape=[jax.ShapeDtypeStruct((4, height, 128), BF)] * 2,
        compiler_params=params(),
        cost_estimate=SHORT,
    )(me, *operands)


def gelu_grad_kernel(dz_ref, w_ref, slope_ref, du_ref):
    du_ref[...] = (nt(dz_ref[...], w_ref[...]) * slope_ref[...].astype(F32)).astype(BF)


def gelu_grad(dz, w, slope):
    rows, width = dz.shape
    hidden = w.shape[0]
    block = 512
    wide = pl.BlockSpec((rows, block), lambda i: (0, i))
    return pl.pallas_call(
        gelu_grad_kernel,
        grid=(hidden // block,),
        in_specs=[
            pl.BlockSpec((rows, width), lambda i: (0, 0)),
            pl.BlockSpec((block, width), lambda i: (i, 0)),
            wide,
        ],
        out_specs=wide,
        out_shape=jax.ShapeDtypeStruct((rows, hidden), BF),
        compiler_params=params(),
        cost_estimate=SHORT,
    )(dz, w, slope)


def kv_grad_kernel(dk_ref, dv_ref, wk_ref, wv_ref, x_ref, part_ref, sums_ref):
    part = nt(dk_ref[0], wk_ref[...]) + nt(dv_ref[0], wv_ref[...])
    part_ref[0] = part.astype(BF)
    _, normed, _ = layer_norm(x_ref[...].astype(F32), 1.0, 0.0)

    @pl.when(pl.program_id(0) == 0)
    def _():
        sums_ref[...] = jnp.zeros_like(sums_ref)

    sums_ref[0:1] += jnp.sum(part * normed, axis=0, keepdims=True)
    sums_ref[1:2] += jnp.sum(part, axis=0, keepdims=True)


def kv_grad(dqkv, w, x, n):
    _, rows, width = dqkv.shape
    block = rows // n
    return pl.pallas_call(
        kv_grad_kernel,
        grid=(n,),
        in_specs=[
            pl.BlockSpec((1, block, width), lambda i: (1, i, 0)),
            pl.BlockSpec((1, block, width), lambda i: (2, i, 0)),
            pl.BlockSpec((width, width), lambda i: (0, 1)),
            pl.BlockSpec((width, width), lambda i: (0, 2)),
            pl.BlockSpec((block, width), lambda i: (i, 0)),
        ],
        out_specs=[
            pl.BlockSpec((1, block, width), lambda i: (i, 0, 0)),
            pl.BlockSpec((8, width), lambda i: (0, 0)),
        ],
        out_shape=[jax.ShapeDtypeStruct((n, block, width), BF), jax.ShapeDtypeStruct((8, width), F32)],
        compiler_params=params(),
        cost_estimate=SHORT,
    )(dqkv, dqkv, w, w, x)


def add(*terms):
    total = terms[0].astype(F32)
    for t in terms[1:]:
        total = total + t.astype(F32)
    return total.astype(BF)


def pick(v, i, half):
    rows = v.shape[1] // 2
    return v[i, half * rows : (half + 1) * rows]


def sum_near(keep, got, *wait):
    keep, got = all_after((keep, got), *wait)
    term = lambda i, h: add(pick(keep, i, h), pick(got, i, h))
    xa, yb = jnp.stack([term(1, 0), term(3, 0)]), jnp.stack([term(2, 1), term(3, 1)])
    return (swap(xa, 2), swap(yb, 4)), (xa, yb)


def sum_far(keep, got, near, *wait):
    xa, yb, keep, got = all_after(tuple(near) + (keep, got), *wait)
    ya = add(pick(keep, 2, 0), pick(got, 2, 0), xa[1])
    xb = add(pick(keep, 1, 1), pick(got, 1, 1), yb[1])
    return (swap(ya, 4), swap(xb, 2)), (ya, xb)


def sum_own(keep, got, near, far):
    halves = [add(pick(keep, 0, h), pick(got, 0, h), near[h][0], far[h]) for h in (0, 1)]
    return jnp.concatenate(halves, axis=0)


def shift(v, n, step, pairs):
    return lax.ppermute(v, "seq", [(a, a + step) for a in pairs if 0 <= a + step < n])


def gather_rows(v, z, n):
    right, left = [v], [v]
    for s in range(n - 1):
        right.append(shift(right[-1], n, 1, range(s, n)))
        left.append(shift(left[-1], n, -1, range(0, n - s)))
    out = []
    for k in range(n):
        val = v
        for d in range(1, n):
            if k + d < n:
                val = jnp.where(z == k + d, right[d], val)
            if k - d >= 0:
                val = jnp.where(z == k - d, left[d], val)
        out.append(val)
    return jnp.concatenate(out, axis=0)


def scatter_rows(v, z, n, wait=()):
    part = lambda t: lax.dynamic_index_in_dim(v, jnp.clip(t, 0, n - 1), 0, keepdims=False).astype(F32)
    r = l = None
    for p in range(1, n):
        rv, lv = part(n - p + z), part(p - n + z)
        if r is not None:
            r, l = all_after((r, l), *wait)
            rv, lv = rv + r.astype(F32), lv + l.astype(F32)
        r = shift(rv.astype(BF), n, 1, range(0, p))
        l = shift(lv.astype(BF), n, -1, range(n - p, n))
    return part(z) + r.astype(F32) + l.astype(F32)


def twin(v, bit):
    return lax.ppermute(v, "seq", [(i, i ^ bit) for i in range(4)])


def take_part(v, at, count):
    rows = v.shape[0] // count
    return lax.dynamic_slice_in_dim(v, at * rows, rows)


def in_order(mine, other, bit):
    return jnp.where(bit == 0, jnp.concatenate([mine, other]), jnp.concatenate([other, mine]))


def local(
    tokens, enc_states, order, lengths, enc_lengths, attn_in, attn_out, cross_q, cross_kv,
    cross_out, ffn_in, ffn_out, proj_bias, gains, ln_bias, ffn_bias, cotangent,
):
    n_dp, n_seq = lax.axis_size("dp"), lax.axis_size("seq")
    z = lax.axis_index("seq")
    dp = lax.axis_index("dp")
    me = dp.astype(jnp.int32).reshape(1)
    fast = n_dp == 8 and n_seq == 4 and attn_out.shape[1] % 128 == 0
    x = tokens[0]
    rows, width = x.shape
    enc_rows = enc_states.shape[1] * n_seq
    group_rows = rows * n_seq
    shard = attn_out.shape[1]

    small = jnp.concatenate([proj_bias, gains, ln_bias, ffn_bias.reshape(-1, shard)], axis=0)
    count = small.shape[0]
    if fast:
        pad_rows = 32
        w = attn_in.shape[1]
        flat = jnp.concatenate([small.reshape(-1), jnp.zeros((pad_rows * w - small.size,), BF)])
        a_near = send_shard([jnp.concatenate([attn_in, flat.reshape(pad_rows, w)], axis=0)])
        x_full = lax.all_gather(x, "seq", axis=0, tiled=True)
        a_far = send_diagonal(a_near)
        b_near = send_shard([cross_kv, attn_out, cross_q, cross_out], *a_near[1:])
        states = lax.all_gather(after(enc_states[0], x_full), "seq", axis=0, tiled=True)
        (first,) = assemble(me, *send_core(a_near + a_far), (w,))
        b_far = send_diagonal(b_near, first)
        w_in = first[:width]
        small_all = first[width:].reshape(pad_rows, n_dp, w).transpose(1, 0, 2).reshape(n_dp, -1)
        small_all = small_all[:, : small.size].reshape(n_dp, count, shard)
    else:
        x_full = gather_rows(x, z, n_seq)
        states = gather_rows(enc_states[0], z, n_seq)
        gather = lambda v: lax.all_gather(v, "dp", axis=1, tiled=True)
        w_in, w_ckv, w_out, w_cq = gather(attn_in), gather(cross_kv), gather(attn_out), gather(cross_q)
        w_cout, w_up, w_down = gather(cross_out), gather(ffn_in), gather(ffn_out)
        small_all = lax.all_gather(small, "dp", axis=0, tiled=False)
    n_bias, n_norm = proj_bias.shape[0], gains.shape[0]
    rows_all = small_all[:, : n_bias + 2 * n_norm].transpose(1, 0, 2).reshape(-1, width).astype(F32)
    bias = rows_all[:n_bias]
    gain = rows_all[n_bias : n_bias + n_norm]
    shift_v = rows_all[n_bias + n_norm :]
    up_bias = small_all[:, n_bias + 2 * n_norm :].reshape(-1).astype(F32)

    place = order[0]
    seg = segment_ids(place, lengths[0])
    seg_enc = segment_ids(jnp.arange(enc_rows, dtype=jnp.int32), enc_lengths[0])
    my_place = lax.dynamic_slice_in_dim(place, z * rows, rows)
    my_seg = lax.dynamic_slice_in_dim(seg, z * rows, rows)
    self_keep = (seg[:, None] == my_seg[None, :]) & (place[:, None] <= my_place[None, :])
    self_bias = jnp.where(self_keep, 0.0, NEG).astype(F32)
    cross_bias = jnp.where(seg_enc[:, None] == my_seg[None, :], 0.0, NEG).astype(F32)
    zero_row = jnp.zeros((width,), F32)

    xf = x_full.astype(F32)
    v1, _, _ = layer_norm(xf, gain[0], shift_v[0])
    a1_full = v1.astype(BF)
    x32 = x.astype(F32)
    v1_own, xh1, rs1 = layer_norm(x32, gain[0], shift_v[0])
    a1 = v1_own.astype(BF)
    kv = (dense(a1_full, w_in[:, width:]) + jnp.concatenate([zero_row, bias[1]])).astype(BF)
    q = (dense(a1, w_in[:, :width]) + bias[0]).astype(BF)
    if fast:
        b_parts, b_other = send_core(b_near + b_far, kv)
        c_near = send_shard([ffn_in], kv)
        q, kv, *_ = all_after((q, kv), *b_far, states)
    half = HEADS // 4
    attn_a, lse_a = attn_fwd(q, kv, self_bias, 0, half)
    if fast:
        q, attn_a, lse_a = all_after((q, attn_a, lse_a), *c_near[1:], *b_other)
        c_far = send_diagonal(c_near, attn_a)
        d_near = send_shard([ffn_out], attn_a)
    attn_b, lse_b = attn_fwd(q, kv, self_bias, half, half)
    attn = jnp.concatenate([attn_a, attn_b], axis=1)
    lse = jnp.concatenate([lse_a, lse_b], axis=0)
    if fast:
        attn, lse = all_after((attn, lse), *c_far)
        widths = tuple(v.shape[1] for v in (cross_kv, attn_out, cross_q, cross_out))
        c_parts, c_other = send_core(c_near + c_far, attn)
        b_parts = all_after(b_parts, attn)
        w_ckv, w_out, w_cq, w_cout = assemble(me, b_parts, b_other, widths)
    h1 = x32 + dense(attn, w_out) + bias[2]
    v2, xh2, rs2 = layer_norm(h1, gain[1], shift_v[1])
    a2 = v2.astype(BF)
    cq = (dense(a2, w_cq) + bias[3]).astype(BF)
    ekv = (dense(states, w_ckv) + jnp.concatenate([zero_row, bias[4]])).astype(BF)
    if fast:
        cq = after(cq, ekv, *c_other, *d_near[1:])
        d_far = send_diagonal(d_near, cq)
    cattn, clse = attn_fwd(cq, ekv, cross_bias)
    if fast:
        cattn = after(cattn, *d_far)
        d_parts, d_other = send_core(d_near + d_far, cattn)
        c_parts = all_after(c_parts, cattn)
        (w_up,) = assemble(me, c_parts, c_other, (ffn_in.shape[1],))
    h2 = h1 + dense(cattn, w_cout) + bias[5]
    v3, xh3, rs3 = layer_norm(h2, gain[2], shift_v[2])
    a3 = v3.astype(BF)
    up = dense(a3, w_up) + up_bias
    gelu, slope = gelu_both(up)
    gelu_h, slope = gelu.astype(BF), slope.astype(BF)
    if fast:
        d_parts = all_after(d_parts, gelu_h)
        (w_down,) = assemble(me, d_parts, d_other, (shard,))
    h3 = h2 + dense(gelu_h, w_down) + bias[6]
    out, xh4, rs4 = layer_norm(h3, gain[3], shift_v[3])

    total = lambda v: jnp.sum(v, axis=0, dtype=F32)
    by_columns = lambda a, b: lax.psum_scatter(dense_left(a, b), "dp", scatter_dimension=1, tiled=True).astype(BF)
    ct = cotangent[0].astype(F32)
    g3, s3 = norm_sums(xh4, ct)
    dh3 = norm_input_grad(xh4, rs4, gain[3], ct)
    dz = dh3.astype(BF)
    z_row = z.astype(jnp.int32).reshape(1)

    def by_chain(v, turn=0):
        listed = [(turn + i) % n_seq for i in range(n_seq)]
        return lax.psum(v, "seq", axis_index_groups=[listed])

    if fast:
        dz, gelu_h = all_after((dz, gelu_h))
        d_keep, d_send = wgrad(me, (gelu_h, dz[None]))
        dz, d_keep, d_send = all_after((dz, d_keep, d_send))
        d_got = swap(d_send, 1)
    du = gelu_grad(dz, w_down, slope)
    if fast:
        du, d_got = all_after((du, d_got))
        d_n, sent = sum_near(d_keep, d_got, du)
        du, *_ = all_after((du,), *sent)
        c_keep, c_send = wgrad(me, (a3, du[None]))
        du, c_send = all_after((du, c_send))
        c_got = swap(c_send, 1)
    c3 = dense_t(du, w_up)
    g2, s2 = norm_sums(xh3, c3)
    dh2 = dh3 + norm_input_grad(xh3, rs3, gain[2], c3)
    dc = dh2.astype(BF)
    if fast:
        dc, c_got = all_after((dc, c_got))
    dcattn = dense_t(dc, w_cout).astype(BF)
    if fast:
        dcattn, *_ = all_after((dcattn,), *d_n)
        d_f, sent = sum_far(d_keep, d_got, d_n, dcattn)
        dcattn = after(dcattn, *sent)
    dcq, dekv = attn_bwd(z_row, cq, ekv, cross_bias, clse, cattn, dcattn, False)
    if fast:
        dcq, dekv = all_after((dcq, dekv), *d_f)
        c_n, sent = sum_near(c_keep, c_got, dcq)
        d_sum = sum_own(d_keep, d_got, d_n, d_f)
        low, high = z % 2, z // 2
        d_other = take_part(d_sum, 1 - low, 2)
        dcq, dekv, *_ = all_after((dcq, dekv), d_other, *sent)
        d_got_a = twin(d_other, 1)
        e_keep, e_send = wgrad(me, (cattn, dc[None]), (a2, dcq[None]), (states, dekv))
        dcq, dekv, e_keep, e_send, d_got_a = all_after((dcq, dekv, e_keep, e_send, d_got_a), *c_n)
        d_half = add(take_part(d_sum, low, 2), d_got_a)
        d_other = take_part(d_half, 1 - high, 2)
        dcq = after(dcq, d_other)
        d_got_b = twin(d_other, 2)
        e_got = swap(e_send, 1)
        c_f, sent = sum_far(c_keep, c_got, c_n, dcq)
        dcq = after(dcq, *sent)
    enc_part = dense_t(dekv[0], w_ckv[:, :width]) + dense_t(dekv[1], w_ckv[:, width:])
    if fast:
        enc_part = enc_part.astype(BF)
        dcq = after(dcq, enc_part)
    c2 = dense_t(dcq, w_cq)
    g1, s1 = norm_sums(xh2, c2)
    dh1 = dh2 + norm_input_grad(xh2, rs2, gain[1], c2)
    da = dh1.astype(BF)
    if fast:
        da, e_got = all_after((da, e_got))
    dattn = dense_t(da, w_out).astype(BF)
    if fast:
        dattn, d_got_b = all_after((dattn, d_got_b), *c_f)
        d_quarter = add(take_part(d_half, high, 2), d_got_b)
        e_n, sent = sum_near(e_keep, e_got, dattn)
        c_sum = sum_own(c_keep, c_got, c_n, c_f)
        c_all = by_chain(c_sum, 1)
        dattn = after(dattn, c_sum, d_quarter, *sent)
        d_got_c = twin(d_quarter, 2)
    dq, dqkv = attn_bwd(z_row, q, kv, self_bias, lse, attn, dattn, True, 0, 5)
    if fast:
        enc_sum = lax.psum_scatter(enc_part, "seq", scatter_dimension=0, tiled=True)
        dattn, dq, dqkv, d_got_c = all_after((dattn, dq, dqkv, d_got_c), *e_n, enc_sum)
        d_half = in_order(d_quarter, d_got_c, high)
        e_f, sent = sum_far(e_keep, e_got, e_n, dattn)
        dattn = after(dattn, d_half, *sent)
        d_got_d = twin(d_half, 1)
    dq, dqkv = attn_bwd(z_row, q, kv, self_bias, lse, attn, dattn, True, 5, 3, (dq, dqkv))
    if fast:
        dq, dqkv, d_got_d = all_after((dq, dqkv, d_got_d), *e_f)
        d_all = in_order(d_half, d_got_d, low)
        e_sum = sum_own(e_keep, e_got, e_n, e_f)
        e_all = by_chain(e_sum, 2)
        dqkv = after(dqkv, e_sum)
        i_keep, i_send = wgrad(me, (attn, da[None]), (a1_full, dqkv))
        dq, dqkv, i_keep, i_send = all_after((dq, dqkv, i_keep, i_send), c_all)
        i_got = swap(i_send, 1)
    if fast:
        c1_part, c1_sums = kv_grad(dqkv, first, x_full, n_seq)
        c1_part, c1_sums, i_got = all_after((c1_part, c1_sums, i_got))
        i_n, sent = sum_near(i_keep, i_got)
        c1_part = after(c1_part, *sent)
        c1_q = dense_t(dq, w_in[:, :width])
        g0, s0 = (a + b for a, b in zip((c1_sums[0], c1_sums[1]), norm_sums(xh1, c1_q)))
        c1_q = after(c1_q, g0, s0)
    else:
        c1_part = dense_t(dqkv[1], w_in[:, width : 2 * width]) + dense_t(dqkv[2], w_in[:, 2 * width :])
        c1_q = dense_t(dq, w_in[:, :width])
        _, xh1_full, _ = layer_norm(xf, gain[0], shift_v[0])
        g0, s0 = (a + b for a, b in zip(norm_sums(xh1_full, c1_part), norm_sums(xh1, c1_q)))

    bias_rows = [total(dq), total(dqkv[2]), total(dh1), total(dcq), total(dekv[1]), total(dh2), total(dh3)]
    small_rows = jnp.stack(bias_rows + [g0, g1, g2, g3, s0, s1, s2, s3])
    small_rows = small_rows.reshape(-1, n_dp, shard).transpose(1, 0, 2)
    small_rows = jnp.concatenate([small_rows, total(du).reshape(n_dp, -1, shard)], axis=1)
    dh1, c1_q = all_after((dh1, c1_q), small_rows)
    if fast:
        c1_sum = scatter_rows(c1_part, z, n_seq)
        i_f, _ = sum_far(i_keep, i_got, i_n)
        i_sum = after(sum_own(i_keep, i_got, i_n, i_f), e_all)
        i_all = by_chain(i_sum, 3)
        e_all, c_all, d_all = all_after((e_all, c_all, d_all), i_sum)
        enc_grad = enc_sum.astype(F32)
        c1 = c1_sum + c1_q
        flat_out = lambda v, r: jnp.concatenate(jnp.split(v, v.shape[0] // r, axis=0), axis=1).astype(F32)
        r_up, r_down = flat_out(c_all, width), d_all.astype(F32)
        r_in, r_out = flat_out(i_all[width:], width), i_all[:width].astype(F32)
        r_cout, r_cq, r_ckv = (flat_out(v, width) for v in jnp.split(e_all, [width, 2 * width], axis=0))
    else:
        c1 = lax.psum_scatter(c1_part, "seq", scatter_dimension=0, tiled=True) + c1_q
        enc_grad = lax.psum_scatter(enc_part, "seq", scatter_dimension=0, tiled=True)
        flat = lambda v: jnp.concatenate(list(v), axis=1)
        pairs = [(a1_full, flat(dqkv)), (attn, da), (a2, dcq), (states, flat(dekv)), (cattn, dc), (a3, du), (gelu_h, dz)]
        grads = [by_chain(by_columns(a, b)).astype(F32) for a, b in pairs]
        r_in, r_out, r_cq, r_ckv, r_cout, r_up, r_down = grads
    if fast:
        small_rows = after(small_rows, i_sum)
        for bit in (1, 2, 4):
            small_rows = small_rows + swap(small_rows, bit)
        for bit in (1, 2):
            small_rows = small_rows + lax.ppermute(small_rows, "seq", [(i, i ^ bit) for i in range(n_seq)])
    else:
        small_rows = lax.psum(small_rows, ("dp", "seq"))
    tokens_grad = dh1 + norm_input_grad(xh1, rs1, gain[0], c1)
    small_own = lax.dynamic_index_in_dim(small_rows, dp, 0, keepdims=False)
    return (
        out.astype(BF)[None],
        tokens_grad[None],
        enc_grad[None],
        r_in,
        r_out,
        r_cq,
        r_ckv,
        r_cout,
        r_up,
        r_down,
        small_own[:n_bias],
        small_own[n_bias : n_bias + n_norm],
        small_own[n_bias + n_norm : n_bias + 2 * n_norm],
        small_own[n_bias + 2 * n_norm :].reshape(1, -1),
    )


def solution(mesh):
    rows, cols, per_dp = P("dp", "seq", None), P(None, "dp"), P("dp", None)
    in_specs = (rows, rows, per_dp, per_dp, per_dp) + (cols,) * 11 + (rows,)
    out_specs = (rows,) * 3 + (cols,) * 11
    return jax.shard_map(local, mesh=mesh, in_specs=in_specs, out_specs=out_specs, check_vma=False)
```

```python
import functools

import jax
import jax.numpy as jnp
from jax import lax
from jax.experimental import pallas as pl
from jax.experimental.pallas import tpu as pltpu
from jax.sharding import PartitionSpec as P

HEADS = 16
EPSILON = 1e-05
BF = jnp.bfloat16
F32 = jnp.float32
NEG = -1e30
VMEM_LIMIT = 56 * 1024 * 1024
SHORT = pl.CostEstimate(flops=0, bytes_accessed=0, transcendentals=0)


def params(**kw):
    return pltpu.CompilerParams(vmem_limit_bytes=VMEM_LIMIT, **kw)


def layer_norm(v, gain, shift):
    center = v - jnp.mean(v, axis=-1, keepdims=True)
    inv = lax.rsqrt(jnp.mean(center * center, axis=-1, keepdims=True) + EPSILON)
    normed = center * inv
    return normed * gain + shift, normed, inv


def norm_input_grad(normed, inv, gain, c):
    e = c * gain
    return inv * (
        e
        - jnp.mean(e, axis=-1, keepdims=True)
        - normed * jnp.mean(e * normed, axis=-1, keepdims=True)
    )


def norm_sums(normed, c):
    return jnp.sum(c * normed, axis=0), jnp.sum(c, axis=0)


def dense(a, b):
    return jnp.dot(a, b, preferred_element_type=F32)


def dense_t(a, b):
    return lax.dot_general(a, b, (((1,), (1,)), ((), ())), preferred_element_type=F32)


def dense_left(a, b):
    return lax.dot_general(a, b, (((0,), (0,)), ((), ())), preferred_element_type=F32)


def gelu_both(u):
    c = 0.7978845608028654
    sq = u * u
    t = jnp.tanh(c * u * (1.0 + 0.044715 * sq))
    half = 0.5 * (1.0 + t)
    return u * half, half + 0.5 * c * u * (1.0 - t * t) * (1.0 + 0.134145 * sq)


def segment_ids(positions, lengths):
    ends = jnp.cumsum(lengths)
    return jnp.sum((positions[:, None] >= ends[None, :]).astype(jnp.int32), axis=1)


def split_heads(block, scale):
    head = block.shape[1] // 2
    lane = lax.broadcasted_iota(jnp.int32, block.shape, 1)
    zero = jnp.zeros_like(block)
    both = jnp.concatenate(
        [jnp.where(lane < head, block, zero), jnp.where(lane >= head, block, zero)], axis=0
    )
    return both if scale is None else both * jnp.asarray(scale, both.dtype)


def join_heads(acc):
    head, rows = acc.shape[0] // 2, acc.shape[1] // 2
    return jnp.concatenate([acc[:head, :rows], acc[head:, rows:]], axis=0)


def nt(a, b):
    return lax.dot_general(a, b, (((1,), (1,)), ((), ())), preferred_element_type=F32)


def tn(a, b):
    return lax.dot_general(a, b, (((0,), (0,)), ((), ())), preferred_element_type=F32)


def attn_fwd_kernel(scale, chunk, q_ref, k_ref, v_ref, bias_ref, o_ref, lse_ref):
    both = split_heads(q_ref[...], scale)
    top = jnp.full(lse_ref.shape[1:], NEG, F32)
    total = jnp.zeros_like(top)
    acc = None
    for c in range(k_ref.shape[0] // chunk):
        rows = slice(c * chunk, (c + 1) * chunk)
        b = bias_ref[rows, :]
        s = nt(k_ref[rows, :], both) + jnp.concatenate([b, b], axis=1)
        new = jnp.maximum(top, jnp.max(s, axis=0, keepdims=True))
        p = jnp.exp(s - new)
        part = tn(v_ref[rows, :], p.astype(BF))
        if acc is None:
            total, acc = jnp.sum(p, axis=0, keepdims=True), part
        else:
            alpha = jnp.exp(top - new)
            total = total * alpha + jnp.sum(p, axis=0, keepdims=True)
            acc = acc * alpha + part
        top = new
    o_ref[...] = jnp.transpose(join_heads(acc / total)).astype(BF)
    lse_ref[0] = top + jnp.log(total)


def attn_fwd(q, kv, bias, first=0, count=HEADS // 2):
    nq, width = q.shape
    nk = kv.shape[0]
    head = width // HEADS
    pairs, pw = HEADS // 2, 2 * head
    chunk = 512
    return pl.pallas_call(
        functools.partial(attn_fwd_kernel, head**-0.5, chunk),
        grid=(count,),
        in_specs=[
            pl.BlockSpec((nq, pw), lambda i: (0, first + i)),
            pl.BlockSpec((nk, pw), lambda i: (0, first + i)),
            pl.BlockSpec((nk, pw), lambda i: (0, pairs + first + i)),
            pl.BlockSpec((nk, nq), lambda i: (0, 0)),
        ],
        out_specs=[
            pl.BlockSpec((nq, pw), lambda i: (0, i)),
            pl.BlockSpec((1, 1, 2 * nq), lambda i: (i, 0, 0)),
        ],
        out_shape=[
            jax.ShapeDtypeStruct((nq, count * pw), BF),
            jax.ShapeDtypeStruct((count, 1, 2 * nq), F32),
        ],
        compiler_params=params(),
        cost_estimate=SHORT,
    )(q, kv, kv, bias)


def attn_bwd_kernel(scale, chunk, padded, z_ref, q_ref, k_ref, v_ref, do_ref, out_ref, bias_ref, lse_ref, *refs):
    dq_ref, dkv_ref = refs[-2:]
    both = split_heads(q_ref[...], scale)
    dboth = split_heads(do_ref[...], None)
    lse = lse_ref[0]
    prod = do_ref[...].astype(F32) * out_ref[...].astype(F32)
    head = prod.shape[1] // 2
    lane = lax.broadcasted_iota(jnp.int32, (8, 2 * head), 1)
    row = lax.broadcasted_iota(jnp.int32, (8, 2 * head), 0)
    pick_head = jnp.where(lane // head == row, 1.0, 0.0)
    delta = lax.dot_general(
        pick_head, prod, (((1,), (1,)), ((), ())), precision=lax.Precision.HIGHEST, preferred_element_type=F32
    )
    delta = jnp.concatenate([delta[0:1], delta[1:2]], axis=1)
    acc = 0.0
    for c in range(k_ref.shape[0] // chunk):
        rows = slice(c * chunk, (c + 1) * chunk)
        b = bias_ref[rows, :]
        k = k_ref[rows, :]
        p = jnp.exp(nt(k, both) + jnp.concatenate([b, b], axis=1) - lse)
        ds = (p * (nt(v_ref[rows, :], dboth) - delta)).astype(BF)
        dkv_ref[padded, rows, :] = dense(ds, both).astype(BF)
        dkv_ref[padded + 1, rows, :] = dense(p.astype(BF), dboth).astype(BF)
        acc = acc + tn(k, ds)
    dq = jnp.transpose(join_heads(acc) * scale).astype(BF)
    dq_ref[...] = dq
    if padded:
        n = dq.shape[0]
        dkv_ref[0] = jnp.zeros(dkv_ref.shape[1:], BF)
        dkv_ref[0, pl.ds(pl.multiple_of(z_ref[0] * n, n), n), :] = dq


def attn_bwd(z, q, kv, bias, lse, out, dout, padded, first=0, count=HEADS // 2, into=()):
    nq, width = q.shape
    nk = kv.shape[0]
    head = width // HEADS
    pairs, pw = HEADS // 2, 2 * head
    chunk = 512
    row_spec = pl.BlockSpec((nq, pw), lambda i, z_ref: (0, first + i))
    key_spec = pl.BlockSpec((nk, pw), lambda i, z_ref: (0, first + i))
    vec_spec = pl.BlockSpec((1, 1, 2 * nq), lambda i, z_ref: (first + i, 0, 0))
    depth = 3 if padded else 2
    return pl.pallas_call(
        functools.partial(attn_bwd_kernel, head**-0.5, chunk, depth - 2),
        grid_spec=pltpu.PrefetchScalarGridSpec(
            num_scalar_prefetch=1,
            grid=(count,),
            in_specs=[
                row_spec,
                key_spec,
                pl.BlockSpec((nk, pw), lambda i, z_ref: (0, pairs + first + i)),
                row_spec,
                row_spec,
                pl.BlockSpec((nk, nq), lambda i, z_ref: (0, 0)),
                vec_spec,
            ]
            + [pl.BlockSpec(memory_space=pl.ANY)] * len(into),
            out_specs=[row_spec, pl.BlockSpec((depth, nk, pw), lambda i, z_ref: (0, 0, first + i))],
        ),
        out_shape=[
            jax.ShapeDtypeStruct((nq, width), BF),
            jax.ShapeDtypeStruct((depth, nk, width), BF),
        ],
        input_output_aliases={8: 0, 9: 1} if into else {},
        compiler_params=params(),
        cost_estimate=SHORT,
    )(z, q, kv, kv, dout, out, bias, lse, *into)


def swap(v, bit):
    return lax.ppermute(v, "dp", [(i, i ^ bit) for i in range(8)])


def assemble_kernel(widths, me_ref, *refs):
    ins, out_refs = refs[:10], refs[10:]
    upper = pl.program_id(0) < pl.num_programs(0) // 2
    start = 0
    for n, out_ref in zip(widths, out_refs):
        cols = slice(start, start + n)
        start += n

        def put(t, i, value):
            d = jnp.bitwise_xor(me_ref[0], 2 * i + t)
            out_ref[:, pl.ds(pl.multiple_of(d * n, 128), n)] = value

        for t in (0, 1):
            for i in range(3):
                put(t, i, ins[5 * t + i][:, cols])

            @pl.when(upper)
            def _():
                put(t, 3, ins[5 * t + 3][:, cols])

            @pl.when(jnp.logical_not(upper))
            def _():
                put(t, 3, ins[5 * t + 4][:, cols])


def assemble(me, mine, other, widths):
    rows, total = mine[0].shape
    block = next(b for b in (512, 256, 176, 128, 96, 64, 32, 16) if rows // 2 % b == 0)
    last = rows // 2 // block - 1
    every = pl.BlockSpec((block, total), lambda i, me_ref: (i, 0))
    upper = pl.BlockSpec((block, total), lambda i, me_ref: (jnp.minimum(i, last), 0))
    lower = pl.BlockSpec((block, total), lambda i, me_ref: (jnp.maximum(i - last - 1, 0), 0))
    return pl.pallas_call(
        functools.partial(assemble_kernel, widths),
        grid_spec=pltpu.PrefetchScalarGridSpec(
            num_scalar_prefetch=1,
            grid=(rows // block,),
            in_specs=[every, every, every, upper, lower] * 2,
            out_specs=[pl.BlockSpec((block, 8 * n), lambda i, me_ref: (i, 0)) for n in widths],
        ),
        out_shape=[jax.ShapeDtypeStruct((rows, 8 * n), BF) for n in widths],
        compiler_params=params(),
        cost_estimate=SHORT,
    )(me, *mine, *other)


def project_kernel(z_ref, x_ref, w_ref, gain_ref, shift_ref, bias_ref, a_ref, q_ref, kv_ref):
    width = x_ref.shape[1]
    a = layer_norm(x_ref[...].astype(F32), gain_ref[...], shift_ref[...])[0].astype(BF)
    a_ref[...] = a
    kv_ref[...] = (dense(a, w_ref[:, width:]) + bias_ref[:, width:]).astype(BF)

    @pl.when(pl.program_id(0) == z_ref[0])
    def _():
        q_ref[...] = (dense(a, w_ref[:, :width]) + bias_ref[:, :width]).astype(BF)


def project(z, x, w, gain, shift_row, bias, n):
    total, width = x.shape
    rows = total // n
    whole = lambda v: pl.BlockSpec(v.shape, lambda i, z_ref: (0, 0))
    block = lambda cols: pl.BlockSpec((rows, cols), lambda i, z_ref: (i, 0))
    return pl.pallas_call(
        project_kernel,
        grid_spec=pltpu.PrefetchScalarGridSpec(
            num_scalar_prefetch=1,
            grid=(n,),
            in_specs=[
                block(width),
                pl.BlockSpec((width, 3 * width), lambda i, z_ref: (0, 0)),
                whole(gain),
                whole(shift_row),
                whole(bias),
            ],
            out_specs=[block(width), pl.BlockSpec((rows, width), lambda i, z_ref: (0, 0)), block(2 * width)],
        ),
        out_shape=[
            jax.ShapeDtypeStruct((total, width), BF),
            jax.ShapeDtypeStruct((rows, width), BF),
            jax.ShapeDtypeStruct((total, 2 * width), BF),
        ],
        compiler_params=params(),
        cost_estimate=SHORT,
    )(z, x, w, gain, shift_row, bias)


def assemble_dot_kernel(gelu, me_ref, *refs):
    parts, (x_ref, bias_ref) = refs[:10], refs[10:12]
    w_ref, *outs = refs[12:] if gelu else refs[13:]
    rows, n = parts[0].shape
    step = pl.program_id(0)
    for t in (0, 1):
        cols = pl.ds(pl.multiple_of(jnp.bitwise_xor(me_ref[0] % 2, t) * n, 128), n)
        for k in range(3):

            @pl.when(step == k)
            def _():
                w_ref[:, cols] = parts[5 * t + k][...]

        @pl.when(step == 3)
        def _():
            w_ref[: rows // 2, cols] = parts[5 * t + 3][...]
            w_ref[rows // 2 :, cols] = parts[5 * t + 4][...]

    value = dense(x_ref[...], w_ref[...]) + bias_ref[...]
    if gelu:
        value, slope = gelu_both(value)
        outs[0][...] = value.astype(BF)
        outs[1][...] = slope.astype(BF)
    else:
        outs[0][...] = refs[12][...] + value


def assemble_dot(me, mine, other, x, bias, onto=None):
    rows, n = mine[0].shape
    tok = x.shape[0]
    whole = lambda v: pl.BlockSpec(v.shape, lambda i, me_ref: (0, 0))
    pair = lambda r: pl.BlockSpec((r, 2 * n), lambda i, me_ref: (0, jnp.bitwise_xor(me_ref[0] // 2, i)))
    gelu = onto is None
    outs = [BF, BF] if gelu else [F32]
    return pl.pallas_call(
        functools.partial(assemble_dot_kernel, gelu),
        grid_spec=pltpu.PrefetchScalarGridSpec(
            num_scalar_prefetch=1,
            grid=(4,),
            in_specs=[whole(v) for v in mine + other] + [whole(x), pair(1)] + ([] if gelu else [pair(tok)]),
            out_specs=[pair(rows)] + [pair(tok)] * len(outs),
        ),
        out_shape=[jax.ShapeDtypeStruct((rows, 8 * n), BF)] + [jax.ShapeDtypeStruct((tok, 8 * n), t) for t in outs],
        compiler_params=params(),
        cost_estimate=SHORT,
    )(me, *mine, *other, x, bias, *([] if gelu else [onto]))


def after(v, *others):
    return lax.optimization_barrier((v,) + others)[0]


def all_after(vs, *others):
    return lax.optimization_barrier(tuple(vs) + others)[: len(vs)]


def send_shard(ws, *wait):
    w = after(jnp.concatenate(ws, axis=1) if len(ws) > 1 else ws[0], *wait)
    return w, swap(w, 2), swap(w, 4)


def send_diagonal(got, *wait):
    x, y = all_after(got[1:], *wait)
    half = x.shape[0] // 2
    return swap(x[:half], 4), swap(y[half:], 2)


def send_core(parts, *wait):
    parts = all_after(parts, *wait)
    return parts, tuple(swap(v, 1) for v in parts)


def wgrad_kernel(counts, me_ref, *refs):
    keep_ref, send_ref = refs[-2 - len(counts) : -len(counts)]
    scratch = refs[-len(counts) :]
    at = first = 0
    for blocks, xt_ref in zip(counts, scratch):
        x_ref = refs[at]
        keep_in = [r[0] for r in refs[at + 1 : at + 1 + blocks]]
        send_in = [r[0] for r in refs[at + 1 + blocks : at + 1 + 2 * blocks]]
        at += 1 + 2 * blocks

        @pl.when(pl.program_id(0) == 0)
        def _():
            xt_ref[...] = jnp.transpose(x_ref[...])

        rows = xt_ref.shape[0]
        res = dense(xt_ref[...], jnp.concatenate(keep_in + send_in, axis=1))
        wide = res.shape[1] // 256
        for t, ref in enumerate((keep_ref, send_ref)):
            for j in range(wide):
                col = (t * wide + j) * 128
                ref[0, first + j * rows : first + (j + 1) * rows] = res[:, col : col + 128].astype(BF)
        first += wide * rows


def wgrad(me, *products):
    in_specs, operands, counts, scratch = [], [], [], []
    height = flops = moved = 0
    for x, dy in products:
        tok, rows = x.shape
        parts, _, cols = dy.shape
        n = parts * cols // 8
        width = n if parts == 1 else 128
        per = cols // width
        blocks = n // width
        in_specs.append(pl.BlockSpec((tok, rows), lambda i, me_ref: (0, 0)))
        operands.append(x)
        for t in (0, 1):
            for j in range(blocks):

                def place(i, me_ref, t=t, j=j, blocks=blocks, per=per):
                    b = jnp.bitwise_xor(me_ref[0], 2 * i + t) * blocks + j
                    return (b // per, 0, b % per)

                in_specs.append(pl.BlockSpec((1, tok, width), place))
                operands.append(dy)
        counts.append(blocks)
        scratch.append(pltpu.VMEM((rows, tok), BF))
        height += n // 128 * rows
        flops += 2 * tok * rows * 8 * n
        moved += 2 * (tok * rows + tok * 8 * n + rows * 8 * n)
    out_spec = pl.BlockSpec((1, height, 128), lambda i, me_ref: (i, 0, 0))
    return pl.pallas_call(
        functools.partial(wgrad_kernel, tuple(counts)),
        grid_spec=pltpu.PrefetchScalarGridSpec(
            num_scalar_prefetch=1,
            grid=(4,),
            in_specs=in_specs,
            out_specs=[out_spec, out_spec],
            scratch_shapes=scratch,
        ),
        out_shape=[jax.ShapeDtypeStruct((4, height, 128), BF)] * 2,
        compiler_params=params(),
        cost_estimate=SHORT,
    )(me, *operands)


def up_grad_kernel(me_ref, x_ref, du_ref, w_ref, keep_ref, send_ref, c_ref, xt_ref):
    step = pl.program_id(0)

    @pl.when(step == 0)
    def _():
        xt_ref[...] = jnp.transpose(x_ref[...])

    du = du_ref[...]
    res = dense(xt_ref[...], du)
    rows, n = xt_ref.shape[0], du.shape[1] // 2
    for odd in (0, 1):

        @pl.when(me_ref[0] % 2 == odd)
        def _():
            for t, ref in enumerate((keep_ref, send_ref)):
                for j in range(n // 128):
                    col = (t ^ odd) * n + j * 128
                    ref[0, j * rows : (j + 1) * rows] = res[:, col : col + 128].astype(BF)

    part = nt(du, w_ref[...])

    @pl.when(step == 0)
    def _():
        c_ref[...] = part

    @pl.when(step > 0)
    def _():
        c_ref[...] += part


def up_grad(me, x, du, w):
    tok, rows = x.shape
    n = du.shape[1] // 8
    stacked = n // 128 * rows
    pair = lambda r: pl.BlockSpec((r, 2 * n), lambda i, me_ref: (0, jnp.bitwise_xor(me_ref[0] // 2, i)))
    whole = pl.BlockSpec((tok, rows), lambda i, me_ref: (0, 0))
    shards = pl.BlockSpec((1, stacked, 128), lambda i, me_ref: (i, 0, 0))
    return pl.pallas_call(
        up_grad_kernel,
        grid_spec=pltpu.PrefetchScalarGridSpec(
            num_scalar_prefetch=1,
            grid=(4,),
            in_specs=[whole, pair(tok), pair(rows)],
            out_specs=[shards, shards, whole],
            scratch_shapes=[pltpu.VMEM((rows, tok), BF)],
        ),
        out_shape=[jax.ShapeDtypeStruct((4, stacked, 128), BF)] * 2 + [jax.ShapeDtypeStruct((tok, rows), F32)],
        compiler_params=params(),
        cost_estimate=SHORT,
    )(me, x, du, w)


def gelu_grad_kernel(dz_ref, w_ref, slope_ref, du_ref):
    du_ref[...] = (nt(dz_ref[...], w_ref[...]) * slope_ref[...].astype(F32)).astype(BF)


def gelu_grad(dz, w, slope):
    rows, width = dz.shape
    hidden = w.shape[0]
    block = 512
    wide = pl.BlockSpec((rows, block), lambda i: (0, i))
    return pl.pallas_call(
        gelu_grad_kernel,
        grid=(hidden // block,),
        in_specs=[
            pl.BlockSpec((rows, width), lambda i: (0, 0)),
            pl.BlockSpec((block, width), lambda i: (i, 0)),
            wide,
        ],
        out_specs=wide,
        out_shape=jax.ShapeDtypeStruct((rows, hidden), BF),
        compiler_params=params(),
        cost_estimate=SHORT,
    )(dz, w, slope)


def kv_grad_kernel(dk_ref, dv_ref, wk_ref, wv_ref, x_ref, part_ref, sums_ref):
    part = nt(dk_ref[0], wk_ref[...]) + nt(dv_ref[0], wv_ref[...])
    part_ref[0] = part.astype(BF)
    _, normed, _ = layer_norm(x_ref[...].astype(F32), 1.0, 0.0)

    @pl.when(pl.program_id(0) == 0)
    def _():
        sums_ref[...] = jnp.zeros_like(sums_ref)

    sums_ref[0:1] += jnp.sum(part * normed, axis=0, keepdims=True)
    sums_ref[1:2] += jnp.sum(part, axis=0, keepdims=True)


def kv_grad(dqkv, w, x, n):
    _, rows, width = dqkv.shape
    block = rows // n
    return pl.pallas_call(
        kv_grad_kernel,
        grid=(n,),
        in_specs=[
            pl.BlockSpec((1, block, width), lambda i: (1, i, 0)),
            pl.BlockSpec((1, block, width), lambda i: (2, i, 0)),
            pl.BlockSpec((width, width), lambda i: (0, 1)),
            pl.BlockSpec((width, width), lambda i: (0, 2)),
            pl.BlockSpec((block, width), lambda i: (i, 0)),
        ],
        out_specs=[
            pl.BlockSpec((1, block, width), lambda i: (i, 0, 0)),
            pl.BlockSpec((8, width), lambda i: (0, 0)),
        ],
        out_shape=[jax.ShapeDtypeStruct((n, block, width), BF), jax.ShapeDtypeStruct((8, width), F32)],
        compiler_params=params(),
        cost_estimate=SHORT,
    )(dqkv, dqkv, w, w, x)


def add(*terms):
    total = terms[0].astype(F32)
    for t in terms[1:]:
        total = total + t.astype(F32)
    return total.astype(BF)


def pick(v, i, half):
    rows = v.shape[1] // 2
    return v[i, half * rows : (half + 1) * rows]


def sum_near(keep, got, *wait):
    keep, got = all_after((keep, got), *wait)
    term = lambda i, h: add(pick(keep, i, h), pick(got, i, h))
    xa, yb = jnp.stack([term(1, 0), term(3, 0)]), jnp.stack([term(2, 1), term(3, 1)])
    return (swap(xa, 2), swap(yb, 4)), (xa, yb)


def sum_far(keep, got, near, *wait):
    xa, yb, keep, got = all_after(tuple(near) + (keep, got), *wait)
    ya = add(pick(keep, 2, 0), pick(got, 2, 0), xa[1])
    xb = add(pick(keep, 1, 1), pick(got, 1, 1), yb[1])
    return (swap(ya, 4), swap(xb, 2)), (ya, xb)


def sum_own(keep, got, near, far):
    halves = [add(pick(keep, 0, h), pick(got, 0, h), near[h][0], far[h]) for h in (0, 1)]
    return jnp.concatenate(halves, axis=0)


def shift(v, n, step, pairs):
    return lax.ppermute(v, "seq", [(a, a + step) for a in pairs if 0 <= a + step < n])


def gather_rows(v, z, n):
    right, left = [v], [v]
    for s in range(n - 1):
        right.append(shift(right[-1], n, 1, range(s, n)))
        left.append(shift(left[-1], n, -1, range(0, n - s)))
    out = []
    for k in range(n):
        val = v
        for d in range(1, n):
            if k + d < n:
                val = jnp.where(z == k + d, right[d], val)
            if k - d >= 0:
                val = jnp.where(z == k - d, left[d], val)
        out.append(val)
    return jnp.concatenate(out, axis=0)


def scatter_rows(v, z, n, wait=()):
    part = lambda t: lax.dynamic_index_in_dim(v, jnp.clip(t, 0, n - 1), 0, keepdims=False).astype(F32)
    r = l = None
    for p in range(1, n):
        rv, lv = part(n - p + z), part(p - n + z)
        if r is not None:
            r, l = all_after((r, l), *wait)
            rv, lv = rv + r.astype(F32), lv + l.astype(F32)
        r = shift(rv.astype(BF), n, 1, range(0, p))
        l = shift(lv.astype(BF), n, -1, range(n - p, n))
    return part(z) + r.astype(F32) + l.astype(F32)


def twin(v, bit):
    return lax.ppermute(v, "seq", [(i, i ^ bit) for i in range(4)])


def take_part(v, at, count):
    rows = v.shape[0] // count
    return lax.dynamic_slice_in_dim(v, at * rows, rows)


def in_order(mine, other, bit):
    return jnp.where(bit == 0, jnp.concatenate([mine, other]), jnp.concatenate([other, mine]))


def local(
    tokens, enc_states, order, lengths, enc_lengths, attn_in, attn_out, cross_q, cross_kv,
    cross_out, ffn_in, ffn_out, proj_bias, gains, ln_bias, ffn_bias, cotangent,
):
    n_dp, n_seq = lax.axis_size("dp"), lax.axis_size("seq")
    z = lax.axis_index("seq")
    dp = lax.axis_index("dp")
    me = dp.astype(jnp.int32).reshape(1)
    fast = n_dp == 8 and n_seq == 4 and attn_out.shape[1] % 128 == 0
    x = tokens[0]
    rows, width = x.shape
    enc_rows = enc_states.shape[1] * n_seq
    group_rows = rows * n_seq
    shard = attn_out.shape[1]

    small = jnp.concatenate([proj_bias, gains, ln_bias, ffn_bias.reshape(-1, shard)], axis=0)
    count = small.shape[0]
    if fast:
        pad_rows = 32
        w = attn_in.shape[1]
        flat = jnp.concatenate([small.reshape(-1), jnp.zeros((pad_rows * w - small.size,), BF)])
        a_near = send_shard([jnp.concatenate([attn_in, flat.reshape(pad_rows, w)], axis=0)])
        x_full = lax.all_gather(x, "seq", axis=0, tiled=True)
        a_far = send_diagonal(a_near)
        b_near = send_shard([cross_kv, attn_out, cross_q, cross_out], *a_near[1:])
        states = lax.all_gather(after(enc_states[0], x_full), "seq", axis=0, tiled=True)
        (first,) = assemble(me, *send_core(a_near + a_far), (w,))
        b_far = send_diagonal(b_near, first)
        w_in = first[:width]
        small_all = first[width:].reshape(pad_rows, n_dp, w).transpose(1, 0, 2).reshape(n_dp, -1)
        small_all = small_all[:, : small.size].reshape(n_dp, count, shard)
    else:
        x_full = gather_rows(x, z, n_seq)
        states = gather_rows(enc_states[0], z, n_seq)
        gather = lambda v: lax.all_gather(v, "dp", axis=1, tiled=True)
        w_in, w_ckv, w_out, w_cq = gather(attn_in), gather(cross_kv), gather(attn_out), gather(cross_q)
        w_cout, w_up, w_down = gather(cross_out), gather(ffn_in), gather(ffn_out)
        small_all = lax.all_gather(small, "dp", axis=0, tiled=False)
    n_bias, n_norm = proj_bias.shape[0], gains.shape[0]
    rows_all = small_all[:, : n_bias + 2 * n_norm].transpose(1, 0, 2).reshape(-1, width).astype(F32)
    bias = rows_all[:n_bias]
    gain = rows_all[n_bias : n_bias + n_norm]
    shift_v = rows_all[n_bias + n_norm :]
    up_bias = small_all[:, n_bias + 2 * n_norm :].reshape(-1).astype(F32)

    place = order[0]
    seg = segment_ids(place, lengths[0])
    seg_enc = segment_ids(jnp.arange(enc_rows, dtype=jnp.int32), enc_lengths[0])
    my_place = lax.dynamic_slice_in_dim(place, z * rows, rows)
    my_seg = lax.dynamic_slice_in_dim(seg, z * rows, rows)
    self_keep = (seg[:, None] == my_seg[None, :]) & (place[:, None] <= my_place[None, :])
    self_bias = jnp.where(self_keep, 0.0, NEG).astype(F32)
    cross_bias = jnp.where(seg_enc[:, None] == my_seg[None, :], 0.0, NEG).astype(F32)
    zero_row = jnp.zeros((width,), F32)

    x32 = x.astype(F32)
    v1_own, xh1, rs1 = layer_norm(x32, gain[0], shift_v[0])
    z_row = z.astype(jnp.int32).reshape(1)
    if fast:
        x_full, self_bias, cross_bias = all_after((x_full, self_bias, cross_bias))
        qkv_bias = jnp.concatenate([bias[0], zero_row, bias[1]])[None]
        a1_full, q, kv = project(z_row, x_full, first, gain[:1], shift_v[:1], qkv_bias, n_seq)
    else:
        xf = x_full.astype(F32)
        a1_full = layer_norm(xf, gain[0], shift_v[0])[0].astype(BF)
        kv = (dense(a1_full, w_in[:, width:]) + jnp.concatenate([zero_row, bias[1]])).astype(BF)
        q = (dense(v1_own.astype(BF), w_in[:, :width]) + bias[0]).astype(BF)
    if fast:
        b_parts, b_other = send_core(b_near + b_far, kv)
        c_near = send_shard([ffn_in], kv)
        q, kv, *_ = all_after((q, kv), *b_far)
    half = HEADS // 4
    attn_a, lse_a = attn_fwd(q, kv, self_bias, 0, half)
    if fast:
        widths = tuple(v.shape[1] for v in (cross_kv, attn_out, cross_q, cross_out))
        b_parts = all_after(b_parts, attn_a)
        w_ckv, w_out, w_cq, w_cout = assemble(me, b_parts, b_other, widths)
        q, attn_a, lse_a, w_out, states = all_after((q, attn_a, lse_a, w_out, states), *c_near[1:])
        c_far = send_diagonal(c_near, attn_a)
    attn_b, lse_b = attn_fwd(q, kv, self_bias, half, half)
    attn = jnp.concatenate([attn_a, attn_b], axis=1)
    lse = jnp.concatenate([lse_a, lse_b], axis=0)
    if fast:
        attn, lse = all_after((attn, lse), *c_far)
        d_near = send_shard([ffn_out], attn)
        c_parts, c_other = send_core(c_near + c_far, attn)
    h1 = x32 + dense(attn, w_out) + bias[2]
    v2, xh2, rs2 = layer_norm(h1, gain[1], shift_v[1])
    a2 = v2.astype(BF)
    cq = (dense(a2, w_cq) + bias[3]).astype(BF)
    ekv = (dense(states, w_ckv) + jnp.concatenate([zero_row, bias[4]])).astype(BF)
    if fast:
        cq = after(cq, ekv, *c_other)
    cattn, clse = attn_fwd(cq, ekv, cross_bias)
    if fast:
        cattn = after(cattn, *d_near[1:])
        d_far = send_diagonal(d_near, cattn)
        d_parts, d_other = send_core(d_near, cattn)
        c_parts = all_after(c_parts, cattn)
    h2 = h1 + dense(cattn, w_cout) + bias[5]
    v3, xh3, rs3 = layer_norm(h2, gain[2], shift_v[2])
    a3 = v3.astype(BF)
    if fast:
        w_up, gelu_h, slope = assemble_dot(me, c_parts, c_other, a3, up_bias[None])
        gelu_h, *d_far = all_after((gelu_h,) + d_far)
        d_rest, d_other_rest = send_core(d_far, gelu_h)
        d_parts, d_other = d_parts + d_rest, d_other + d_other_rest
        w_down, h3 = assemble_dot(me, d_parts, d_other, gelu_h, bias[6:7], h2)
    else:
        gelu, slope = gelu_both(dense(a3, w_up) + up_bias)
        gelu_h, slope = gelu.astype(BF), slope.astype(BF)
        h3 = h2 + dense(gelu_h, w_down) + bias[6]
    out, xh4, rs4 = layer_norm(h3, gain[3], shift_v[3])

    total = lambda v: jnp.sum(v, axis=0, dtype=F32)
    by_columns = lambda a, b: lax.psum_scatter(dense_left(a, b), "dp", scatter_dimension=1, tiled=True).astype(BF)
    ct = cotangent[0].astype(F32)
    g3, s3 = norm_sums(xh4, ct)
    dh3 = norm_input_grad(xh4, rs4, gain[3], ct)
    dz = dh3.astype(BF)

    def by_chain(v, turn=0):
        listed = [(turn + i) % n_seq for i in range(n_seq)]
        return lax.psum(v, "seq", axis_index_groups=[listed])

    if fast:
        dz, gelu_h = all_after((dz, gelu_h))
        d_keep, d_send = wgrad(me, (gelu_h, dz[None]))
        dz, d_keep, d_send = all_after((dz, d_keep, d_send))
        d_got = swap(d_send, 1)
    du = gelu_grad(dz, w_down, slope)
    if fast:
        du, d_got = all_after((du, d_got))
        d_n, sent = sum_near(d_keep, d_got, du)
        du, *_ = all_after((du,), *sent)
        c_keep, c_send, c3 = up_grad(me, a3, du, w_up)
        c3, c_send, *d_n = all_after((c3, c_send) + tuple(d_n))
        c_got = swap(c_send, 1)
    else:
        c3 = dense_t(du, w_up)
    g2, s2 = norm_sums(xh3, c3)
    dh2 = dh3 + norm_input_grad(xh3, rs3, gain[2], c3)
    dc = dh2.astype(BF)
    if fast:
        dc, c_got = all_after((dc, c_got))
    dcattn = dense_t(dc, w_cout).astype(BF)
    if fast:
        dcattn, *_ = all_after((dcattn,), *d_n)
        d_f, sent = sum_far(d_keep, d_got, d_n, dcattn)
        dcattn = after(dcattn, *sent)
    dcq, dekv = attn_bwd(z_row, cq, ekv, cross_bias, clse, cattn, dcattn, False)
    if fast:
        dcq, dekv = all_after((dcq, dekv), *d_f)
        c_n, sent = sum_near(c_keep, c_got, dcq)
        d_sum = sum_own(d_keep, d_got, d_n, d_f)
        low, high = z % 2, z // 2
        d_other = take_part(d_sum, 1 - low, 2)
        dcq, dekv, *_ = all_after((dcq, dekv), d_other, *sent)
        d_got_a = twin(d_other, 1)
        e_keep, e_send = wgrad(me, (cattn, dc[None]), (a2, dcq[None]), (states, dekv))
        dcq, dekv, e_keep, e_send, d_got_a = all_after((dcq, dekv, e_keep, e_send, d_got_a), *c_n)
        d_half = add(take_part(d_sum, low, 2), d_got_a)
        d_other = take_part(d_half, 1 - high, 2)
        dcq = after(dcq, d_other)
        d_got_b = twin(d_other, 2)
        e_got = swap(e_send, 1)
        c_f, sent = sum_far(c_keep, c_got, c_n, dcq)
        dcq = after(dcq, *sent)
    enc_part = dense_t(dekv[0], w_ckv[:, :width]) + dense_t(dekv[1], w_ckv[:, width:])
    if fast:
        enc_part = enc_part.astype(BF)
        dcq = after(dcq, enc_part)
    c2 = dense_t(dcq, w_cq)
    g1, s1 = norm_sums(xh2, c2)
    dh1 = dh2 + norm_input_grad(xh2, rs2, gain[1], c2)
    da = dh1.astype(BF)
    if fast:
        da, e_got = all_after((da, e_got))
    dattn = dense_t(da, w_out).astype(BF)
    if fast:
        dattn, d_got_b = all_after((dattn, d_got_b), *c_f)
        d_quarter = add(take_part(d_half, high, 2), d_got_b)
        e_n, sent = sum_near(e_keep, e_got, dattn)
        c_sum = sum_own(c_keep, c_got, c_n, c_f)
        c_all = by_chain(c_sum, 1)
        dattn = after(dattn, c_sum, d_quarter, *sent)
        d_got_c = twin(d_quarter, 2)
    dq, dqkv = attn_bwd(z_row, q, kv, self_bias, lse, attn, dattn, True, 0, 5)
    if fast:
        enc_sum = lax.psum_scatter(enc_part, "seq", scatter_dimension=0, tiled=True)
        dattn, dq, dqkv, d_got_c = all_after((dattn, dq, dqkv, d_got_c), *e_n, enc_sum)
        d_half = in_order(d_quarter, d_got_c, high)
        e_f, sent = sum_far(e_keep, e_got, e_n, dattn)
        dattn = after(dattn, d_half, *sent)
        d_got_d = twin(d_half, 1)
    dq, dqkv = attn_bwd(z_row, q, kv, self_bias, lse, attn, dattn, True, 5, 3, (dq, dqkv))
    if fast:
        dq, dqkv, d_got_d = all_after((dq, dqkv, d_got_d), *e_f)
        d_all = in_order(d_half, d_got_d, low)
        e_sum = sum_own(e_keep, e_got, e_n, e_f)
        e_all = by_chain(e_sum, 2)
        dqkv = after(dqkv, e_sum)
        i_keep, i_send = wgrad(me, (attn, da[None]), (a1_full, dqkv))
        dq, dqkv, i_keep, i_send = all_after((dq, dqkv, i_keep, i_send), c_all)
        i_got = swap(i_send, 1)
    if fast:
        c1_part, c1_sums = kv_grad(dqkv, first, x_full, n_seq)
        c1_part, c1_sums, i_got = all_after((c1_part, c1_sums, i_got))
        i_n, sent = sum_near(i_keep, i_got)
        c1_part = after(c1_part, *sent)
        c1_q = dense_t(dq, w_in[:, :width])
        g0, s0 = (a + b for a, b in zip((c1_sums[0], c1_sums[1]), norm_sums(xh1, c1_q)))
        c1_q = after(c1_q, g0, s0)
    else:
        c1_part = dense_t(dqkv[1], w_in[:, width : 2 * width]) + dense_t(dqkv[2], w_in[:, 2 * width :])
        c1_q = dense_t(dq, w_in[:, :width])
        _, xh1_full, _ = layer_norm(xf, gain[0], shift_v[0])
        g0, s0 = (a + b for a, b in zip(norm_sums(xh1_full, c1_part), norm_sums(xh1, c1_q)))

    bias_rows = [total(dq), total(dqkv[2]), total(dh1), total(dcq), total(dekv[1]), total(dh2), total(dh3)]
    small_rows = jnp.stack(bias_rows + [g0, g1, g2, g3, s0, s1, s2, s3])
    small_rows = small_rows.reshape(-1, n_dp, shard).transpose(1, 0, 2)
    small_rows = jnp.concatenate([small_rows, total(du).reshape(n_dp, -1, shard)], axis=1)
    dh1, c1_q = all_after((dh1, c1_q), small_rows)
    if fast:
        c1_sum = scatter_rows(c1_part, z, n_seq)
        i_f, _ = sum_far(i_keep, i_got, i_n)
        i_sum = after(sum_own(i_keep, i_got, i_n, i_f), e_all)
        i_all = by_chain(i_sum, 3)
        e_all, c_all, d_all = all_after((e_all, c_all, d_all), i_sum)
        enc_grad = enc_sum.astype(F32)
        c1 = c1_sum + c1_q
        flat_out = lambda v, r: jnp.concatenate(jnp.split(v, v.shape[0] // r, axis=0), axis=1).astype(F32)
        r_up, r_down = flat_out(c_all, width), d_all.astype(F32)
        r_in, r_out = flat_out(i_all[width:], width), i_all[:width].astype(F32)
        r_cout, r_cq, r_ckv = (flat_out(v, width) for v in jnp.split(e_all, [width, 2 * width], axis=0))
    else:
        c1 = lax.psum_scatter(c1_part, "seq", scatter_dimension=0, tiled=True) + c1_q
        enc_grad = lax.psum_scatter(enc_part, "seq", scatter_dimension=0, tiled=True)
        flat = lambda v: jnp.concatenate(list(v), axis=1)
        pairs = [(a1_full, flat(dqkv)), (attn, da), (a2, dcq), (states, flat(dekv)), (cattn, dc), (a3, du), (gelu_h, dz)]
        grads = [by_chain(by_columns(a, b)).astype(F32) for a, b in pairs]
        r_in, r_out, r_cq, r_ckv, r_cout, r_up, r_down = grads
    if fast:
        small_rows = after(small_rows, i_sum)
        for bit in (1, 2, 4):
            small_rows = small_rows + swap(small_rows, bit)
        for bit in (1, 2):
            small_rows = small_rows + lax.ppermute(small_rows, "seq", [(i, i ^ bit) for i in range(n_seq)])
    else:
        small_rows = lax.psum(small_rows, ("dp", "seq"))
    tokens_grad = dh1 + norm_input_grad(xh1, rs1, gain[0], c1)
    small_own = lax.dynamic_index_in_dim(small_rows, dp, 0, keepdims=False)
    return (
        out.astype(BF)[None],
        tokens_grad[None],
        enc_grad[None],
        r_in,
        r_out,
        r_cq,
        r_ckv,
        r_cout,
        r_up,
        r_down,
        small_own[:n_bias],
        small_own[n_bias : n_bias + n_norm],
        small_own[n_bias + n_norm : n_bias + 2 * n_norm],
        small_own[n_bias + 2 * n_norm :].reshape(1, -1),
    )


def solution(mesh):
    rows, cols, per_dp = P("dp", "seq", None), P(None, "dp"), P("dp", None)
    in_specs = (rows, rows, per_dp, per_dp, per_dp) + (cols,) * 11 + (rows,)
    out_specs = (rows,) * 3 + (cols,) * 11
    return jax.shard_map(local, mesh=mesh, in_specs=in_specs, out_specs=out_specs, check_vma=False)
```

```python
import functools

import jax
import jax.numpy as jnp
from jax import lax
from jax.experimental import pallas as pl
from jax.experimental.pallas import tpu as pltpu
from jax.sharding import PartitionSpec as P

HEADS = 16
EPSILON = 1e-05
BF = jnp.bfloat16
F32 = jnp.float32
NEG = -1e30
VMEM_LIMIT = 56 * 1024 * 1024
SHORT = pl.CostEstimate(flops=0, bytes_accessed=0, transcendentals=0)


def params(**kw):
    return pltpu.CompilerParams(vmem_limit_bytes=VMEM_LIMIT, **kw)


def layer_norm(v, gain, shift):
    center = v - jnp.mean(v, axis=-1, keepdims=True)
    inv = lax.rsqrt(jnp.mean(center * center, axis=-1, keepdims=True) + EPSILON)
    normed = center * inv
    return normed * gain + shift, normed, inv


def norm_input_grad(normed, inv, gain, c):
    e = c * gain
    return inv * (
        e
        - jnp.mean(e, axis=-1, keepdims=True)
        - normed * jnp.mean(e * normed, axis=-1, keepdims=True)
    )


def norm_sums(normed, c):
    return jnp.sum(c * normed, axis=0), jnp.sum(c, axis=0)


def dense(a, b):
    return jnp.dot(a, b, preferred_element_type=F32)


def dense_t(a, b):
    return lax.dot_general(a, b, (((1,), (1,)), ((), ())), preferred_element_type=F32)


def dense_left(a, b):
    return lax.dot_general(a, b, (((0,), (0,)), ((), ())), preferred_element_type=F32)


def gelu_both(u):
    c = 0.7978845608028654
    sq = u * u
    t = jnp.tanh(c * u * (1.0 + 0.044715 * sq))
    half = 0.5 * (1.0 + t)
    return u * half, half + 0.5 * c * u * (1.0 - t * t) * (1.0 + 0.134145 * sq)


def segment_ids(positions, lengths):
    ends = jnp.cumsum(lengths)
    return jnp.sum((positions[:, None] >= ends[None, :]).astype(jnp.int32), axis=1)


def split_heads(block, scale):
    head = block.shape[1] // 2
    lane = lax.broadcasted_iota(jnp.int32, block.shape, 1)
    zero = jnp.zeros_like(block)
    both = jnp.concatenate(
        [jnp.where(lane < head, block, zero), jnp.where(lane >= head, block, zero)], axis=0
    )
    return both if scale is None else both * jnp.asarray(scale, both.dtype)


def join_heads(acc):
    head, rows = acc.shape[0] // 2, acc.shape[1] // 2
    return jnp.concatenate([acc[:head, :rows], acc[head:, rows:]], axis=0)


def nt(a, b):
    return lax.dot_general(a, b, (((1,), (1,)), ((), ())), preferred_element_type=F32)


def tn(a, b):
    return lax.dot_general(a, b, (((0,), (0,)), ((), ())), preferred_element_type=F32)


def attn_fwd_kernel(scale, chunk, q_ref, k_ref, v_ref, bias_ref, o_ref, lse_ref):
    both = split_heads(q_ref[...], scale)
    top = jnp.full(lse_ref.shape[1:], NEG, F32)
    total = jnp.zeros_like(top)
    acc = None
    for c in range(k_ref.shape[0] // chunk):
        rows = slice(c * chunk, (c + 1) * chunk)
        b = bias_ref[rows, :]
        s = nt(k_ref[rows, :], both) + jnp.concatenate([b, b], axis=1)
        new = jnp.maximum(top, jnp.max(s, axis=0, keepdims=True))
        p = jnp.exp(s - new)
        part = tn(v_ref[rows, :], p.astype(BF))
        if acc is None:
            total, acc = jnp.sum(p, axis=0, keepdims=True), part
        else:
            alpha = jnp.exp(top - new)
            total = total * alpha + jnp.sum(p, axis=0, keepdims=True)
            acc = acc * alpha + part
        top = new
    o_ref[...] = jnp.transpose(join_heads(acc / total)).astype(BF)
    lse_ref[0] = top + jnp.log(total)


def attn_fwd(q, kv, bias, first=0, count=HEADS // 2):
    nq, width = q.shape
    nk = kv.shape[0]
    head = width // HEADS
    pairs, pw = HEADS // 2, 2 * head
    chunk = 512
    return pl.pallas_call(
        functools.partial(attn_fwd_kernel, head**-0.5, chunk),
        grid=(count,),
        in_specs=[
            pl.BlockSpec((nq, pw), lambda i: (0, first + i)),
            pl.BlockSpec((nk, pw), lambda i: (0, first + i)),
            pl.BlockSpec((nk, pw), lambda i: (0, pairs + first + i)),
            pl.BlockSpec((nk, nq), lambda i: (0, 0)),
        ],
        out_specs=[
            pl.BlockSpec((nq, pw), lambda i: (0, i)),
            pl.BlockSpec((1, 1, 2 * nq), lambda i: (i, 0, 0)),
        ],
        out_shape=[
            jax.ShapeDtypeStruct((nq, count * pw), BF),
            jax.ShapeDtypeStruct((count, 1, 2 * nq), F32),
        ],
        compiler_params=params(),
        cost_estimate=SHORT,
    )(q, kv, kv, bias)


def attn_bwd_kernel(scale, chunk, padded, z_ref, q_ref, k_ref, v_ref, do_ref, out_ref, bias_ref, lse_ref, *refs):
    dq_ref, dkv_ref = refs[-2:]
    both = split_heads(q_ref[...], scale)
    dboth = split_heads(do_ref[...], None)
    lse = lse_ref[0]
    prod = do_ref[...].astype(F32) * out_ref[...].astype(F32)
    head = prod.shape[1] // 2
    lane = lax.broadcasted_iota(jnp.int32, (8, 2 * head), 1)
    row = lax.broadcasted_iota(jnp.int32, (8, 2 * head), 0)
    pick_head = jnp.where(lane // head == row, 1.0, 0.0)
    delta = lax.dot_general(
        pick_head, prod, (((1,), (1,)), ((), ())), precision=lax.Precision.HIGHEST, preferred_element_type=F32
    )
    delta = jnp.concatenate([delta[0:1], delta[1:2]], axis=1)
    acc = 0.0
    for c in range(k_ref.shape[0] // chunk):
        rows = slice(c * chunk, (c + 1) * chunk)
        b = bias_ref[rows, :]
        k = k_ref[rows, :]
        p = jnp.exp(nt(k, both) + jnp.concatenate([b, b], axis=1) - lse)
        ds = (p * (nt(v_ref[rows, :], dboth) - delta)).astype(BF)
        dkv_ref[padded, rows, :] = dense(ds, both).astype(BF)
        dkv_ref[padded + 1, rows, :] = dense(p.astype(BF), dboth).astype(BF)
        acc = acc + tn(k, ds)
    dq = jnp.transpose(join_heads(acc) * scale).astype(BF)
    dq_ref[...] = dq
    if padded:
        n = dq.shape[0]
        dkv_ref[0] = jnp.zeros(dkv_ref.shape[1:], BF)
        dkv_ref[0, pl.ds(pl.multiple_of(z_ref[0] * n, n), n), :] = dq


def attn_bwd(z, q, kv, bias, lse, out, dout, padded, first=0, count=HEADS // 2, into=()):
    nq, width = q.shape
    nk = kv.shape[0]
    head = width // HEADS
    pairs, pw = HEADS // 2, 2 * head
    chunk = min(768, nk)
    row_spec = pl.BlockSpec((nq, pw), lambda i, z_ref: (0, first + i))
    key_spec = pl.BlockSpec((nk, pw), lambda i, z_ref: (0, first + i))
    vec_spec = pl.BlockSpec((1, 1, 2 * nq), lambda i, z_ref: (first + i, 0, 0))
    depth = 3 if padded else 2
    return pl.pallas_call(
        functools.partial(attn_bwd_kernel, head**-0.5, chunk, depth - 2),
        grid_spec=pltpu.PrefetchScalarGridSpec(
            num_scalar_prefetch=1,
            grid=(count,),
            in_specs=[
                row_spec,
                key_spec,
                pl.BlockSpec((nk, pw), lambda i, z_ref: (0, pairs + first + i)),
                row_spec,
                row_spec,
                pl.BlockSpec((nk, nq), lambda i, z_ref: (0, 0)),
                vec_spec,
            ]
            + [pl.BlockSpec(memory_space=pl.ANY)] * len(into),
            out_specs=[row_spec, pl.BlockSpec((depth, nk, pw), lambda i, z_ref: (0, 0, first + i))],
        ),
        out_shape=[
            jax.ShapeDtypeStruct((nq, width), BF),
            jax.ShapeDtypeStruct((depth, nk, width), BF),
        ],
        input_output_aliases={8: 0, 9: 1} if into else {},
        compiler_params=params(),
        cost_estimate=SHORT,
    )(z, q, kv, kv, dout, out, bias, lse, *into)


def swap(v, bit):
    return lax.ppermute(v, "dp", [(i, i ^ bit) for i in range(8)])


def assemble_kernel(widths, me_ref, *refs):
    ins, out_refs = refs[:10], refs[10:]
    upper = pl.program_id(0) < pl.num_programs(0) // 2
    start = 0
    for n, out_ref in zip(widths, out_refs):
        cols = slice(start, start + n)
        start += n

        def put(t, i, value):
            d = jnp.bitwise_xor(me_ref[0], 2 * i + t)
            out_ref[:, pl.ds(pl.multiple_of(d * n, 128), n)] = value

        for t in (0, 1):
            for i in range(3):
                put(t, i, ins[5 * t + i][:, cols])

            @pl.when(upper)
            def _():
                put(t, 3, ins[5 * t + 3][:, cols])

            @pl.when(jnp.logical_not(upper))
            def _():
                put(t, 3, ins[5 * t + 4][:, cols])


def assemble(me, mine, other, widths):
    rows, total = mine[0].shape
    block = next(b for b in (512, 256, 176, 128, 96, 64, 32, 16) if rows // 2 % b == 0)
    last = rows // 2 // block - 1
    every = pl.BlockSpec((block, total), lambda i, me_ref: (i, 0))
    upper = pl.BlockSpec((block, total), lambda i, me_ref: (jnp.minimum(i, last), 0))
    lower = pl.BlockSpec((block, total), lambda i, me_ref: (jnp.maximum(i - last - 1, 0), 0))
    return pl.pallas_call(
        functools.partial(assemble_kernel, widths),
        grid_spec=pltpu.PrefetchScalarGridSpec(
            num_scalar_prefetch=1,
            grid=(rows // block,),
            in_specs=[every, every, every, upper, lower] * 2,
            out_specs=[pl.BlockSpec((block, 8 * n), lambda i, me_ref: (i, 0)) for n in widths],
        ),
        out_shape=[jax.ShapeDtypeStruct((rows, 8 * n), BF) for n in widths],
        compiler_params=params(),
        cost_estimate=SHORT,
    )(me, *mine, *other)


def project_kernel(z_ref, x_ref, w_ref, gain_ref, shift_ref, bias_ref, a_ref, q_ref, kv_ref):
    width = x_ref.shape[1]
    a = layer_norm(x_ref[...].astype(F32), gain_ref[...], shift_ref[...])[0].astype(BF)
    a_ref[...] = a
    kv_ref[...] = (dense(a, w_ref[:, width:]) + bias_ref[:, width:]).astype(BF)

    @pl.when(pl.program_id(0) == z_ref[0])
    def _():
        q_ref[...] = (dense(a, w_ref[:, :width]) + bias_ref[:, :width]).astype(BF)


def project(z, x, w, gain, shift_row, bias, n):
    total, width = x.shape
    rows = total // n
    whole = lambda v: pl.BlockSpec(v.shape, lambda i, z_ref: (0, 0))
    block = lambda cols: pl.BlockSpec((rows, cols), lambda i, z_ref: (i, 0))
    return pl.pallas_call(
        project_kernel,
        grid_spec=pltpu.PrefetchScalarGridSpec(
            num_scalar_prefetch=1,
            grid=(n,),
            in_specs=[
                block(width),
                pl.BlockSpec((width, 3 * width), lambda i, z_ref: (0, 0)),
                whole(gain),
                whole(shift_row),
                whole(bias),
            ],
            out_specs=[block(width), pl.BlockSpec((rows, width), lambda i, z_ref: (0, 0)), block(2 * width)],
        ),
        out_shape=[
            jax.ShapeDtypeStruct((total, width), BF),
            jax.ShapeDtypeStruct((rows, width), BF),
            jax.ShapeDtypeStruct((total, 2 * width), BF),
        ],
        compiler_params=params(),
        cost_estimate=SHORT,
    )(z, x, w, gain, shift_row, bias)


def assemble_dot_kernel(gelu, me_ref, *refs):
    parts, (x_ref, bias_ref) = refs[:10], refs[10:12]
    w_ref, *outs = refs[12:] if gelu else refs[13:]
    rows, n = parts[0].shape
    step = pl.program_id(0)
    for t in (0, 1):
        cols = pl.ds(pl.multiple_of(jnp.bitwise_xor(me_ref[0] % 2, t) * n, 128), n)
        for k in range(3):

            @pl.when(step == k)
            def _():
                w_ref[:, cols] = parts[5 * t + k][...]

        @pl.when(step == 3)
        def _():
            w_ref[: rows // 2, cols] = parts[5 * t + 3][...]
            w_ref[rows // 2 :, cols] = parts[5 * t + 4][...]

    value = dense(x_ref[...], w_ref[...]) + bias_ref[...]
    if gelu:
        value, slope = gelu_both(value)
        outs[0][...] = value.astype(BF)
        outs[1][...] = slope.astype(BF)
    else:
        outs[0][...] = refs[12][...] + value


def assemble_dot(me, mine, other, x, bias, onto=None):
    rows, n = mine[0].shape
    tok = x.shape[0]
    whole = lambda v: pl.BlockSpec(v.shape, lambda i, me_ref: (0, 0))
    pair = lambda r: pl.BlockSpec((r, 2 * n), lambda i, me_ref: (0, jnp.bitwise_xor(me_ref[0] // 2, i)))
    gelu = onto is None
    outs = [BF, BF] if gelu else [F32]
    return pl.pallas_call(
        functools.partial(assemble_dot_kernel, gelu),
        grid_spec=pltpu.PrefetchScalarGridSpec(
            num_scalar_prefetch=1,
            grid=(4,),
            in_specs=[whole(v) for v in mine + other] + [whole(x), pair(1)] + ([] if gelu else [pair(tok)]),
            out_specs=[pair(rows)] + [pair(tok)] * len(outs),
        ),
        out_shape=[jax.ShapeDtypeStruct((rows, 8 * n), BF)] + [jax.ShapeDtypeStruct((tok, 8 * n), t) for t in outs],
        compiler_params=params(),
        cost_estimate=SHORT,
    )(me, *mine, *other, x, bias, *([] if gelu else [onto]))


def after(v, *others):
    return lax.optimization_barrier((v,) + others)[0]


def all_after(vs, *others):
    return lax.optimization_barrier(tuple(vs) + others)[: len(vs)]


def send_shard(ws, *wait):
    w = after(jnp.concatenate(ws, axis=1) if len(ws) > 1 else ws[0], *wait)
    return w, swap(w, 2), swap(w, 4)


def send_diagonal(got, *wait):
    x, y = all_after(got[1:], *wait)
    half = x.shape[0] // 2
    return swap(x[:half], 4), swap(y[half:], 2)


def send_core(parts, *wait):
    parts = all_after(parts, *wait)
    return parts, tuple(swap(v, 1) for v in parts)


def wgrad_kernel(counts, me_ref, *refs):
    keep_ref, send_ref = refs[-2 - len(counts) : -len(counts)]
    scratch = refs[-len(counts) :]
    at = first = 0
    for blocks, xt_ref in zip(counts, scratch):
        x_ref = refs[at]
        keep_in = [r[0] for r in refs[at + 1 : at + 1 + blocks]]
        send_in = [r[0] for r in refs[at + 1 + blocks : at + 1 + 2 * blocks]]
        at += 1 + 2 * blocks

        @pl.when(pl.program_id(0) == 0)
        def _():
            xt_ref[...] = jnp.transpose(x_ref[...])

        rows = xt_ref.shape[0]
        res = dense(xt_ref[...], jnp.concatenate(keep_in + send_in, axis=1))
        wide = res.shape[1] // 256
        for t, ref in enumerate((keep_ref, send_ref)):
            for j in range(wide):
                col = (t * wide + j) * 128
                ref[0, first + j * rows : first + (j + 1) * rows] = res[:, col : col + 128].astype(BF)
        first += wide * rows


def wgrad(me, *products):
    in_specs, operands, counts, scratch = [], [], [], []
    height = flops = moved = 0
    for x, dy in products:
        tok, rows = x.shape
        parts, _, cols = dy.shape
        n = parts * cols // 8
        width = n if parts == 1 else 128
        per = cols // width
        blocks = n // width
        in_specs.append(pl.BlockSpec((tok, rows), lambda i, me_ref: (0, 0)))
        operands.append(x)
        for t in (0, 1):
            for j in range(blocks):

                def place(i, me_ref, t=t, j=j, blocks=blocks, per=per):
                    b = jnp.bitwise_xor(me_ref[0], 2 * i + t) * blocks + j
                    return (b // per, 0, b % per)

                in_specs.append(pl.BlockSpec((1, tok, width), place))
                operands.append(dy)
        counts.append(blocks)
        scratch.append(pltpu.VMEM((rows, tok), BF))
        height += n // 128 * rows
        flops += 2 * tok * rows * 8 * n
        moved += 2 * (tok * rows + tok * 8 * n + rows * 8 * n)
    out_spec = pl.BlockSpec((1, height, 128), lambda i, me_ref: (i, 0, 0))
    return pl.pallas_call(
        functools.partial(wgrad_kernel, tuple(counts)),
        grid_spec=pltpu.PrefetchScalarGridSpec(
            num_scalar_prefetch=1,
            grid=(4,),
            in_specs=in_specs,
            out_specs=[out_spec, out_spec],
            scratch_shapes=scratch,
        ),
        out_shape=[jax.ShapeDtypeStruct((4, height, 128), BF)] * 2,
        compiler_params=params(),
        cost_estimate=SHORT,
    )(me, *operands)


def up_grad_kernel(me_ref, x_ref, du_ref, w_ref, keep_ref, send_ref, c_ref, xt_ref):
    step = pl.program_id(0)

    @pl.when(step == 0)
    def _():
        xt_ref[...] = jnp.transpose(x_ref[...])

    du = du_ref[...]
    res = dense(xt_ref[...], du)
    rows, n = xt_ref.shape[0], du.shape[1] // 2
    for odd in (0, 1):

        @pl.when(me_ref[0] % 2 == odd)
        def _():
            for t, ref in enumerate((keep_ref, send_ref)):
                for j in range(n // 128):
                    col = (t ^ odd) * n + j * 128
                    ref[0, j * rows : (j + 1) * rows] = res[:, col : col + 128].astype(BF)

    part = nt(du, w_ref[...])

    @pl.when(step == 0)
    def _():
        c_ref[...] = part

    @pl.when(step > 0)
    def _():
        c_ref[...] += part


def up_grad(me, x, du, w):
    tok, rows = x.shape
    n = du.shape[1] // 8
    stacked = n // 128 * rows
    pair = lambda r: pl.BlockSpec((r, 2 * n), lambda i, me_ref: (0, jnp.bitwise_xor(me_ref[0] // 2, i)))
    whole = pl.BlockSpec((tok, rows), lambda i, me_ref: (0, 0))
    shards = pl.BlockSpec((1, stacked, 128), lambda i, me_ref: (i, 0, 0))
    return pl.pallas_call(
        up_grad_kernel,
        grid_spec=pltpu.PrefetchScalarGridSpec(
            num_scalar_prefetch=1,
            grid=(4,),
            in_specs=[whole, pair(tok), pair(rows)],
            out_specs=[shards, shards, whole],
            scratch_shapes=[pltpu.VMEM((rows, tok), BF)],
        ),
        out_shape=[jax.ShapeDtypeStruct((4, stacked, 128), BF)] * 2 + [jax.ShapeDtypeStruct((tok, rows), F32)],
        compiler_params=params(),
        cost_estimate=SHORT,
    )(me, x, du, w)


def gelu_grad_kernel(dz_ref, w_ref, slope_ref, du_ref):
    du_ref[...] = (nt(dz_ref[...], w_ref[...]) * slope_ref[...].astype(F32)).astype(BF)


def gelu_grad(dz, w, slope):
    rows, width = dz.shape
    hidden = w.shape[0]
    block = 1024
    wide = pl.BlockSpec((rows, block), lambda i: (0, i))
    return pl.pallas_call(
        gelu_grad_kernel,
        grid=(hidden // block,),
        in_specs=[
            pl.BlockSpec((rows, width), lambda i: (0, 0)),
            pl.BlockSpec((block, width), lambda i: (i, 0)),
            wide,
        ],
        out_specs=wide,
        out_shape=jax.ShapeDtypeStruct((rows, hidden), BF),
        compiler_params=params(),
        cost_estimate=SHORT,
    )(dz, w, slope)


def kv_grad_kernel(dk_ref, dv_ref, wk_ref, wv_ref, x_ref, part_ref, sums_ref):
    part = nt(dk_ref[0], wk_ref[...]) + nt(dv_ref[0], wv_ref[...])
    part_ref[0] = part.astype(BF)
    _, normed, _ = layer_norm(x_ref[...].astype(F32), 1.0, 0.0)

    @pl.when(pl.program_id(0) == 0)
    def _():
        sums_ref[...] = jnp.zeros_like(sums_ref)

    sums_ref[0:1] += jnp.sum(part * normed, axis=0, keepdims=True)
    sums_ref[1:2] += jnp.sum(part, axis=0, keepdims=True)


def kv_grad(dqkv, w, x, n):
    _, rows, width = dqkv.shape
    block = rows // n
    return pl.pallas_call(
        kv_grad_kernel,
        grid=(n,),
        in_specs=[
            pl.BlockSpec((1, block, width), lambda i: (1, i, 0)),
            pl.BlockSpec((1, block, width), lambda i: (2, i, 0)),
            pl.BlockSpec((width, width), lambda i: (0, 1)),
            pl.BlockSpec((width, width), lambda i: (0, 2)),
            pl.BlockSpec((block, width), lambda i: (i, 0)),
        ],
        out_specs=[
            pl.BlockSpec((1, block, width), lambda i: (i, 0, 0)),
            pl.BlockSpec((8, width), lambda i: (0, 0)),
        ],
        out_shape=[jax.ShapeDtypeStruct((n, block, width), BF), jax.ShapeDtypeStruct((8, width), F32)],
        compiler_params=params(),
        cost_estimate=SHORT,
    )(dqkv, dqkv, w, w, x)


def add(*terms):
    total = terms[0].astype(F32)
    for t in terms[1:]:
        total = total + t.astype(F32)
    return total.astype(BF)


def pick(v, i, half):
    rows = v.shape[1] // 2
    return v[i, half * rows : (half + 1) * rows]


def sum_near(keep, got, *wait):
    keep, got = all_after((keep, got), *wait)
    half = keep.shape[1] // 2
    xa = add(keep[1:4:2, :half], got[1:4:2, :half])
    yb = add(keep[2:4, half:], got[2:4, half:])
    return (swap(xa, 2), swap(yb, 4)), (xa, yb)


def sum_far(keep, got, near, *wait):
    xa, yb, keep, got = all_after(tuple(near) + (keep, got), *wait)
    ya = add(pick(keep, 2, 0), pick(got, 2, 0), xa[1])
    xb = add(pick(keep, 1, 1), pick(got, 1, 1), yb[1])
    return (swap(ya, 4), swap(xb, 2)), (ya, xb)


def sum_own(keep, got, near, far):
    halves = [add(pick(keep, 0, h), pick(got, 0, h), near[h][0], far[h]) for h in (0, 1)]
    return jnp.concatenate(halves, axis=0)


def shift(v, n, step, pairs):
    return lax.ppermute(v, "seq", [(a, a + step) for a in pairs if 0 <= a + step < n])


def gather_rows(v, z, n):
    right, left = [v], [v]
    for s in range(n - 1):
        right.append(shift(right[-1], n, 1, range(s, n)))
        left.append(shift(left[-1], n, -1, range(0, n - s)))
    out = []
    for k in range(n):
        val = v
        for d in range(1, n):
            if k + d < n:
                val = jnp.where(z == k + d, right[d], val)
            if k - d >= 0:
                val = jnp.where(z == k - d, left[d], val)
        out.append(val)
    return jnp.concatenate(out, axis=0)


def scatter_rows(v, z, n, wait=()):
    part = lambda t: lax.dynamic_index_in_dim(v, jnp.clip(t, 0, n - 1), 0, keepdims=False).astype(F32)
    r = l = None
    for p in range(1, n):
        rv, lv = part(n - p + z), part(p - n + z)
        if r is not None:
            r, l = all_after((r, l), *wait)
            rv, lv = rv + r.astype(F32), lv + l.astype(F32)
        r = shift(rv.astype(BF), n, 1, range(0, p))
        l = shift(lv.astype(BF), n, -1, range(n - p, n))
    return part(z) + r.astype(F32) + l.astype(F32)


def twin(v, bit):
    return lax.ppermute(v, "seq", [(i, i ^ bit) for i in range(4)])


def take_part(v, at, count):
    rows = v.shape[0] // count
    return lax.dynamic_slice_in_dim(v, at * rows, rows)


def in_order(mine, other, bit):
    return jnp.where(bit == 0, jnp.concatenate([mine, other]), jnp.concatenate([other, mine]))


def local(
    tokens, enc_states, order, lengths, enc_lengths, attn_in, attn_out, cross_q, cross_kv,
    cross_out, ffn_in, ffn_out, proj_bias, gains, ln_bias, ffn_bias, cotangent,
):
    n_dp, n_seq = lax.axis_size("dp"), lax.axis_size("seq")
    z = lax.axis_index("seq")
    dp = lax.axis_index("dp")
    me = dp.astype(jnp.int32).reshape(1)
    fast = n_dp == 8 and n_seq == 4 and attn_out.shape[1] % 128 == 0
    x = tokens[0]
    rows, width = x.shape
    enc_rows = enc_states.shape[1] * n_seq
    group_rows = rows * n_seq
    shard = attn_out.shape[1]

    small = jnp.concatenate([proj_bias, gains, ln_bias, ffn_bias.reshape(-1, shard)], axis=0)
    count = small.shape[0]
    if fast:
        pad_rows = 32
        w = attn_in.shape[1]
        flat = jnp.concatenate([small.reshape(-1), jnp.zeros((pad_rows * w - small.size,), BF)])
        a_near = send_shard([jnp.concatenate([attn_in, flat.reshape(pad_rows, w)], axis=0)])
        x_full = lax.all_gather(x, "seq", axis=0, tiled=True)
        a_far = send_diagonal(a_near)
        b_near = send_shard([cross_kv, attn_out, cross_q, cross_out], *a_near[1:])
        states = lax.all_gather(after(enc_states[0], x_full), "seq", axis=0, tiled=True)
        (first,) = assemble(me, *send_core(a_near + a_far), (w,))
        b_far = send_diagonal(b_near, first)
        w_in = first[:width]
        small_all = first[width:].reshape(pad_rows, n_dp, w).transpose(1, 0, 2).reshape(n_dp, -1)
        small_all = small_all[:, : small.size].reshape(n_dp, count, shard)
    else:
        x_full = gather_rows(x, z, n_seq)
        states = gather_rows(enc_states[0], z, n_seq)
        gather = lambda v: lax.all_gather(v, "dp", axis=1, tiled=True)
        w_in, w_ckv, w_out, w_cq = gather(attn_in), gather(cross_kv), gather(attn_out), gather(cross_q)
        w_cout, w_up, w_down = gather(cross_out), gather(ffn_in), gather(ffn_out)
        small_all = lax.all_gather(small, "dp", axis=0, tiled=False)
    n_bias, n_norm = proj_bias.shape[0], gains.shape[0]
    rows_all = small_all[:, : n_bias + 2 * n_norm].transpose(1, 0, 2).reshape(-1, width).astype(F32)
    bias = rows_all[:n_bias]
    gain = rows_all[n_bias : n_bias + n_norm]
    shift_v = rows_all[n_bias + n_norm :]
    up_bias = small_all[:, n_bias + 2 * n_norm :].reshape(-1).astype(F32)

    place = order[0]
    seg = segment_ids(place, lengths[0])
    seg_enc = segment_ids(jnp.arange(enc_rows, dtype=jnp.int32), enc_lengths[0])
    my_place = lax.dynamic_slice_in_dim(place, z * rows, rows)
    my_seg = lax.dynamic_slice_in_dim(seg, z * rows, rows)
    self_keep = (seg[:, None] == my_seg[None, :]) & (place[:, None] <= my_place[None, :])
    self_bias = jnp.where(self_keep, 0.0, NEG).astype(F32)
    cross_bias = jnp.where(seg_enc[:, None] == my_seg[None, :], 0.0, NEG).astype(F32)
    zero_row = jnp.zeros((width,), F32)

    x32 = x.astype(F32)
    v1_own, xh1, rs1 = layer_norm(x32, gain[0], shift_v[0])
    z_row = z.astype(jnp.int32).reshape(1)
    if fast:
        x_full, self_bias, cross_bias = all_after((x_full, self_bias, cross_bias))
        qkv_bias = jnp.concatenate([bias[0], zero_row, bias[1]])[None]
        a1_full, q, kv = project(z_row, x_full, first, gain[:1], shift_v[:1], qkv_bias, n_seq)
    else:
        xf = x_full.astype(F32)
        a1_full = layer_norm(xf, gain[0], shift_v[0])[0].astype(BF)
        kv = (dense(a1_full, w_in[:, width:]) + jnp.concatenate([zero_row, bias[1]])).astype(BF)
        q = (dense(v1_own.astype(BF), w_in[:, :width]) + bias[0]).astype(BF)
    if fast:
        b_parts, b_other = send_core(b_near + b_far, kv)
        c_near = send_shard([ffn_in], kv)
        q, kv, *_ = all_after((q, kv), *b_far)
    half = HEADS // 4
    attn_a, lse_a = attn_fwd(q, kv, self_bias, 0, half)
    if fast:
        widths = tuple(v.shape[1] for v in (cross_kv, attn_out, cross_q, cross_out))
        b_parts = all_after(b_parts, attn_a)
        w_ckv, w_out, w_cq, w_cout = assemble(me, b_parts, b_other, widths)
        q, attn_a, lse_a, w_out, states = all_after((q, attn_a, lse_a, w_out, states), *c_near[1:])
        c_far = send_diagonal(c_near, attn_a)
    attn_b, lse_b = attn_fwd(q, kv, self_bias, half, half)
    attn = jnp.concatenate([attn_a, attn_b], axis=1)
    lse = jnp.concatenate([lse_a, lse_b], axis=0)
    if fast:
        attn, lse = all_after((attn, lse), *c_far)
        d_near = send_shard([ffn_out], attn)
        c_parts, c_other = send_core(c_near + c_far, attn)
    h1 = x32 + dense(attn, w_out) + bias[2]
    v2, xh2, rs2 = layer_norm(h1, gain[1], shift_v[1])
    a2 = v2.astype(BF)
    cq = (dense(a2, w_cq) + bias[3]).astype(BF)
    ekv = (dense(states, w_ckv) + jnp.concatenate([zero_row, bias[4]])).astype(BF)
    if fast:
        cq = after(cq, ekv, *c_other)
    cattn, clse = attn_fwd(cq, ekv, cross_bias)
    if fast:
        cattn = after(cattn, *d_near[1:])
        d_far = send_diagonal(d_near, cattn)
        d_parts, d_other = send_core(d_near, cattn)
        c_parts = all_after(c_parts, cattn)
    h2 = h1 + dense(cattn, w_cout) + bias[5]
    v3, xh3, rs3 = layer_norm(h2, gain[2], shift_v[2])
    a3 = v3.astype(BF)
    if fast:
        w_up, gelu_h, slope = assemble_dot(me, c_parts, c_other, a3, up_bias[None])
        gelu_h, *d_far = all_after((gelu_h,) + d_far)
        d_rest, d_other_rest = send_core(d_far, gelu_h)
        d_parts, d_other = d_parts + d_rest, d_other + d_other_rest
        w_down, h3 = assemble_dot(me, d_parts, d_other, gelu_h, bias[6:7], h2)
    else:
        gelu, slope = gelu_both(dense(a3, w_up) + up_bias)
        gelu_h, slope = gelu.astype(BF), slope.astype(BF)
        h3 = h2 + dense(gelu_h, w_down) + bias[6]
    out, xh4, rs4 = layer_norm(h3, gain[3], shift_v[3])

    total = lambda v: jnp.sum(v, axis=0, dtype=F32)
    by_columns = lambda a, b: lax.psum_scatter(dense_left(a, b), "dp", scatter_dimension=1, tiled=True).astype(BF)
    ct = cotangent[0].astype(F32)
    g3, s3 = norm_sums(xh4, ct)
    dh3 = norm_input_grad(xh4, rs4, gain[3], ct)
    dz = dh3.astype(BF)

    def by_chain(v, turn=0):
        listed = [(turn + i) % n_seq for i in range(n_seq)]
        return lax.psum(v, "seq", axis_index_groups=[listed])

    if fast:
        dz, gelu_h = all_after((dz, gelu_h))
        d_keep, d_send = wgrad(me, (gelu_h, dz[None]))
        dz, d_keep, d_send = all_after((dz, d_keep, d_send))
        d_got = swap(d_send, 1)
    du = gelu_grad(dz, w_down, slope)
    if fast:
        du, d_got = all_after((du, d_got))
        d_n, sent = sum_near(d_keep, d_got, du)
        du, *_ = all_after((du,), *sent)
        c_keep, c_send, c3 = up_grad(me, a3, du, w_up)
        c3, c_send, *d_n = all_after((c3, c_send) + tuple(d_n))
        c_got = swap(c_send, 1)
    else:
        c3 = dense_t(du, w_up)
    g2, s2 = norm_sums(xh3, c3)
    dh2 = dh3 + norm_input_grad(xh3, rs3, gain[2], c3)
    dc = dh2.astype(BF)
    dcattn = dense_t(dc, w_cout).astype(BF)
    if fast:
        dcattn, *_ = all_after((dcattn,), *d_n)
        d_f, sent = sum_far(d_keep, d_got, d_n, dcattn)
        dcattn = after(dcattn, *sent)
    dcq, dekv = attn_bwd(z_row, cq, ekv, cross_bias, clse, cattn, dcattn, False)
    if fast:
        dcq, dekv = all_after((dcq, dekv), *d_f)
        c_n, sent = sum_near(c_keep, c_got, dcq)
        d_sum = sum_own(d_keep, d_got, d_n, d_f)
        low, high = z % 2, z // 2
        d_other = take_part(d_sum, 1 - low, 2)
        dcq, dekv, *_ = all_after((dcq, dekv), d_other, *sent)
        d_got_a = twin(d_other, 1)
        e_keep, e_send = wgrad(me, (cattn, dc[None]), (a2, dcq[None]), (states, dekv))
        dcq, dekv, e_keep, e_send, d_got_a = all_after((dcq, dekv, e_keep, e_send, d_got_a), *c_n)
        d_half = add(take_part(d_sum, low, 2), d_got_a)
        d_other = take_part(d_half, 1 - high, 2)
        dcq = after(dcq, d_other)
        d_got_b = twin(d_other, 2)
        e_got = swap(e_send, 1)
        c_f, sent = sum_far(c_keep, c_got, c_n, dcq)
        dcq = after(dcq, *sent)
    enc_part = dense_t(dekv[0], w_ckv[:, :width]) + dense_t(dekv[1], w_ckv[:, width:])
    if fast:
        enc_part = enc_part.astype(BF)
        dcq = after(dcq, enc_part)
    c2 = dense_t(dcq, w_cq)
    g1, s1 = norm_sums(xh2, c2)
    dh1 = dh2 + norm_input_grad(xh2, rs2, gain[1], c2)
    da = dh1.astype(BF)
    if fast:
        da, e_got = all_after((da, e_got))
    dattn = dense_t(da, w_out).astype(BF)
    if fast:
        dattn, d_got_b = all_after((dattn, d_got_b), *c_f)
        d_quarter = add(take_part(d_half, high, 2), d_got_b)
        e_n, sent = sum_near(e_keep, e_got, dattn)
        c_sum = sum_own(c_keep, c_got, c_n, c_f)
        c_all = by_chain(c_sum, 1)
        dattn = after(dattn, c_sum, d_quarter, *sent)
        d_got_c = twin(d_quarter, 2)
    dq, dqkv = attn_bwd(z_row, q, kv, self_bias, lse, attn, dattn, True, 0, 5)
    if fast:
        enc_sum = lax.psum_scatter(enc_part, "seq", scatter_dimension=0, tiled=True)
        dattn, dq, dqkv, d_got_c = all_after((dattn, dq, dqkv, d_got_c), *e_n, enc_sum)
        d_half = in_order(d_quarter, d_got_c, high)
        e_f, sent = sum_far(e_keep, e_got, e_n, dattn)
        dattn = after(dattn, d_half, *sent)
        d_got_d = twin(d_half, 1)
    dq, dqkv = attn_bwd(z_row, q, kv, self_bias, lse, attn, dattn, True, 5, 3, (dq, dqkv))
    if fast:
        dq, dqkv, d_got_d = all_after((dq, dqkv, d_got_d), *e_f)
        d_all = in_order(d_half, d_got_d, low)
        e_sum = sum_own(e_keep, e_got, e_n, e_f)
        e_all = by_chain(e_sum, 2)
        dqkv = after(dqkv, e_sum)
        i_keep, i_send = wgrad(me, (attn, da[None]), (a1_full, dqkv))
        dq, dqkv, i_keep, i_send = all_after((dq, dqkv, i_keep, i_send), c_all)
        i_got = swap(i_send, 1)
    if fast:
        c1_part, c1_sums = kv_grad(dqkv, first, x_full, n_seq)
        c1_part, c1_sums, i_got = all_after((c1_part, c1_sums, i_got))
        i_n, sent = sum_near(i_keep, i_got)
        c1_part = after(c1_part, *sent)
        c1_q = dense_t(dq, w_in[:, :width])
        g0, s0 = (a + b for a, b in zip((c1_sums[0], c1_sums[1]), norm_sums(xh1, c1_q)))
        c1_q = after(c1_q, g0, s0)
    else:
        c1_part = dense_t(dqkv[1], w_in[:, width : 2 * width]) + dense_t(dqkv[2], w_in[:, 2 * width :])
        c1_q = dense_t(dq, w_in[:, :width])
        _, xh1_full, _ = layer_norm(xf, gain[0], shift_v[0])
        g0, s0 = (a + b for a, b in zip(norm_sums(xh1_full, c1_part), norm_sums(xh1, c1_q)))

    bias_rows = [total(dq), total(dqkv[2]), total(dh1), total(dcq), total(dekv[1]), total(dh2), total(dh3)]
    small_rows = jnp.stack(bias_rows + [g0, g1, g2, g3, s0, s1, s2, s3])
    small_rows = small_rows.reshape(-1, n_dp, shard).transpose(1, 0, 2)
    small_rows = jnp.concatenate([small_rows, total(du).reshape(n_dp, -1, shard)], axis=1)
    dh1, c1_q = all_after((dh1, c1_q), small_rows)
    if fast:
        c1_sum = scatter_rows(c1_part, z, n_seq)
        i_f, _ = sum_far(i_keep, i_got, i_n)
        i_sum = after(sum_own(i_keep, i_got, i_n, i_f), e_all)
        i_all = by_chain(i_sum, 3)
        e_all, c_all, d_all = all_after((e_all, c_all, d_all), i_sum)
        enc_grad = enc_sum.astype(F32)
        c1 = c1_sum + c1_q
        flat_out = lambda v, r: jnp.concatenate(jnp.split(v, v.shape[0] // r, axis=0), axis=1).astype(F32)
        r_up, r_down = flat_out(c_all, width), d_all.astype(F32)
        r_in, r_out = flat_out(i_all[width:], width), i_all[:width].astype(F32)
        r_cout, r_cq, r_ckv = (flat_out(v, width) for v in jnp.split(e_all, [width, 2 * width], axis=0))
    else:
        c1 = lax.psum_scatter(c1_part, "seq", scatter_dimension=0, tiled=True) + c1_q
        enc_grad = lax.psum_scatter(enc_part, "seq", scatter_dimension=0, tiled=True)
        flat = lambda v: jnp.concatenate(list(v), axis=1)
        pairs = [(a1_full, flat(dqkv)), (attn, da), (a2, dcq), (states, flat(dekv)), (cattn, dc), (a3, du), (gelu_h, dz)]
        grads = [by_chain(by_columns(a, b)).astype(F32) for a, b in pairs]
        r_in, r_out, r_cq, r_ckv, r_cout, r_up, r_down = grads
    if fast:
        small_rows = after(small_rows, i_sum)
        for bit in (1, 2, 4):
            small_rows = small_rows + swap(small_rows, bit)
        for bit in (1, 2):
            small_rows = small_rows + lax.ppermute(small_rows, "seq", [(i, i ^ bit) for i in range(n_seq)])
    else:
        small_rows = lax.psum(small_rows, ("dp", "seq"))
    tokens_grad = dh1 + norm_input_grad(xh1, rs1, gain[0], c1)
    small_own = lax.dynamic_index_in_dim(small_rows, dp, 0, keepdims=False)
    return (
        out.astype(BF)[None],
        tokens_grad[None],
        enc_grad[None],
        r_in,
        r_out,
        r_cq,
        r_ckv,
        r_cout,
        r_up,
        r_down,
        small_own[:n_bias],
        small_own[n_bias : n_bias + n_norm],
        small_own[n_bias + n_norm : n_bias + 2 * n_norm],
        small_own[n_bias + 2 * n_norm :].reshape(1, -1),
    )


def solution(mesh):
    rows, cols, per_dp = P("dp", "seq", None), P(None, "dp"), P("dp", None)
    in_specs = (rows, rows, per_dp, per_dp, per_dp) + (cols,) * 11 + (rows,)
    out_specs = (rows,) * 3 + (cols,) * 11
    return jax.shard_map(local, mesh=mesh, in_specs=in_specs, out_specs=out_specs, check_vma=False)
```

```python
import functools

import jax
import jax.numpy as jnp
from jax import lax
from jax.experimental import pallas as pl
from jax.experimental.pallas import tpu as pltpu
from jax.sharding import PartitionSpec as P

HEADS = 16
EPSILON = 1e-05
BF = jnp.bfloat16
F32 = jnp.float32
NEG = -1e30
VMEM_LIMIT = 56 * 1024 * 1024
SHORT = pl.CostEstimate(flops=0, bytes_accessed=0, transcendentals=0)


def params(**kw):
    return pltpu.CompilerParams(vmem_limit_bytes=VMEM_LIMIT, **kw)


def layer_norm(v, gain, shift):
    center = v - jnp.mean(v, axis=-1, keepdims=True)
    inv = lax.rsqrt(jnp.mean(center * center, axis=-1, keepdims=True) + EPSILON)
    normed = center * inv
    return normed * gain + shift, normed, inv


def norm_input_grad(normed, inv, gain, c):
    e = c * gain
    return inv * (
        e
        - jnp.mean(e, axis=-1, keepdims=True)
        - normed * jnp.mean(e * normed, axis=-1, keepdims=True)
    )


def norm_sums(normed, c):
    return jnp.sum(c * normed, axis=0), jnp.sum(c, axis=0)


def dense(a, b):
    return jnp.dot(a, b, preferred_element_type=F32)


def dense_t(a, b):
    return lax.dot_general(a, b, (((1,), (1,)), ((), ())), preferred_element_type=F32)


def dense_left(a, b):
    return lax.dot_general(a, b, (((0,), (0,)), ((), ())), preferred_element_type=F32)


def gelu_both(u):
    c = 0.7978845608028654
    sq = u * u
    t = jnp.tanh(c * u * (1.0 + 0.044715 * sq))
    half = 0.5 * (1.0 + t)
    return u * half, half + 0.5 * c * u * (1.0 - t * t) * (1.0 + 0.134145 * sq)


def segment_ids(positions, lengths):
    ends = jnp.cumsum(lengths)
    return jnp.sum((positions[:, None] >= ends[None, :]).astype(jnp.int32), axis=1)


def split_heads(block, scale):
    head = block.shape[1] // 2
    lane = lax.broadcasted_iota(jnp.int32, block.shape, 1)
    zero = jnp.zeros_like(block)
    both = jnp.concatenate(
        [jnp.where(lane < head, block, zero), jnp.where(lane >= head, block, zero)], axis=0
    )
    return both if scale is None else both * jnp.asarray(scale, both.dtype)


def join_heads(acc):
    head, rows = acc.shape[0] // 2, acc.shape[1] // 2
    return jnp.concatenate([acc[:head, :rows], acc[head:, rows:]], axis=0)


def nt(a, b):
    return lax.dot_general(a, b, (((1,), (1,)), ((), ())), preferred_element_type=F32)


def tn(a, b):
    return lax.dot_general(a, b, (((0,), (0,)), ((), ())), preferred_element_type=F32)


def attn_fwd_kernel(scale, chunk, q_ref, k_ref, v_ref, bias_ref, o_ref, lse_ref):
    both = split_heads(q_ref[...], scale)
    top = jnp.full(lse_ref.shape[1:], NEG, F32)
    total = jnp.zeros_like(top)
    acc = None
    for c in range(k_ref.shape[0] // chunk):
        rows = slice(c * chunk, (c + 1) * chunk)
        b = bias_ref[rows, :]
        s = nt(k_ref[rows, :], both) + jnp.concatenate([b, b], axis=1)
        new = jnp.maximum(top, jnp.max(s, axis=0, keepdims=True))
        p = jnp.exp(s - new)
        part = tn(v_ref[rows, :], p.astype(BF))
        if acc is None:
            total, acc = jnp.sum(p, axis=0, keepdims=True), part
        else:
            alpha = jnp.exp(top - new)
            total = total * alpha + jnp.sum(p, axis=0, keepdims=True)
            acc = acc * alpha + part
        top = new
    o_ref[...] = jnp.transpose(join_heads(acc / total)).astype(BF)
    lse_ref[0] = top + jnp.log(total)


def attn_fwd(q, kv, bias, first=0, count=HEADS // 2):
    nq, width = q.shape
    nk = kv.shape[0]
    head = width // HEADS
    pairs, pw = HEADS // 2, 2 * head
    chunk = min(768, nk)
    return pl.pallas_call(
        functools.partial(attn_fwd_kernel, head**-0.5, chunk),
        grid=(count,),
        in_specs=[
            pl.BlockSpec((nq, pw), lambda i: (0, first + i)),
            pl.BlockSpec((nk, pw), lambda i: (0, first + i)),
            pl.BlockSpec((nk, pw), lambda i: (0, pairs + first + i)),
            pl.BlockSpec((nk, nq), lambda i: (0, 0)),
        ],
        out_specs=[
            pl.BlockSpec((nq, pw), lambda i: (0, i)),
            pl.BlockSpec((1, 1, 2 * nq), lambda i: (i, 0, 0)),
        ],
        out_shape=[
            jax.ShapeDtypeStruct((nq, count * pw), BF),
            jax.ShapeDtypeStruct((count, 1, 2 * nq), F32),
        ],
        compiler_params=params(),
        cost_estimate=SHORT,
    )(q, kv, kv, bias)


def attn_bwd_kernel(scale, chunk, padded, z_ref, q_ref, k_ref, v_ref, do_ref, out_ref, bias_ref, lse_ref, *refs):
    dq_ref, dkv_ref = refs[-2:]
    both = split_heads(q_ref[...], scale)
    dboth = split_heads(do_ref[...], None)
    lse = lse_ref[0]
    prod = do_ref[...].astype(F32) * out_ref[...].astype(F32)
    head = prod.shape[1] // 2
    lane = lax.broadcasted_iota(jnp.int32, (8, 2 * head), 1)
    row = lax.broadcasted_iota(jnp.int32, (8, 2 * head), 0)
    pick_head = jnp.where(lane // head == row, 1.0, 0.0)
    delta = lax.dot_general(
        pick_head, prod, (((1,), (1,)), ((), ())), precision=lax.Precision.HIGHEST, preferred_element_type=F32
    )
    delta = jnp.concatenate([delta[0:1], delta[1:2]], axis=1)
    acc = 0.0
    for c in range(k_ref.shape[0] // chunk):
        rows = slice(c * chunk, (c + 1) * chunk)
        b = bias_ref[rows, :]
        k = k_ref[rows, :]
        p = jnp.exp(nt(k, both) + jnp.concatenate([b, b], axis=1) - lse)
        ds = (p * (nt(v_ref[rows, :], dboth) - delta)).astype(BF)
        dkv_ref[padded, rows, :] = dense(ds, both).astype(BF)
        dkv_ref[padded + 1, rows, :] = dense(p.astype(BF), dboth).astype(BF)
        acc = acc + tn(k, ds)
    dq = jnp.transpose(join_heads(acc) * scale).astype(BF)
    dq_ref[...] = dq
    if padded:
        n = dq.shape[0]
        dkv_ref[0] = jnp.zeros(dkv_ref.shape[1:], BF)
        dkv_ref[0, pl.ds(pl.multiple_of(z_ref[0] * n, n), n), :] = dq


def attn_bwd(z, q, kv, bias, lse, out, dout, padded, first=0, count=HEADS // 2, into=()):
    nq, width = q.shape
    nk = kv.shape[0]
    head = width // HEADS
    pairs, pw = HEADS // 2, 2 * head
    chunk = min(768, nk)
    row_spec = pl.BlockSpec((nq, pw), lambda i, z_ref: (0, first + i))
    key_spec = pl.BlockSpec((nk, pw), lambda i, z_ref: (0, first + i))
    vec_spec = pl.BlockSpec((1, 1, 2 * nq), lambda i, z_ref: (first + i, 0, 0))
    depth = 3 if padded else 2
    return pl.pallas_call(
        functools.partial(attn_bwd_kernel, head**-0.5, chunk, depth - 2),
        grid_spec=pltpu.PrefetchScalarGridSpec(
            num_scalar_prefetch=1,
            grid=(count,),
            in_specs=[
                row_spec,
                key_spec,
                pl.BlockSpec((nk, pw), lambda i, z_ref: (0, pairs + first + i)),
                row_spec,
                row_spec,
                pl.BlockSpec((nk, nq), lambda i, z_ref: (0, 0)),
                vec_spec,
            ]
            + [pl.BlockSpec(memory_space=pl.ANY)] * len(into),
            out_specs=[row_spec, pl.BlockSpec((depth, nk, pw), lambda i, z_ref: (0, 0, first + i))],
        ),
        out_shape=[
            jax.ShapeDtypeStruct((nq, width), BF),
            jax.ShapeDtypeStruct((depth, nk, width), BF),
        ],
        input_output_aliases={8: 0, 9: 1} if into else {},
        compiler_params=params(),
        cost_estimate=SHORT,
    )(z, q, kv, kv, dout, out, bias, lse, *into)


def swap(v, bit):
    return lax.ppermute(v, "dp", [(i, i ^ bit) for i in range(8)])


def assemble_kernel(widths, me_ref, *refs):
    ins, out_refs = refs[:10], refs[10:]
    upper = pl.program_id(0) < pl.num_programs(0) // 2
    start = 0
    for n, out_ref in zip(widths, out_refs):
        cols = slice(start, start + n)
        start += n

        def put(t, i, value):
            d = jnp.bitwise_xor(me_ref[0], 2 * i + t)
            out_ref[:, pl.ds(pl.multiple_of(d * n, 128), n)] = value

        for t in (0, 1):
            for i in range(3):
                put(t, i, ins[5 * t + i][:, cols])

            @pl.when(upper)
            def _():
                put(t, 3, ins[5 * t + 3][:, cols])

            @pl.when(jnp.logical_not(upper))
            def _():
                put(t, 3, ins[5 * t + 4][:, cols])


def assemble(me, mine, other, widths):
    rows, total = mine[0].shape
    block = next(b for b in (512, 256, 176, 128, 96, 64, 32, 16) if rows // 2 % b == 0)
    last = rows // 2 // block - 1
    every = pl.BlockSpec((block, total), lambda i, me_ref: (i, 0))
    upper = pl.BlockSpec((block, total), lambda i, me_ref: (jnp.minimum(i, last), 0))
    lower = pl.BlockSpec((block, total), lambda i, me_ref: (jnp.maximum(i - last - 1, 0), 0))
    return pl.pallas_call(
        functools.partial(assemble_kernel, widths),
        grid_spec=pltpu.PrefetchScalarGridSpec(
            num_scalar_prefetch=1,
            grid=(rows // block,),
            in_specs=[every, every, every, upper, lower] * 2,
            out_specs=[pl.BlockSpec((block, 8 * n), lambda i, me_ref: (i, 0)) for n in widths],
        ),
        out_shape=[jax.ShapeDtypeStruct((rows, 8 * n), BF) for n in widths],
        compiler_params=params(),
        cost_estimate=SHORT,
    )(me, *mine, *other)


def project_kernel(z_ref, x_ref, w_ref, gain_ref, shift_ref, bias_ref, a_ref, q_ref, kv_ref):
    width = x_ref.shape[1]
    a = layer_norm(x_ref[...].astype(F32), gain_ref[...], shift_ref[...])[0].astype(BF)
    a_ref[...] = a
    kv_ref[...] = (dense(a, w_ref[:, width:]) + bias_ref[:, width:]).astype(BF)

    @pl.when(pl.program_id(0) == z_ref[0])
    def _():
        q_ref[...] = (dense(a, w_ref[:, :width]) + bias_ref[:, :width]).astype(BF)


def project(z, x, w, gain, shift_row, bias, n):
    total, width = x.shape
    rows = total // n
    whole = lambda v: pl.BlockSpec(v.shape, lambda i, z_ref: (0, 0))
    block = lambda cols: pl.BlockSpec((rows, cols), lambda i, z_ref: (i, 0))
    return pl.pallas_call(
        project_kernel,
        grid_spec=pltpu.PrefetchScalarGridSpec(
            num_scalar_prefetch=1,
            grid=(n,),
            in_specs=[
                block(width),
                pl.BlockSpec((width, 3 * width), lambda i, z_ref: (0, 0)),
                whole(gain),
                whole(shift_row),
                whole(bias),
            ],
            out_specs=[block(width), pl.BlockSpec((rows, width), lambda i, z_ref: (0, 0)), block(2 * width)],
        ),
        out_shape=[
            jax.ShapeDtypeStruct((total, width), BF),
            jax.ShapeDtypeStruct((rows, width), BF),
            jax.ShapeDtypeStruct((total, 2 * width), BF),
        ],
        compiler_params=params(),
        cost_estimate=SHORT,
    )(z, x, w, gain, shift_row, bias)


def assemble_dot_kernel(gelu, me_ref, *refs):
    parts, (x_ref, bias_ref) = refs[:10], refs[10:12]
    w_ref, *outs = refs[12:] if gelu else refs[13:]
    rows, n = parts[0].shape
    step = pl.program_id(0)
    for t in (0, 1):
        cols = pl.ds(pl.multiple_of(jnp.bitwise_xor(me_ref[0] % 2, t) * n, 128), n)
        for k in range(3):

            @pl.when(step == k)
            def _():
                w_ref[:, cols] = parts[5 * t + k][...]

        @pl.when(step == 3)
        def _():
            w_ref[: rows // 2, cols] = parts[5 * t + 3][...]
            w_ref[rows // 2 :, cols] = parts[5 * t + 4][...]

    value = dense(x_ref[...], w_ref[...]) + bias_ref[...]
    if gelu:
        value, slope = gelu_both(value)
        outs[0][...] = value.astype(BF)
        outs[1][...] = slope.astype(BF)
    else:
        outs[0][...] = refs[12][...] + value


def assemble_dot(me, mine, other, x, bias, onto=None):
    rows, n = mine[0].shape
    tok = x.shape[0]
    whole = lambda v: pl.BlockSpec(v.shape, lambda i, me_ref: (0, 0))
    pair = lambda r: pl.BlockSpec((r, 2 * n), lambda i, me_ref: (0, jnp.bitwise_xor(me_ref[0] // 2, i)))
    gelu = onto is None
    outs = [BF, BF] if gelu else [F32]
    return pl.pallas_call(
        functools.partial(assemble_dot_kernel, gelu),
        grid_spec=pltpu.PrefetchScalarGridSpec(
            num_scalar_prefetch=1,
            grid=(4,),
            in_specs=[whole(v) for v in mine + other] + [whole(x), pair(1)] + ([] if gelu else [pair(tok)]),
            out_specs=[pair(rows)] + [pair(tok)] * len(outs),
        ),
        out_shape=[jax.ShapeDtypeStruct((rows, 8 * n), BF)] + [jax.ShapeDtypeStruct((tok, 8 * n), t) for t in outs],
        compiler_params=params(),
        cost_estimate=SHORT,
    )(me, *mine, *other, x, bias, *([] if gelu else [onto]))


def after(v, *others):
    return lax.optimization_barrier((v,) + others)[0]


def all_after(vs, *others):
    return lax.optimization_barrier(tuple(vs) + others)[: len(vs)]


def send_shard(ws, *wait):
    w = after(jnp.concatenate(ws, axis=1) if len(ws) > 1 else ws[0], *wait)
    return w, swap(w, 2), swap(w, 4)


def send_diagonal(got, *wait):
    x, y = all_after(got[1:], *wait)
    half = x.shape[0] // 2
    return swap(x[:half], 4), swap(y[half:], 2)


def send_core(parts, *wait):
    parts = all_after(parts, *wait)
    return parts, tuple(swap(v, 1) for v in parts)


def wgrad_kernel(counts, me_ref, *refs):
    keep_ref, send_ref = refs[-2 - len(counts) : -len(counts)]
    scratch = refs[-len(counts) :]
    at = first = 0
    for blocks, xt_ref in zip(counts, scratch):
        x_ref = refs[at]
        keep_in = [r[0] for r in refs[at + 1 : at + 1 + blocks]]
        send_in = [r[0] for r in refs[at + 1 + blocks : at + 1 + 2 * blocks]]
        at += 1 + 2 * blocks

        @pl.when(pl.program_id(0) == 0)
        def _():
            xt_ref[...] = jnp.transpose(x_ref[...])

        rows = xt_ref.shape[0]
        res = dense(xt_ref[...], jnp.concatenate(keep_in + send_in, axis=1))
        wide = res.shape[1] // 256
        for t, ref in enumerate((keep_ref, send_ref)):
            for j in range(wide):
                col = (t * wide + j) * 128
                ref[0, first + j * rows : first + (j + 1) * rows] = res[:, col : col + 128].astype(BF)
        first += wide * rows


def wgrad(me, *products):
    in_specs, operands, counts, scratch = [], [], [], []
    height = flops = moved = 0
    for x, dy in products:
        tok, rows = x.shape
        parts, _, cols = dy.shape
        n = parts * cols // 8
        width = n if parts == 1 else 128
        per = cols // width
        blocks = n // width
        in_specs.append(pl.BlockSpec((tok, rows), lambda i, me_ref: (0, 0)))
        operands.append(x)
        for t in (0, 1):
            for j in range(blocks):

                def place(i, me_ref, t=t, j=j, blocks=blocks, per=per):
                    b = jnp.bitwise_xor(me_ref[0], 2 * i + t) * blocks + j
                    return (b // per, 0, b % per)

                in_specs.append(pl.BlockSpec((1, tok, width), place))
                operands.append(dy)
        counts.append(blocks)
        scratch.append(pltpu.VMEM((rows, tok), BF))
        height += n // 128 * rows
        flops += 2 * tok * rows * 8 * n
        moved += 2 * (tok * rows + tok * 8 * n + rows * 8 * n)
    out_spec = pl.BlockSpec((1, height, 128), lambda i, me_ref: (i, 0, 0))
    return pl.pallas_call(
        functools.partial(wgrad_kernel, tuple(counts)),
        grid_spec=pltpu.PrefetchScalarGridSpec(
            num_scalar_prefetch=1,
            grid=(4,),
            in_specs=in_specs,
            out_specs=[out_spec, out_spec],
            scratch_shapes=scratch,
        ),
        out_shape=[jax.ShapeDtypeStruct((4, height, 128), BF)] * 2,
        compiler_params=params(),
        cost_estimate=SHORT,
    )(me, *operands)


def up_grad_kernel(me_ref, x_ref, du_ref, w_ref, keep_ref, send_ref, c_ref, xt_ref):
    step = pl.program_id(0)

    @pl.when(step == 0)
    def _():
        xt_ref[...] = jnp.transpose(x_ref[...])

    du = du_ref[...]
    res = dense(xt_ref[...], du)
    rows, n = xt_ref.shape[0], du.shape[1] // 2
    for odd in (0, 1):

        @pl.when(me_ref[0] % 2 == odd)
        def _():
            for t, ref in enumerate((keep_ref, send_ref)):
                for j in range(n // 128):
                    col = (t ^ odd) * n + j * 128
                    ref[0, j * rows : (j + 1) * rows] = res[:, col : col + 128].astype(BF)

    part = nt(du, w_ref[...])

    @pl.when(step == 0)
    def _():
        c_ref[...] = part

    @pl.when(step > 0)
    def _():
        c_ref[...] += part


def up_grad(me, x, du, w):
    tok, rows = x.shape
    n = du.shape[1] // 8
    stacked = n // 128 * rows
    pair = lambda r: pl.BlockSpec((r, 2 * n), lambda i, me_ref: (0, jnp.bitwise_xor(me_ref[0] // 2, i)))
    whole = pl.BlockSpec((tok, rows), lambda i, me_ref: (0, 0))
    shards = pl.BlockSpec((1, stacked, 128), lambda i, me_ref: (i, 0, 0))
    return pl.pallas_call(
        up_grad_kernel,
        grid_spec=pltpu.PrefetchScalarGridSpec(
            num_scalar_prefetch=1,
            grid=(4,),
            in_specs=[whole, pair(tok), pair(rows)],
            out_specs=[shards, shards, whole],
            scratch_shapes=[pltpu.VMEM((rows, tok), BF)],
        ),
        out_shape=[jax.ShapeDtypeStruct((4, stacked, 128), BF)] * 2 + [jax.ShapeDtypeStruct((tok, rows), F32)],
        compiler_params=params(),
        cost_estimate=SHORT,
    )(me, x, du, w)


def gelu_grad_kernel(dz_ref, w_ref, slope_ref, du_ref):
    du_ref[...] = (nt(dz_ref[...], w_ref[...]) * slope_ref[...].astype(F32)).astype(BF)


def gelu_grad(dz, w, slope):
    rows, width = dz.shape
    hidden = w.shape[0]
    block = 2048
    wide = pl.BlockSpec((rows, block), lambda i: (0, i))
    return pl.pallas_call(
        gelu_grad_kernel,
        grid=(hidden // block,),
        in_specs=[
            pl.BlockSpec((rows, width), lambda i: (0, 0)),
            pl.BlockSpec((block, width), lambda i: (i, 0)),
            wide,
        ],
        out_specs=wide,
        out_shape=jax.ShapeDtypeStruct((rows, hidden), BF),
        compiler_params=params(),
        cost_estimate=SHORT,
    )(dz, w, slope)


def kv_grad_kernel(dk_ref, dv_ref, wk_ref, wv_ref, x_ref, part_ref, sums_ref):
    part = nt(dk_ref[0], wk_ref[...]) + nt(dv_ref[0], wv_ref[...])
    part_ref[0] = part.astype(BF)
    _, normed, _ = layer_norm(x_ref[...].astype(F32), 1.0, 0.0)

    @pl.when(pl.program_id(0) == 0)
    def _():
        sums_ref[...] = jnp.zeros_like(sums_ref)

    sums_ref[0:1] += jnp.sum(part * normed, axis=0, keepdims=True)
    sums_ref[1:2] += jnp.sum(part, axis=0, keepdims=True)


def kv_grad(dqkv, w, x, n):
    _, rows, width = dqkv.shape
    block = rows // n
    return pl.pallas_call(
        kv_grad_kernel,
        grid=(n,),
        in_specs=[
            pl.BlockSpec((1, block, width), lambda i: (1, i, 0)),
            pl.BlockSpec((1, block, width), lambda i: (2, i, 0)),
            pl.BlockSpec((width, width), lambda i: (0, 1)),
            pl.BlockSpec((width, width), lambda i: (0, 2)),
            pl.BlockSpec((block, width), lambda i: (i, 0)),
        ],
        out_specs=[
            pl.BlockSpec((1, block, width), lambda i: (i, 0, 0)),
            pl.BlockSpec((8, width), lambda i: (0, 0)),
        ],
        out_shape=[jax.ShapeDtypeStruct((n, block, width), BF), jax.ShapeDtypeStruct((8, width), F32)],
        compiler_params=params(),
        cost_estimate=SHORT,
    )(dqkv, dqkv, w, w, x)


def add(*terms):
    total = terms[0].astype(F32)
    for t in terms[1:]:
        total = total + t.astype(F32)
    return total.astype(BF)


def pick(v, i, half):
    rows = v.shape[1] // 2
    return v[i, half * rows : (half + 1) * rows]


def sum_near(keep, got, *wait):
    keep, got = all_after((keep, got), *wait)
    half = keep.shape[1] // 2
    xa = add(keep[1:4:2, :half], got[1:4:2, :half])
    yb = add(keep[2:4, half:], got[2:4, half:])
    return (swap(xa, 2), swap(yb, 4)), (xa, yb)


def sum_far(keep, got, near, *wait):
    xa, yb, keep, got = all_after(tuple(near) + (keep, got), *wait)
    ya = add(pick(keep, 2, 0), pick(got, 2, 0), xa[1])
    xb = add(pick(keep, 1, 1), pick(got, 1, 1), yb[1])
    return (swap(ya, 4), swap(xb, 2)), (ya, xb)


def sum_own(keep, got, near, far):
    halves = [add(pick(keep, 0, h), pick(got, 0, h), near[h][0], far[h]) for h in (0, 1)]
    return jnp.concatenate(halves, axis=0)


def shift(v, n, step, pairs):
    return lax.ppermute(v, "seq", [(a, a + step) for a in pairs if 0 <= a + step < n])


def gather_rows(v, z, n):
    right, left = [v], [v]
    for s in range(n - 1):
        right.append(shift(right[-1], n, 1, range(s, n)))
        left.append(shift(left[-1], n, -1, range(0, n - s)))
    out = []
    for k in range(n):
        val = v
        for d in range(1, n):
            if k + d < n:
                val = jnp.where(z == k + d, right[d], val)
            if k - d >= 0:
                val = jnp.where(z == k - d, left[d], val)
        out.append(val)
    return jnp.concatenate(out, axis=0)


def scatter_rows(v, z, n, wait=()):
    part = lambda t: lax.dynamic_index_in_dim(v, jnp.clip(t, 0, n - 1), 0, keepdims=False).astype(F32)
    r = l = None
    for p in range(1, n):
        rv, lv = part(n - p + z), part(p - n + z)
        if r is not None:
            r, l = all_after((r, l), *wait)
            rv, lv = rv + r.astype(F32), lv + l.astype(F32)
        r = shift(rv.astype(BF), n, 1, range(0, p))
        l = shift(lv.astype(BF), n, -1, range(n - p, n))
    return part(z) + r.astype(F32) + l.astype(F32)


def twin(v, bit):
    return lax.ppermute(v, "seq", [(i, i ^ bit) for i in range(4)])


def take_part(v, at, count):
    rows = v.shape[0] // count
    return lax.dynamic_slice_in_dim(v, at * rows, rows)


def in_order(mine, other, bit):
    return jnp.where(bit == 0, jnp.concatenate([mine, other]), jnp.concatenate([other, mine]))


def local(
    tokens, enc_states, order, lengths, enc_lengths, attn_in, attn_out, cross_q, cross_kv,
    cross_out, ffn_in, ffn_out, proj_bias, gains, ln_bias, ffn_bias, cotangent,
):
    n_dp, n_seq = lax.axis_size("dp"), lax.axis_size("seq")
    z = lax.axis_index("seq")
    dp = lax.axis_index("dp")
    me = dp.astype(jnp.int32).reshape(1)
    fast = n_dp == 8 and n_seq == 4 and attn_out.shape[1] % 128 == 0
    x = tokens[0]
    rows, width = x.shape
    enc_rows = enc_states.shape[1] * n_seq
    group_rows = rows * n_seq
    shard = attn_out.shape[1]

    small = jnp.concatenate([proj_bias, gains, ln_bias, ffn_bias.reshape(-1, shard)], axis=0)
    count = small.shape[0]
    if fast:
        pad_rows = 32
        w = attn_in.shape[1]
        flat = jnp.concatenate([small.reshape(-1), jnp.zeros((pad_rows * w - small.size,), BF)])
        a_near = send_shard([jnp.concatenate([attn_in, flat.reshape(pad_rows, w)], axis=0)])
        x_full = lax.all_gather(x, "seq", axis=0, tiled=True)
        a_far = send_diagonal(a_near)
        b_near = send_shard([cross_kv, attn_out, cross_q, cross_out], *a_near[1:])
        states = lax.all_gather(after(enc_states[0], x_full), "seq", axis=0, tiled=True)
        (first,) = assemble(me, *send_core(a_near + a_far), (w,))
        b_far = send_diagonal(b_near, first)
        w_in = first[:width]
        small_all = first[width:].reshape(pad_rows, n_dp, w).transpose(1, 0, 2).reshape(n_dp, -1)
        small_all = small_all[:, : small.size].reshape(n_dp, count, shard)
    else:
        x_full = gather_rows(x, z, n_seq)
        states = gather_rows(enc_states[0], z, n_seq)
        gather = lambda v: lax.all_gather(v, "dp", axis=1, tiled=True)
        w_in, w_ckv, w_out, w_cq = gather(attn_in), gather(cross_kv), gather(attn_out), gather(cross_q)
        w_cout, w_up, w_down = gather(cross_out), gather(ffn_in), gather(ffn_out)
        small_all = lax.all_gather(small, "dp", axis=0, tiled=False)
    n_bias, n_norm = proj_bias.shape[0], gains.shape[0]
    rows_all = small_all[:, : n_bias + 2 * n_norm].transpose(1, 0, 2).reshape(-1, width).astype(F32)
    bias = rows_all[:n_bias]
    gain = rows_all[n_bias : n_bias + n_norm]
    shift_v = rows_all[n_bias + n_norm :]
    up_bias = small_all[:, n_bias + 2 * n_norm :].reshape(-1).astype(F32)

    place = order[0]
    seg = segment_ids(place, lengths[0])
    seg_enc = segment_ids(jnp.arange(enc_rows, dtype=jnp.int32), enc_lengths[0])
    my_place = lax.dynamic_slice_in_dim(place, z * rows, rows)
    my_seg = lax.dynamic_slice_in_dim(seg, z * rows, rows)
    self_keep = (seg[:, None] == my_seg[None, :]) & (place[:, None] <= my_place[None, :])
    self_bias = jnp.where(self_keep, 0.0, NEG).astype(F32)
    cross_bias = jnp.where(seg_enc[:, None] == my_seg[None, :], 0.0, NEG).astype(F32)
    zero_row = jnp.zeros((width,), F32)

    x32 = x.astype(F32)
    v1_own, xh1, rs1 = layer_norm(x32, gain[0], shift_v[0])
    z_row = z.astype(jnp.int32).reshape(1)
    if fast:
        x_full, self_bias, cross_bias = all_after((x_full, self_bias, cross_bias))
        qkv_bias = jnp.concatenate([bias[0], zero_row, bias[1]])[None]
        a1_full, q, kv = project(z_row, x_full, first, gain[:1], shift_v[:1], qkv_bias, n_seq)
    else:
        xf = x_full.astype(F32)
        a1_full = layer_norm(xf, gain[0], shift_v[0])[0].astype(BF)
        kv = (dense(a1_full, w_in[:, width:]) + jnp.concatenate([zero_row, bias[1]])).astype(BF)
        q = (dense(v1_own.astype(BF), w_in[:, :width]) + bias[0]).astype(BF)
    if fast:
        b_parts, b_other = send_core(b_near + b_far, kv)
        c_near = send_shard([ffn_in], kv)
        q, kv, *_ = all_after((q, kv), *b_far)
    half = HEADS // 4
    attn_a, lse_a = attn_fwd(q, kv, self_bias, 0, half)
    if fast:
        widths = tuple(v.shape[1] for v in (cross_kv, attn_out, cross_q, cross_out))
        b_parts = all_after(b_parts, attn_a)
        w_ckv, w_out, w_cq, w_cout = assemble(me, b_parts, b_other, widths)
        q, attn_a, lse_a, w_out, states = all_after((q, attn_a, lse_a, w_out, states), *c_near[1:])
        c_far = send_diagonal(c_near, attn_a)
    attn_b, lse_b = attn_fwd(q, kv, self_bias, half, half)
    attn = jnp.concatenate([attn_a, attn_b], axis=1)
    lse = jnp.concatenate([lse_a, lse_b], axis=0)
    if fast:
        attn, lse = all_after((attn, lse), *c_far)
        d_near = send_shard([ffn_out], attn)
        c_parts, c_other = send_core(c_near + c_far, attn)
    h1 = x32 + dense(attn, w_out) + bias[2]
    v2, xh2, rs2 = layer_norm(h1, gain[1], shift_v[1])
    a2 = v2.astype(BF)
    cq = (dense(a2, w_cq) + bias[3]).astype(BF)
    ekv = (dense(states, w_ckv) + jnp.concatenate([zero_row, bias[4]])).astype(BF)
    if fast:
        cq = after(cq, ekv, *c_other)
    cattn, clse = attn_fwd(cq, ekv, cross_bias)
    if fast:
        cattn = after(cattn, *d_near[1:])
        d_far = send_diagonal(d_near, cattn)
        d_parts, d_other = send_core(d_near, cattn)
        c_parts = all_after(c_parts, cattn)
    h2 = h1 + dense(cattn, w_cout) + bias[5]
    v3, xh3, rs3 = layer_norm(h2, gain[2], shift_v[2])
    a3 = v3.astype(BF)
    if fast:
        w_up, gelu_h, slope = assemble_dot(me, c_parts, c_other, a3, up_bias[None])
        gelu_h, *d_far = all_after((gelu_h,) + d_far)
        d_rest, d_other_rest = send_core(d_far, gelu_h)
        d_parts, d_other = d_parts + d_rest, d_other + d_other_rest
        w_down, h3 = assemble_dot(me, d_parts, d_other, gelu_h, bias[6:7], h2)
    else:
        gelu, slope = gelu_both(dense(a3, w_up) + up_bias)
        gelu_h, slope = gelu.astype(BF), slope.astype(BF)
        h3 = h2 + dense(gelu_h, w_down) + bias[6]
    out, xh4, rs4 = layer_norm(h3, gain[3], shift_v[3])

    total = lambda v: jnp.sum(v, axis=0, dtype=F32)
    by_columns = lambda a, b: lax.psum_scatter(dense_left(a, b), "dp", scatter_dimension=1, tiled=True).astype(BF)
    ct = cotangent[0].astype(F32)
    g3, s3 = norm_sums(xh4, ct)
    dh3 = norm_input_grad(xh4, rs4, gain[3], ct)
    dz = dh3.astype(BF)

    def by_chain(v, turn=0):
        listed = [(turn + i) % n_seq for i in range(n_seq)]
        return lax.psum(v, "seq", axis_index_groups=[listed])

    if fast:
        dz, gelu_h = all_after((dz, gelu_h))
        d_keep, d_send = wgrad(me, (gelu_h, dz[None]))
        dz, d_keep, d_send = all_after((dz, d_keep, d_send))
        d_got = swap(d_send, 1)
    du = gelu_grad(dz, w_down, slope)
    if fast:
        du, d_got = all_after((du, d_got))
        d_n, sent = sum_near(d_keep, d_got, du)
        du, *_ = all_after((du,), *sent)
        c_keep, c_send, c3 = up_grad(me, a3, du, w_up)
        c3, c_send, *d_n = all_after((c3, c_send) + tuple(d_n))
        c_got = swap(c_send, 1)
    else:
        c3 = dense_t(du, w_up)
    g2, s2 = norm_sums(xh3, c3)
    dh2 = dh3 + norm_input_grad(xh3, rs3, gain[2], c3)
    dc = dh2.astype(BF)
    dcattn = dense_t(dc, w_cout).astype(BF)
    if fast:
        dcattn, *_ = all_after((dcattn,), *d_n)
        d_f, sent = sum_far(d_keep, d_got, d_n, dcattn)
        dcattn = after(dcattn, *sent)
    dcq, dekv = attn_bwd(z_row, cq, ekv, cross_bias, clse, cattn, dcattn, False)
    if fast:
        dcq, dekv = all_after((dcq, dekv), *d_f)
        c_n, sent = sum_near(c_keep, c_got, dcq)
        d_sum = sum_own(d_keep, d_got, d_n, d_f)
        low, high = z % 2, z // 2
        d_other = take_part(d_sum, 1 - low, 2)
        dcq, dekv, *_ = all_after((dcq, dekv), d_other, *sent)
        d_got_a = twin(d_other, 1)
        e_keep, e_send = wgrad(me, (cattn, dc[None]), (a2, dcq[None]), (states, dekv))
        dcq, dekv, e_keep, e_send, d_got_a = all_after((dcq, dekv, e_keep, e_send, d_got_a), *c_n)
        d_half = add(take_part(d_sum, low, 2), d_got_a)
        d_other = take_part(d_half, 1 - high, 2)
        dcq = after(dcq, d_other)
        d_got_b = twin(d_other, 2)
        e_got = swap(e_send, 1)
        c_f, sent = sum_far(c_keep, c_got, c_n, dcq)
        dcq = after(dcq, *sent)
    enc_part = dense_t(dekv[0], w_ckv[:, :width]) + dense_t(dekv[1], w_ckv[:, width:])
    if fast:
        enc_part = enc_part.astype(BF)
        dcq = after(dcq, enc_part)
    c2 = dense_t(dcq, w_cq)
    g1, s1 = norm_sums(xh2, c2)
    dh1 = dh2 + norm_input_grad(xh2, rs2, gain[1], c2)
    da = dh1.astype(BF)
    dattn = dense_t(da, w_out).astype(BF)
    if fast:
        dattn, d_got_b = all_after((dattn, d_got_b), *c_f)
        d_quarter = add(take_part(d_half, high, 2), d_got_b)
        e_n, sent = sum_near(e_keep, e_got, dattn)
        c_sum = sum_own(c_keep, c_got, c_n, c_f)
        c_all = by_chain(c_sum, 1)
        dattn = after(dattn, c_sum, d_quarter, *sent)
        d_got_c = twin(d_quarter, 2)
    dq, dqkv = attn_bwd(z_row, q, kv, self_bias, lse, attn, dattn, True, 0, 5)
    if fast:
        enc_sum = lax.psum_scatter(enc_part, "seq", scatter_dimension=0, tiled=True)
        dattn, dq, dqkv, d_got_c = all_after((dattn, dq, dqkv, d_got_c), *e_n, enc_sum)
        d_half = in_order(d_quarter, d_got_c, high)
        e_f, sent = sum_far(e_keep, e_got, e_n, dattn)
        dattn = after(dattn, d_half, *sent)
        d_got_d = twin(d_half, 1)
    dq, dqkv = attn_bwd(z_row, q, kv, self_bias, lse, attn, dattn, True, 5, 3, (dq, dqkv))
    if fast:
        dq, dqkv, d_got_d = all_after((dq, dqkv, d_got_d), *e_f)
        d_all = in_order(d_half, d_got_d, low)
        e_sum = sum_own(e_keep, e_got, e_n, e_f)
        e_all = by_chain(e_sum, 2)
        dqkv = after(dqkv, e_sum)
        i_keep, i_send = wgrad(me, (attn, da[None]), (a1_full, dqkv))
        dq, dqkv, i_keep, i_send = all_after((dq, dqkv, i_keep, i_send), c_all)
        i_got = swap(i_send, 1)
    if fast:
        c1_part, c1_sums = kv_grad(dqkv, first, x_full, n_seq)
        c1_part, c1_sums, i_got = all_after((c1_part, c1_sums, i_got))
        i_n, sent = sum_near(i_keep, i_got)
        c1_part = after(c1_part, *sent)
        c1_q = dense_t(dq, w_in[:, :width])
        g0, s0 = (a + b for a, b in zip((c1_sums[0], c1_sums[1]), norm_sums(xh1, c1_q)))
        c1_q = after(c1_q, g0, s0)
    else:
        c1_part = dense_t(dqkv[1], w_in[:, width : 2 * width]) + dense_t(dqkv[2], w_in[:, 2 * width :])
        c1_q = dense_t(dq, w_in[:, :width])
        _, xh1_full, _ = layer_norm(xf, gain[0], shift_v[0])
        g0, s0 = (a + b for a, b in zip(norm_sums(xh1_full, c1_part), norm_sums(xh1, c1_q)))

    bias_rows = [total(dq), total(dqkv[2]), total(dh1), total(dcq), total(dekv[1]), total(dh2), total(dh3)]
    small_rows = jnp.stack(bias_rows + [g0, g1, g2, g3, s0, s1, s2, s3])
    small_rows = small_rows.reshape(-1, n_dp, shard).transpose(1, 0, 2)
    small_rows = jnp.concatenate([small_rows, total(du).reshape(n_dp, -1, shard)], axis=1)
    dh1, c1_q = all_after((dh1, c1_q), small_rows)
    if fast:
        c1_sum = scatter_rows(c1_part, z, n_seq)
        i_f, _ = sum_far(i_keep, i_got, i_n)
        i_sum = after(sum_own(i_keep, i_got, i_n, i_f), e_all)
        i_all = by_chain(i_sum, 3)
        e_all, c_all, d_all = all_after((e_all, c_all, d_all), i_sum)
        enc_grad = enc_sum.astype(F32)
        c1 = c1_sum + c1_q
        flat_out = lambda v, r: jnp.concatenate(jnp.split(v, v.shape[0] // r, axis=0), axis=1).astype(F32)
        r_up, r_down = flat_out(c_all, width), d_all.astype(F32)
        r_in, r_out = flat_out(i_all[width:], width), i_all[:width].astype(F32)
        r_cout, r_cq, r_ckv = (flat_out(v, width) for v in jnp.split(e_all, [width, 2 * width], axis=0))
    else:
        c1 = lax.psum_scatter(c1_part, "seq", scatter_dimension=0, tiled=True) + c1_q
        enc_grad = lax.psum_scatter(enc_part, "seq", scatter_dimension=0, tiled=True)
        flat = lambda v: jnp.concatenate(list(v), axis=1)
        pairs = [(a1_full, flat(dqkv)), (attn, da), (a2, dcq), (states, flat(dekv)), (cattn, dc), (a3, du), (gelu_h, dz)]
        grads = [by_chain(by_columns(a, b)).astype(F32) for a, b in pairs]
        r_in, r_out, r_cq, r_ckv, r_cout, r_up, r_down = grads
    if fast:
        small_rows = after(small_rows, i_sum)
        for bit in (1, 2, 4):
            small_rows = small_rows + swap(small_rows, bit)
        for bit in (1, 2):
            small_rows = small_rows + lax.ppermute(small_rows, "seq", [(i, i ^ bit) for i in range(n_seq)])
    else:
        small_rows = lax.psum(small_rows, ("dp", "seq"))
    tokens_grad = dh1 + norm_input_grad(xh1, rs1, gain[0], c1)
    small_own = lax.dynamic_index_in_dim(small_rows, dp, 0, keepdims=False)
    return (
        out.astype(BF)[None],
        tokens_grad[None],
        enc_grad[None],
        r_in,
        r_out,
        r_cq,
        r_ckv,
        r_cout,
        r_up,
        r_down,
        small_own[:n_bias],
        small_own[n_bias : n_bias + n_norm],
        small_own[n_bias + n_norm : n_bias + 2 * n_norm],
        small_own[n_bias + 2 * n_norm :].reshape(1, -1),
    )


def solution(mesh):
    rows, cols, per_dp = P("dp", "seq", None), P(None, "dp"), P("dp", None)
    in_specs = (rows, rows, per_dp, per_dp, per_dp) + (cols,) * 11 + (rows,)
    out_specs = (rows,) * 3 + (cols,) * 11
    return jax.shard_map(local, mesh=mesh, in_specs=in_specs, out_specs=out_specs, check_vma=False)
```
